32 devices in a mesh: ra: 4 (over z), dec: 4 (over y, x), band: 2 (over core).
Axes of the slice: x: 2, y: 2, z: 4, core: 2. Of those that a mesh axis runs over, the one named last changes fastest.
Arguments:
- morphology: bfloat16 [4, 4, 128, 4096], P('ra', 'dec'), may hold values from 0 to 1
- sed_amps: float32 [4, 4, 6, 128], P('ra', 'dec', 'band'), may hold values from 0.1 to 2
- slot_lists: int32 [4, 4, 5, 128], P('ra', 'dec'), may hold values from 0 to 16, as said below
- morph_step: float32 [4, 4, 128], P('ra', 'dec'), may hold values from 0.01 to 0.04
- sed_step: float32 [4, 4, 128], P('ra', 'dec'), may hold values from 9.765625e-06 to 3.90625e-05
- psf_kernels: bfloat16 [6, 32, 4096], P('band', 'ra'), may hold values from -0.75 to 0.75
- observed: bfloat16 [4, 4, 6, 16, 4096], P('ra', 'dec', 'band'), may hold values from -16 to 16
Outputs:
- morph_out: float32 [4, 4, 128, 4096], P('ra', 'dec', None, 'band')
- sed_out: float32 [4, 4, 6, 128], P('ra', 'dec', 'band')
The draws below stay inside these ranges and needn't reach their ends.
Inputs may be any that keep to these rules, and one draw needn't show every extreme that they name: `slot_lists`: in each home tile the sources 0 to some count - 1 are live (the count at least 32, and 128 in some tile); a live source has a slot below 16 in row 0; every other entry of a dead source is 16. No source lands beyond the declination edges. Each of rows 1 to 4 of a home tile holds at most 32 entries below 16, and some tile's row 1 holds exactly 32.
All inputs are finite; a program needn't handle non-finite values.
Results may differ from the reference program's by a relative error of at most 0.015.
Values may be sent and summed in bfloat16 or wider, within the bound.
No kernel may reach another device: no remote copies, remote signals or barrier semaphores. Data moves between devices by JAX's collectives and lax.ppermute only.
A program may use at most 256 MiB of HBM per device.

```python
import math
import jax
import jax.numpy as jnp
from jax import lax

SIDE = 64
PIX = 4096
BANDS = 6
KERN = 32
SRC = 128
CAP = 32
SLOTS = 16
DIRS = 5
ITERS = 2
N_RA = 4
N_DEC = 4


def draw_slot_lists(key, part):
    key = jax.random.fold_in(key, 7)
    key_live, key_slot, key_over, key_full = jax.random.split(key, 4)
    tiles = N_RA * N_DEC
    live_count = jax.random.randint(key_live, (tiles,), SRC // 4, SRC + 1)
    full_tile = jax.random.randint(key_full, (), 0, tiles)
    tile_ids = jnp.arange(tiles)
    live_count = jnp.where(tile_ids == full_tile, SRC, live_count)
    alive = jnp.arange(SRC)[None, :] < live_count[:, None]
    slot_pick = jax.random.randint(key_slot, (tiles, DIRS, SRC), 0, SLOTS)
    intersections = jax.random.randint(key_over, (tiles, DIRS, SRC), 0, 10) < 3
    direction = jnp.arange(DIRS)
    forced = (tile_ids[:, None] == full_tile) & (direction[None, :] == 1)
    intersections = intersections | forced[:, :, None]
    dec_index = tile_ids % N_DEC
    edge_block = (direction[None, :] == 3) & (dec_index[:, None] == N_DEC - 1) | (direction[None, :] == 4) & (dec_index[:, None] == 0)
    candidate = alive[:, None, :] & intersections & (~edge_block)[:, :, None]
    rank = jnp.cumsum(candidate.astype(jnp.int32), axis=2)
    capped = candidate & (rank <= CAP)
    home_row = (direction == 0)[None, :, None]
    used = jnp.where(home_row, alive[:, None, :], capped)
    result = jnp.where(used, slot_pick, SLOTS)
    return result.reshape(N_RA, N_DEC, DIRS, SRC).astype(jnp.int32)


def levels(own_key, extent, shards, least, top_value):
    factor_of = 1.0
    for position, shards_of in shards:
        heights = jax.random.uniform(jax.random.fold_in(jax.random.fold_in(own_key, 6), position), (shards_of,), jnp.float32, least / len(shards), top_value / len(shards))
        factor_of = factor_of * jnp.repeat(jnp.exp(heights), extent[position] // shards_of).reshape((-1,) + (1,) * (len(extent) - 1 - position))
    return factor_of


def bell_draw(key, shape, width, reach, shards=(), held_as=jnp.bfloat16):
    drawn = width * jax.random.normal(key, shape, jnp.float32)
    if shards:
        drawn = drawn * levels(key, shape, shards, -0.22, 0.18)
    return jnp.clip(drawn, -reach, reach).astype(held_as)


def setup_inputs(seed: int = 0) -> dict:
    splits = jax.random.split(jax.random.key(seed), 8)
    morphology = jnp.clip(1.0 * jax.random.uniform(splits[0], (N_RA, N_DEC, SRC, PIX), jnp.float32) ** levels(splits[0], (N_RA, N_DEC, SRC, PIX), ((0, 4), (1, 4)), -0.2, 0.2), 0.0, 1.0).astype(jnp.bfloat16)
    sed_amps = jnp.clip(jnp.exp(math.log(2.0) - 2.9957323 * jax.random.uniform(splits[1], (N_RA, N_DEC, BANDS, SRC), jnp.float32) ** levels(splits[1], (N_RA, N_DEC, BANDS, SRC), ((0, 4), (1, 4), (2, 2)), -0.2, 0.2)), 0.1, 2.0)
    slot_lists = draw_slot_lists(jax.random.fold_in(splits[7], 71), 0)
    morph_step = jnp.clip(jnp.exp(math.log(0.04) - 1.3862944 * jax.random.uniform(splits[3], (N_RA, N_DEC, SRC), jnp.float32) ** levels(splits[3], (N_RA, N_DEC, SRC), ((0, 4), (1, 4)), -0.2, 0.2)), 0.01, 0.04)
    sed_step = jnp.clip(jnp.exp(math.log(3.9062499126885086e-05) - 1.3862944 * jax.random.uniform(splits[4], (N_RA, N_DEC, SRC), jnp.float32) ** levels(splits[4], (N_RA, N_DEC, SRC), ((0, 4), (1, 4)), -0.2, 0.2)), 9.765624781721272e-06, 3.9062499126885086e-05)
    psf_kernels = bell_draw(splits[5], (BANDS, KERN, PIX), SIDE ** -0.5, 0.75, ((0, 2), (1, 4)))
    observed = bell_draw(splits[6], (N_RA, N_DEC, BANDS, SLOTS, PIX), 3.0, 16.0, ((0, 4), (1, 4), (2, 2)))
    return dict(morphology=morphology, sed_amps=sed_amps, slot_lists=slot_lists, morph_step=morph_step, sed_step=sed_step, psf_kernels=psf_kernels, observed=observed)


def pick_kernels(psf_band, kern_index):
    selector = (kern_index[:, None] == jnp.arange(KERN, dtype=jnp.int32)[None, :]).astype(jnp.float32)
    picked = jnp.einsum('sk,bkp->bsp', selector, psf_band.astype(jnp.float32)).astype(jnp.bfloat16)
    return picked.reshape(picked.shape[0], picked.shape[1], SIDE, SIDE)


def convolve(morph_q, kernels):
    stamps = morph_q.reshape(morph_q.shape[0], SIDE, SIDE).astype(jnp.float32)
    kern_f = kernels.astype(jnp.float32)
    inner_prod = jnp.einsum('sij,bscj->bsic', stamps, kern_f).astype(jnp.bfloat16)
    convolved = jnp.einsum('bsai,bsic->bsac', kern_f, inner_prod.astype(jnp.float32))
    return convolved.reshape(convolved.shape[0], convolved.shape[1], SIDE * SIDE)


def partial_image(weighted, slot_row):
    selector = (slot_row[None, :] == jnp.arange(SLOTS, dtype=jnp.int32)[:, None]).astype(jnp.float32)
    return jnp.einsum('qs,bsp->bqp', selector, weighted, precision=lax.Precision.HIGHEST).astype(jnp.bfloat16)


def reference(morphology, sed_amps, slot_lists, morph_step, sed_step, psf_kernels, observed):
    tiles = N_RA * N_DEC
    flat_lists = slot_lists.reshape(tiles, DIRS, SRC)
    state_m = morphology.astype(jnp.float32).reshape(tiles, SRC, PIX)
    state_a = sed_amps.reshape(tiles, BANDS, SRC)
    eta_m = morph_step.reshape(tiles, SRC, 1)
    eta_a = sed_step.reshape(tiles, 1, SRC)
    obs_f = observed.astype(jnp.float32)
    tile_ids = jnp.arange(tiles, dtype=jnp.int32)
    for sweep in range(ITERS):
        morph_q = state_m.astype(jnp.bfloat16)
        sed_q = state_a.astype(jnp.bfloat16)

        def forward(tile_index):
            lists_here = flat_lists[tile_index]
            kernels = pick_kernels(psf_kernels, lists_here[0] % KERN)
            conv_here = convolve(morph_q[tile_index], kernels)
            weighted = sed_q[tile_index].astype(jnp.float32)[:, :, None] * conv_here
            return jnp.stack([partial_image(weighted, lists_here[direction]) for direction in range(DIRS)])

        images = lax.map(forward, tile_ids).reshape(N_RA, N_DEC, DIRS, BANDS, SLOTS, PIX)
        zero_row = jnp.zeros((N_RA, 1, BANDS, SLOTS, PIX), jnp.bfloat16)
        summed = images[:, :, 0].astype(jnp.float32)
        summed = summed + jnp.roll(images[:, :, 1], 1, axis=0).astype(jnp.float32)
        summed = summed + jnp.roll(images[:, :, 2], -1, axis=0).astype(jnp.float32)
        summed = summed + jnp.concatenate([zero_row, images[:, :-1, 3]], axis=1).astype(jnp.float32)
        summed = summed + jnp.concatenate([images[:, 1:, 4], zero_row], axis=1).astype(jnp.float32)
        residual = (summed - obs_f).astype(jnp.bfloat16)
        padded = jnp.concatenate([zero_row, residual, zero_row], axis=1)

        def backward(tile_index):
            ra_pos = tile_index // N_DEC
            dec_pos = tile_index % N_DEC + 1
            lists_here = flat_lists[tile_index]
            neighbours = [padded[ra_pos, dec_pos], padded[(ra_pos + 1) % N_RA, dec_pos],
                          padded[(ra_pos - 1) % N_RA, dec_pos], padded[ra_pos, dec_pos + 1],
                          padded[ra_pos, dec_pos - 1]]
            gathered = jnp.zeros((BANDS, SRC, PIX), jnp.float32)
            for direction in range(DIRS):
                selector = (lists_here[direction][None, :] == jnp.arange(SLOTS, dtype=jnp.int32)[:, None]).astype(jnp.float32)
                gathered = gathered + jnp.einsum('qs,bqp->bsp', selector, neighbours[direction].astype(jnp.float32))
            gathered_q = gathered.astype(jnp.bfloat16)
            kernels = pick_kernels(psf_kernels, lists_here[0] % KERN)
            conv_here = convolve(morph_q[tile_index], kernels)
            kern_f = kernels.astype(jnp.float32)
            res_stamps = gathered_q.astype(jnp.float32).reshape(BANDS, SRC, SIDE, SIDE)
            left_prod = jnp.einsum('bsai,bsac->bsic', kern_f, res_stamps).astype(jnp.bfloat16)
            back_prod = jnp.einsum('bsic,bscj->bsij', left_prod.astype(jnp.float32), kern_f)
            weights_here = sed_q[tile_index].astype(jnp.float32)[:, :, None, None]
            grad_m = jnp.sum(weights_here * back_prod, axis=0).reshape(SRC, PIX)
            grad_a = jnp.sum(conv_here * gathered_q.astype(jnp.float32), axis=2)
            return grad_m, grad_a

        grad_m, grad_a = lax.map(backward, tile_ids)
        state_m = jnp.maximum(state_m - eta_m * grad_m, 0.0)
        state_a = jnp.maximum(state_a - eta_a * grad_a, 0.0)
    return state_m.reshape(N_RA, N_DEC, SRC, PIX), state_a.reshape(N_RA, N_DEC, BANDS, SRC)
```

```python
import functools

import jax
import jax.numpy as jnp
from jax import lax
from jax.experimental import pallas as pl
from jax.experimental.pallas import tpu as pltpu
from jax.sharding import PartitionSpec as P

SIDE = 64
KERN = 32
ITERS = 2
CAP = 32
LANES = 128
ROWS = SIDE * SIDE // LANES
HALF = ROWS // 2
WIDE = 4 * SIDE
LIST = 40
NEAR = 4
GROUP = 4
STRIDE = 4
F32 = jnp.float32
BF16 = jnp.bfloat16


def dot(a, b):
    return lax.dot_general(a, b, (((1,), (0,)), ((), ())), preferred_element_type=F32)


def dot_nt(a, b, precision=None):
    return lax.dot_general(
        a, b, (((1,), (1,)), ((), ())), precision=precision, preferred_element_type=F32
    )


def iota(shape, dim):
    return lax.broadcasted_iota(jnp.int32, shape, dim)


def low_lanes(rows, dtype=F32):
    return (iota((rows, LANES), 1) < SIDE).astype(F32).astype(dtype)


def half_masks(rows):
    low = iota((rows, LANES), 1) < SIDE
    return low, jnp.logical_not(low)


def turned(value):
    return pltpu.roll(value, SIDE, 1)


def half_rows(other):
    band = lax.axis_index("band")
    return pl.multiple_of(((1 - band) if other else band) * HALF, HALF)


def list_hots(slots, num_slots):
    sources = slots.shape[1]
    valid = (slots < num_slots).astype(F32)
    upper = (iota((sources, sources), 0) <= iota((sources, sources), 1)).astype(F32)
    rank = dot(valid.astype(BF16), upper.astype(BF16))
    place = iota((LANES, sources), 0).astype(F32)
    hots = []
    for near in range(1, NEAR + 1):
        hit = (place == rank[near : near + 1] - 1.0).astype(F32)
        hots.append(hit * valid[near : near + 1])
    return hots


def write_meta(messages, slots, amps, hots):
    row = iota((2 * 8, slots.shape[1]), 0)
    for near in range(NEAR):
        meta = jnp.where(row == 0, slots[near + 1 : near + 2].astype(F32) + 1.0, 0.0)
        meta = jnp.where(row == 1, slots[0:1].astype(F32), meta)
        for band in range(amps.shape[0]):
            meta = jnp.where(row == 2 + band, amps[band : band + 1], meta)
        placed = dot_nt(meta.astype(BF16), hots[near].astype(BF16))
        messages[near][CAP] = placed.astype(BF16)


def pack_kernel(num_slots, lists, slots_ref, amps_ref, morph, *out):
    messages, places, amps_q = out[:NEAR], out[NEAR], out[NEAR + 1]
    slots = slots_ref[...]
    blank = jnp.zeros((HALF, LANES), BF16)
    for near in range(NEAR):
        for n in range(CAP):
            messages[near][n] = blank

    def clear(n, carry):
        places[n] = 0
        return carry

    lax.fori_loop(0, NEAR * LIST, clear, 0)
    rows = pl.ds(half_rows(False), HALF)

    def step(s, counts):
        stamp = morph[s, rows, :]
        after = []
        for near in range(NEAR):
            messages[near][counts[near]] = stamp
            places[near * LIST + counts[near]] = s
            after.append(counts[near] + (lists[near + 1, s] < num_slots).astype(jnp.int32))
        return tuple(after)

    lax.fori_loop(0, slots.shape[1], step, (jnp.int32(0),) * NEAR, unroll=4)
    amps = amps_ref[...]
    write_meta(messages, slots, amps, list_hots(slots, num_slots))
    amps_q[...] = amps.astype(BF16).astype(F32)


def order_kernel(num_slots, *refs):
    own, (order, kernel_of, slot_of, amps, count) = refs[:NEAR], refs[NEAR:]
    none = NEAR * CAP
    bands = amps.shape[0]
    meta = own[0][CAP].astype(F32)
    for near in range(1, NEAR):
        meta = meta + pltpu.roll(own[near][CAP].astype(F32), near * CAP, 1)
    slot, kernel = meta[0:1], meta[1:2]
    amps[...] = meta[2 : 2 + bands]
    slot_of[...] = jnp.maximum(slot - 1.0, 0.0).astype(jnp.int32)
    live = (slot > 0.0).astype(F32)
    hot = (iota((num_slots, none), 0).astype(F32) == kernel).astype(F32) * live
    upto = (iota((none, none), 0) <= iota((none, none), 1)).astype(F32).astype(BF16)
    rank = dot(hot.astype(BF16), upto)
    size = jnp.max(rank, axis=1, keepdims=True)
    filled = ((size.astype(jnp.int32) + (GROUP - 1)) // GROUP).astype(F32)
    before = (iota((num_slots, num_slots), 1) < iota((num_slots, num_slots), 0)).astype(F32).astype(BF16)
    start = dot(before, jnp.broadcast_to(filled, (num_slots, none)).astype(BF16))
    place = jnp.sum(hot * (GROUP * start + rank), axis=0, keepdims=True) - 1.0
    eight = iota((8, none), 0)
    names = jnp.where(eight == 0, iota((8, none), 1).astype(F32) - none, 0.0).astype(BF16)
    for part in range(order.shape[1] // LANES):
        at = (iota((LANES, none), 0) + part * LANES).astype(F32)
        hit = (at == place).astype(F32) * live
        found = dot_nt(names, hit.astype(BF16))[:1] + none
        order[:, part * LANES : (part + 1) * LANES] = found.astype(jnp.int32)
    chunk = iota((num_slots, LANES), 1).astype(F32)
    row = iota((num_slots, LANES), 0).astype(F32)
    inside = (chunk >= start[:, :LANES]) & (chunk < start[:, :LANES] + filled)
    kernel_of[...] = jnp.sum(jnp.where(inside, row, 0.0), axis=0, keepdims=True).astype(jnp.int32)
    total = jnp.sum(filled, axis=0, keepdims=True)
    count[...] = jnp.broadcast_to(total, (1, LANES)).astype(jnp.int32)


def tables_kernel(bands, *refs):
    shards, (t_top, t_low, left, left_t, right, packed) = refs[:-6], refs[-6:]
    count = t_top.shape[0]
    for turn, ref in enumerate(shards):
        held = ref.shape[1]
        first = ((lax.axis_index("ra") + turn) % len(shards)) * (held * ROWS)
        for band in range(bands):
            for r in range(ROWS):
                rows = pl.ds(first + r, held, stride=ROWS)
                packed[band, rows, :] = ref[band, :, r * LANES : (r + 1) * LANES].astype(F32)
    eye = (iota((SIDE, SIDE), 0) == iota((SIDE, SIDE), 1)).astype(F32).astype(BF16)
    row, col = iota((SIDE, SIDE), 0), iota((SIDE, SIDE), 1)
    even = (col == 2 * (row % ROWS) + row // ROWS).astype(F32).astype(BF16)
    even_t = (row == 2 * (col % ROWS) + col // ROWS).astype(F32).astype(BF16)
    twice = (iota((SIDE, LANES), 1) % SIDE == iota((SIDE, LANES), 0)).astype(F32).astype(BF16)
    none = jnp.zeros((SIDE, WIDE), BF16)
    rest = [jnp.zeros((SIDE * (4 - bands), SIDE), BF16)] if bands < 4 else []

    def step(k, carry):
        parts = []
        for band in range(bands):
            both = packed[band, pl.ds(pl.multiple_of(k * ROWS, ROWS), ROWS), :]
            part = jnp.concatenate([both[:, :SIDE], turned(both)[:, :SIDE]], axis=0).astype(BF16)
            turned_part = dot_nt(part, even).astype(BF16)
            left[band, k] = turned_part
            left_t[band, k] = dot_nt(eye, turned_part).astype(BF16)
            parts.append(dot(even_t, part).astype(BF16))
        stack = jnp.concatenate(parts + rest, axis=0)
        first = dot_nt(eye, stack).astype(BF16)
        t_top[k] = jnp.concatenate([first, none], axis=0)
        t_low[k] = jnp.concatenate([none, first], axis=0)
        right[k] = dot(stack, twice).astype(BF16)
        return carry

    lax.fori_loop(0, count, step, 0, unroll=4)


def home_sums_kernel(bands, lists, amps, *refs):
    halves, sums = refs[:-1], refs[-1]
    if len(halves) == 1:
        spans = [(halves[0], 0, ROWS)]
    else:
        spans = [(halves[0], half_rows(False), HALF), (halves[1], half_rows(True), HALF)]
    sums[...] = jnp.zeros_like(sums)

    def add(s, carry):
        q = lists[0, s]
        for ref, start, size in spans:
            rows = pl.ds(start, size)
            stamp = ref[s].astype(F32)
            for band in range(bands):
                sums[band, q, rows, :] += amps[band, s] * stamp
        return carry

    lax.fori_loop(0, lists.shape[1], add, 0, unroll=4)


def home_forward_kernel(bands, sums, t_top, t_low, left, total):
    num_slots = total.shape[1]
    masks = half_masks(SIDE)

    def slot(q, carry):
        image = jnp.concatenate([sums[band, q] for band in range(bands)], axis=0).astype(BF16)
        top, low = dot(image, t_top[q]), dot(image, t_low[q])
        for band in range(bands):
            rows = slice(band * ROWS, (band + 1) * ROWS)
            lanes = slice(band // 2 * LANES, (band // 2 + 1) * LANES)
            inner = jnp.concatenate([top[rows, lanes], low[rows, lanes]], axis=0).astype(BF16)
            total[band, q] = jnp.where(masks[band % 2], dot(left[band, q], inner), 0.0)
        return carry

    lax.fori_loop(0, num_slots, slot, 0, unroll=8)


def visitors_kernel(bands, order, kernel_of, slot_of, amps, count, *refs):
    own, other = refs[:NEAR], refs[NEAR : 2 * NEAR]
    home, observed, t_top, t_low, left, left_t, right = refs[2 * NEAR : 2 * NEAR + 7]
    keep, send, meta, residual = refs[2 * NEAR + 7 : 2 * NEAR + 11]
    stamps, total, inner_all, sums = refs[2 * NEAR + 11 :]
    num_slots = home.shape[1]
    none = NEAR * CAP
    mine, theirs = pl.ds(half_rows(False), HALF), pl.ds(half_rows(True), HALF)
    for near in range(NEAR):

        def place(n, carry, near=near):
            stamps[near * CAP + n, mine, :] = own[near][n]
            stamps[near * CAP + n, theirs, :] = other[near][n]
            return carry

        lax.fori_loop(0, CAP, place, 0, unroll=8)
    stamps[none] = jnp.zeros((ROWS, LANES), BF16)
    total[...] = home[...]
    sums[...] = jnp.zeros_like(sums)
    keep[...] = jnp.zeros_like(keep)
    send[...] = jnp.zeros_like(send)
    masks, row_masks, packed_low = half_masks(SIDE), half_masks(1), half_masks(ROWS)[0]
    rounds = (count[0, 0] + STRIDE - 1) // STRIDE

    def chunk(c):
        members = [order[0, c * GROUP + u] for u in range(GROUP)]
        values = [
            [jnp.where(v < none, amps[band, jnp.minimum(v, none - 1)], 0.0) for v in members]
            for band in range(bands)
        ]
        return kernel_of[0, c], members, [slot_of[0, jnp.minimum(v, none - 1)] for v in members], values

    def forward(turn, carry):
        done = []
        for c in [STRIDE * turn + i for i in range(STRIDE)]:
            k, members, slots, values = chunk(c)
            stack = jnp.concatenate([stamps[v] for v in members], axis=0)
            top, low = dot(stack, t_top[k]), dot(stack, t_low[k])
            tiles = []
            for u in range(GROUP):
                rows = slice(u * ROWS, (u + 1) * ROWS)
                tiles.append(
                    [
                        jnp.concatenate([x[rows, t : t + LANES] for x in (top, low)], axis=0)
                        for t in (0, LANES)
                    ]
                )
            images = []
            for band in range(bands):
                t = band // 2
                pairs = []
                for u in range(0, GROUP, 2):
                    x, y = tiles[u][t], tiles[u + 1][t]
                    x, y = (x, turned(y)) if band % 2 == 0 else (turned(x), y)
                    pairs.append(jnp.where(masks[0], x, y))
                inner = jnp.concatenate(pairs, axis=1).astype(BF16)
                inner_all[c, band] = inner
                images.append(dot(left[band, k], inner))
            done.append((slots, values, images))
        for slots, values, images in done:
            for band in range(bands):
                for u, q in enumerate(slots):
                    lanes = slice(u // 2 * LANES, (u // 2 + 1) * LANES)
                    scale = jnp.where(row_masks[u % 2], values[band][u], 0.0)
                    total[band, q] += images[band][:, lanes] * scale
        return carry

    lax.fori_loop(0, rounds, forward, 0)
    low_rows = half_masks(ROWS)[0]

    def slot(q, carry):
        for band in range(bands):
            seen = observed[band, q].astype(F32)
            flip = turned(seen)
            seen = jnp.concatenate(
                [jnp.where(low_rows, seen, flip), jnp.where(low_rows, flip, seen)], axis=0
            )
            model = total[band, q]
            residual[band, q] = (model + turned(model) - seen).astype(BF16)
        return carry

    lax.fori_loop(0, num_slots, slot, 0, unroll=8)
    first_band = lax.axis_index("band") == 0

    def backward(turn, carry):
        for c in [STRIDE * turn + i for i in range(STRIDE)]:
            k, members, slots, values = chunk(c)
            outers = []
            for band in range(bands):
                pairs = [
                    jnp.where(masks[0], residual[band, slots[u]], residual[band, slots[u + 1]])
                    for u in range(0, GROUP, 2)
                ]
                outer = dot(left_t[band, k], jnp.concatenate(pairs, axis=1))
                along = jnp.sum(inner_all[c, band].astype(F32) * outer, axis=0, keepdims=True)
                scaled = []
                for u in range(0, GROUP, 2):
                    lanes = slice(u // 2 * LANES, (u // 2 + 1) * LANES)
                    for part in (0, 1):
                        row = jnp.where(row_masks[part], along[:, lanes], 0.0)
                        sums[band, pl.ds(members[u + part], 1), :] = row
                    scale = jnp.where(row_masks[0], values[band][u], values[band][u + 1])
                    scaled.append(outer[:, lanes] * scale)
                outers.append(scaled)
            outers += [[jnp.zeros((SIDE, LANES), F32)] * (GROUP // 2)] * (4 - bands)
            stack = []
            for pair in range(GROUP // 2):
                b0, b1, b2, b3 = [outers[band][pair] for band in range(4)]
                if bands > 3:
                    last = [jnp.where(masks[0], b2, turned(b3)), jnp.where(masks[0], turned(b2), b3)]
                else:
                    last = [b2, turned(b2)]
                stack.append(jnp.concatenate([jnp.where(masks[0], b0, turned(b1)), last[0]], axis=1))
                stack.append(jnp.concatenate([jnp.where(masks[0], turned(b0), b1), last[1]], axis=1))
            grads = dot(jnp.concatenate(stack, axis=0).astype(BF16), right[k])
            for u, v in enumerate(members):
                top = grads[u * SIDE : u * SIDE + ROWS]
                low = grads[u * SIDE + ROWS : (u + 1) * SIDE]
                stamp = jnp.where(packed_low, top, low)
                upper, lower = stamp[:HALF], stamp[HALF:]
                keep[v] = jnp.where(first_band, upper, lower).astype(BF16)
                send[v] = jnp.where(first_band, lower, upper).astype(BF16)
        return carry

    lax.fori_loop(0, rounds, backward, 0)
    ones = jnp.ones((8, LANES), F32)
    eight = iota((8, LANES), 0)
    grad_a = jnp.zeros((8, LANES), F32)
    for band in range(bands):
        total_a = dot_nt(ones, sums[band, :none, :], precision=lax.Precision.HIGHEST)
        grad_a = jnp.where(eight == band, total_a, grad_a)
    coarse = grad_a.astype(BF16)
    fine = (grad_a - coarse.astype(F32)).astype(BF16)
    meta[...] = jnp.concatenate([coarse.astype(F32), fine.astype(F32)], axis=0).astype(BF16)


def home_slots_kernel(bands, residual, left_t, right, back):
    num_slots = residual.shape[1]
    back[:, num_slots] = jnp.zeros((bands, ROWS, LANES), F32)
    packed_low = half_masks(ROWS)[0]

    def slot(q, carry):
        for band in range(bands):
            outer = dot(left_t[band, q], residual[band, q]).astype(BF16)
            grad = dot(outer[:, :SIDE], right[q, band * SIDE : (band + 1) * SIDE, :])
            back[band, q] = jnp.where(packed_low, grad[:ROWS], grad[ROWS:])
        return carry

    lax.fori_loop(0, num_slots, slot, 0, unroll=8)


def home_gather_kernel(bands, lists, amps, *refs):
    halves, (back, keep, send, grad_a, sums) = refs[:-5], refs[-5:]
    mine, theirs = pl.ds(half_rows(False), HALF), pl.ds(half_rows(True), HALF)

    def gather(s, carry):
        q = lists[0, s]
        parts = [0.0] * bands
        for turn, (rows, target) in enumerate(((mine, keep), (theirs, send))):
            if len(halves) == 1:
                stamp = halves[0][s, rows, :].astype(F32)
            else:
                stamp = halves[turn][s].astype(F32)
            grad = jnp.zeros((HALF, LANES), F32)
            for band in range(bands):
                seen = back[band, q, rows, :]
                grad = grad + amps[band, s] * seen
                parts[band] = parts[band] + seen * stamp
            target[s] = grad.astype(BF16)
        for band in range(bands):
            sums[band, pl.ds(s, 1), :] = jnp.sum(parts[band], axis=0, keepdims=True)
        return carry

    lax.fori_loop(0, lists.shape[1], gather, 0, unroll=4)
    ones = jnp.ones((8, LANES), F32)
    for band in range(bands):
        grad_a[band : band + 1, :] = dot_nt(ones, sums[band], precision=lax.Precision.HIGHEST)[:1]


def reduce_kernel(keep, received, meta, *messages):
    for near in range(NEAR):
        part = pl.ds(near * CAP, CAP)
        total = keep[part].astype(F32) + received[part].astype(F32)
        messages[near][pl.ds(0, CAP)] = total.astype(BF16)
        messages[near][CAP] = meta[...]


def update_kernel(
    num_slots, first, last, places, eta_m, slots_ref, eta_a, amps_ref, grad_a, morph, keep, received, *refs
):
    grads, out = refs[:NEAR], refs[NEAR:]
    state, amps_out = out[0], out[1]
    work = out[-1]
    sources = slots_ref.shape[1]
    work[...] = keep[...].astype(F32) + received[...].astype(F32)
    for near in range(NEAR):

        def add(n, carry, near=near):
            s = places[near * LIST + n]
            work[s] += grads[near][n].astype(F32)
            return carry

        lax.fori_loop(0, CAP, add, 0, unroll=4)
    rows = pl.ds(half_rows(False), HALF)

    def step(s, carry):
        old = morph[s, rows, :].astype(F32) if first else morph[s]
        new = jnp.maximum(old - eta_m[0, s] * work[s], 0.0)
        if last:
            work[s] = new
        else:
            state[s] = new
            out[2][s] = new.astype(BF16)
        return carry

    lax.fori_loop(0, sources, step, 0, unroll=8)
    if last:
        for r in range(HALF):
            state[:, r * LANES : (r + 1) * LANES] = work[:, r, :]
    slots = slots_ref[...]
    hots = list_hots(slots, num_slots)
    lane = iota((2 * 8, LANES), 1) // CAP
    meta = jnp.zeros((2 * 8, LANES), F32)
    for near in range(NEAR):
        meta = jnp.where(lane == near, grads[near][CAP].astype(F32), meta)
    all_hots = jnp.concatenate([hot[:CAP] for hot in hots], axis=0)
    from_near = dot(meta.astype(BF16), all_hots.astype(BF16))
    bands = amps_ref.shape[0]
    total = grad_a[...] + from_near[:bands] + from_near[8 : 8 + bands]
    amps = jnp.maximum(amps_ref[...] - eta_a[...] * total, 0.0)
    amps_out[...] = amps
    if last:
        return
    half, amps_q, messages = out[2], out[3], out[4 : 4 + NEAR]
    amps_q[...] = amps.astype(BF16).astype(F32)
    for near in range(NEAR):

        def pick(n, carry, near=near):
            messages[near][n] = half[places[near * LIST + n]]
            return carry

        lax.fori_loop(0, CAP, pick, 0, unroll=4)
    write_meta(messages, slots, amps, hots)


def call(body, name, operands, scalars, outs, scratch=(), smem_scratch=(), flops=0, moved=0):
    vmem, smem = pl.BlockSpec(memory_space=pltpu.VMEM), pl.BlockSpec(memory_space=pltpu.SMEM)
    return pl.pallas_call(
        body,
        out_shape=[jax.ShapeDtypeStruct(shape, dtype) for shape, dtype, _ in outs],
        in_specs=[smem if i < scalars else vmem for i in range(len(operands))],
        out_specs=[smem if flag else vmem for _, _, flag in outs],
        scratch_shapes=[pltpu.VMEM(shape, dtype) for shape, dtype in scratch]
        + [pltpu.SMEM(shape, dtype) for shape, dtype in smem_scratch],
        compiler_params=pltpu.CompilerParams(vmem_limit_bytes=40 * 2**20),
        cost_estimate=pl.CostEstimate(flops=flops, bytes_accessed=moved, transcendentals=0),
        name=name,
    )(*operands)


def sent(value, near):
    axis = "ra" if near < 2 else "dec"
    step = 1 if near % 2 == 0 else -1
    return moved_by(value, axis, step)


def returned(value, near):
    axis = "ra" if near < 2 else "dec"
    step = -1 if near % 2 == 0 else 1
    return moved_by(value, axis, step)


def moved_by(value, axis, step):
    count = lax.axis_size(axis)
    if axis == "ra":
        pairs = [(i, (i + step) % count) for i in range(count)]
    else:
        pairs = [(i, i + step) for i in range(count) if 0 <= i + step < count]
    return lax.ppermute(value, axis, pairs)


def swapped(value):
    return lax.ppermute(value, "band", [(0, 1), (1, 0)])


def all_kernels(psf, num_slots, messages):
    shards, held = lax.axis_size("ra"), psf.shape[1]
    if shards == 4 and 2 * held == num_slots:
        far = lax.ppermute(psf, "ra", [(0, 2), (1, 3)])
        here = jnp.where(lax.axis_index("ra") < 2, psf, far)
        here, *messages = lax.optimization_barrier((here, *messages))
        return (here, lax.ppermute(here, "ra", [(0, 1), (1, 0), (2, 3), (3, 2)])), messages
    return (lax.all_gather(psf, "ra", axis=1, tiled=True)[:, :num_slots],), messages


def shards(morphology, sed_amps, slot_lists, morph_step, sed_step, psf_kernels, observed):
    bands, num_slots, sources = sed_amps.shape[2], observed.shape[3], morphology.shape[2]
    lists, amps = slot_lists[0, 0], sed_amps[0, 0]
    eta_m, eta_a = morph_step[0], sed_step[0]
    full = morphology[0, 0].reshape(sources, ROWS, LANES)
    seen = observed[0, 0].reshape(bands, num_slots, ROWS, LANES)
    stamp = ((CAP + 1, HALF, LANES), BF16, False)
    near_all = NEAR * CAP
    chunks = -(-(near_all // GROUP + num_slots) // STRIDE) * STRIDE

    *messages, places, amps_q = call(
        functools.partial(pack_kernel, num_slots),
        "pack",
        (lists, lists, amps, full),
        1,
        [stamp] * NEAR + [((NEAR * LIST,), jnp.int32, True), ((bands, sources), F32, False)],
        moved=2**20,
    )
    kernels, messages = all_kernels(psf_kernels, num_slots, messages)
    square = ((bands, num_slots, SIDE, SIDE), BF16, False)
    full_table = ((num_slots, LANES, WIDE), BF16, False)
    t_top, t_low, left, left_t, right = call(
        functools.partial(tables_kernel, bands),
        "tables",
        kernels,
        0,
        [full_table, full_table, square, square, ((num_slots, WIDE, LANES), BF16, False)],
        [((bands, num_slots * ROWS, LANES), F32)],
        flops=2 * 10**9,
        moved=5 * 2**20,
    )
    slot_stamps = ((bands, num_slots + 1, ROWS, LANES), F32, False)
    morph = (full,)
    state = full
    for sweep in range(ITERS):
        last = sweep == ITERS - 1
        own = [sent(messages[near], near) for near in range(NEAR)]
        sums = call(
            functools.partial(home_sums_kernel, bands),
            "home_sums",
            (lists, amps_q, *morph),
            2,
            [slot_stamps],
            moved=4 * 2**20,
        )[0]
        if sweep == 0:
            sums, t_top, *own = lax.optimization_barrier((sums, t_top, *own))
        else:
            sums, *own = lax.optimization_barrier((sums, *own))
        other = [swapped(x) for x in own]
        home = call(
            functools.partial(home_forward_kernel, bands),
            "home_forward",
            (sums, t_top, t_low, left),
            0,
            [((bands, num_slots, SIDE, LANES), F32, False)],
            flops=2 * 10**9,
            moved=4 * 2**20,
        )[0]
        order = call(
            functools.partial(order_kernel, num_slots),
            "order",
            own,
            0,
            [
                ((1, -(-chunks * GROUP // LANES) * LANES), jnp.int32, False),
                ((1, LANES), jnp.int32, False),
                ((1, LANES), jnp.int32, False),
                ((bands, LANES), F32, False),
                ((1, LANES), jnp.int32, False),
            ],
            moved=2**20,
        )
        keep, send, grad_meta, residual = call(
            functools.partial(visitors_kernel, bands),
            "visitors",
            (
                *order,
                *own,
                *other,
                home,
                seen,
                t_top,
                t_low,
                left,
                left_t,
                right,
            ),
            5,
            [
                ((near_all + 1, HALF, LANES), BF16, False),
                ((near_all + 1, HALF, LANES), BF16, False),
                ((2 * 8, LANES), BF16, False),
                ((bands, num_slots, SIDE, LANES), BF16, False),
            ],
            [
                ((near_all + 1, ROWS, LANES), BF16),
                ((bands, num_slots, SIDE, LANES), F32),
                ((chunks, bands, SIDE, WIDE), BF16),
                ((bands, near_all + 8, LANES), F32),
            ],
            flops=6 * 10**9,
            moved=8 * 2**20,
        )
        received = swapped(send)
        back = call(
            functools.partial(home_slots_kernel, bands),
            "home_slots",
            (residual, left_t, right),
            0,
            [slot_stamps],
            flops=2 * 10**9,
            moved=4 * 2**20,
        )[0]
        received, back = lax.optimization_barrier((received, back))
        grads = call(
            reduce_kernel,
            "reduce",
            (keep, received, grad_meta),
            0,
            [stamp] * NEAR,
            moved=2 * 2**20,
        )
        grads = [returned(grads[near], near) for near in range(NEAR)]
        home_keep, home_send, grad_a = call(
            functools.partial(home_gather_kernel, bands),
            "home_gather",
            (lists, amps_q, *morph, back),
            2,
            [
                ((sources, HALF, LANES), BF16, False),
                ((sources, HALF, LANES), BF16, False),
                ((bands, sources), F32, False),
            ],
            [((bands, sources, LANES), F32)],
            moved=4 * 2**20,
        )
        home_received = swapped(home_send)
        shape = (sources, HALF * LANES) if last else (sources, HALF, LANES)
        outs = [(shape, F32, False), ((bands, sources), F32, False)]
        if not last:
            outs += [((sources, HALF, LANES), BF16, False), ((bands, sources), F32, False)] + [stamp] * NEAR
        state, amps, *more = call(
            functools.partial(update_kernel, num_slots, sweep == 0, last),
            "update",
            (places, eta_m, lists, eta_a, amps, grad_a, state, home_keep, home_received, *grads),
            2,
            outs,
            [((sources, HALF, LANES), F32)],
            moved=3 * 2**20,
        )
        if not last:
            half, amps_q, *messages = more
            morph = (half, swapped(half))
    return state[None, None], amps[None, None]


def solution(mesh):
    in_specs = (
        P("ra", "dec", None, None),
        P("ra", "dec", "band", None),
        P("ra", "dec", None, None),
        P("ra", "dec", None),
        P("ra", "dec", None),
        P("band", "ra", None),
        P("ra", "dec", "band", None, None),
    )
    out_specs = (P("ra", "dec", None, "band"), P("ra", "dec", "band", None))
    return jax.shard_map(shards, mesh=mesh, in_specs=in_specs, out_specs=out_specs, check_vma=False)
```

```python
import functools

import jax
import jax.numpy as jnp
from jax import lax
from jax.experimental import pallas as pl
from jax.experimental.pallas import tpu as pltpu
from jax.sharding import PartitionSpec as P

SIDE = 64
KERN = 32
ITERS = 2
CAP = 32
LANES = 128
ROWS = SIDE * SIDE // LANES
HALF = ROWS // 2
WIDE = 4 * SIDE
ORDER, KERNEL_OF, SLOT_OF, COUNT = range(4)
NEAR = 4
GROUP = 4
STRIDE = 4
F32 = jnp.float32
BF16 = jnp.bfloat16


def dot(a, b):
    return lax.dot_general(a, b, (((1,), (0,)), ((), ())), preferred_element_type=F32)


def dot_nt(a, b):
    return lax.dot_general(a, b, (((1,), (1,)), ((), ())), preferred_element_type=F32)


def iota(shape, dim):
    return lax.broadcasted_iota(jnp.int32, shape, dim)


def low_lanes(rows, dtype=F32):
    return (iota((rows, LANES), 1) < SIDE).astype(F32).astype(dtype)


def lane_sums(rows):
    coarse = rows.astype(BF16)
    fine = (rows - coarse.astype(F32)).astype(BF16)
    ones = jnp.ones((8, rows.shape[1]), BF16)
    return dot_nt(ones, coarse) + dot_nt(ones, fine)


def half_masks(rows):
    low = iota((rows, LANES), 1) < SIDE
    return low, jnp.logical_not(low)


def turned(value):
    return pltpu.roll(value, SIDE, 1)


def twofold(packed):
    low, flip = half_masks(ROWS)[0], turned(packed)
    return jnp.concatenate([jnp.where(low, packed, flip), jnp.where(low, flip, packed)], axis=0)


def half_rows():
    return pl.multiple_of(lax.axis_index("band") * HALF, HALF)


def by_core(mine, theirs):
    first = lax.axis_index("band") == 0
    return jnp.where(first, mine, theirs), jnp.where(first, theirs, mine)


def lists_kernel(num_slots, slots_ref, hots, places):
    slots = slots_ref[...]
    sources = slots.shape[1]
    valid = (slots < num_slots).astype(F32)
    upper = (iota((sources, sources), 0) <= iota((sources, sources), 1)).astype(F32)
    rank = dot(valid.astype(BF16), upper.astype(BF16))
    place = iota((LANES, sources), 0).astype(F32)
    names = iota((8, sources), 1).astype(F32).astype(BF16)
    for near in range(NEAR):
        row = slice(near + 1, near + 2)
        hot = ((place == rank[row] - 1.0).astype(F32) * valid[row]).astype(BF16)
        hots[near] = hot
        places[near : near + 1, :] = dot_nt(names, hot)[:1].astype(jnp.int32)
        count = jnp.broadcast_to(rank[row, sources - 1 :], (1, LANES))
        places[NEAR + near : NEAR + near + 1, :] = count.astype(jnp.int32)


def write_messages(messages, slots, amps, hots, places, stamps):
    first = lax.axis_index("band") == 0
    row = iota((ROWS, slots.shape[1]), 0)
    for turn in range(2):
        near = 2 * turn + lax.axis_index("band")

        def pick(n, carry, near=near, turn=turn):
            messages[turn][n] = stamps[places[near, n]]
            return carry

        lax.fori_loop(0, CAP, pick, 0, unroll=8)
        slot = jnp.where(first, slots[2 * turn + 1 : 2 * turn + 2], slots[2 * turn + 2 : 2 * turn + 3]).astype(F32)
        meta = jnp.where(row == 0, slot + 1.0, 0.0)
        meta = jnp.where(row == 1, slots[0:1].astype(F32), meta)
        for band in range(amps.shape[0]):
            meta = jnp.where(row == 2 + band, amps[band : band + 1], meta)
        hot = jnp.where(first, hots[2 * turn].astype(F32), hots[2 * turn + 1].astype(F32)).astype(BF16)
        messages[turn][CAP] = dot_nt(meta.astype(BF16), hot).astype(BF16)


def pack_kernel(places, slots_ref, amps_mine, amps_theirs, hots, morph, *out):
    messages, amps_out, amps_q = out[:2], out[2], out[3]
    amps = jnp.concatenate(by_core(amps_mine[...], amps_theirs[...]), axis=0)
    write_messages(messages, slots_ref[...], amps, hots, places, morph)
    amps_out[...] = amps
    amps_q[...] = amps.astype(BF16).astype(F32)


def order_kernel(num_slots, *refs):
    plan, amps = refs[NEAR:]
    none = NEAR * CAP
    bands = amps.shape[0]
    meta = jnp.zeros((ROWS, LANES), F32)
    for turn in range(2):
        pair = by_core(refs[turn][CAP].astype(F32), refs[2 + turn][CAP].astype(F32))
        for core in range(2):
            meta = meta + pltpu.roll(pair[core], (2 * turn + core) * CAP, 1)
    slot, kernel = meta[0:1], meta[1:2]
    amps[...] = by_core(meta[2 : 2 + bands], meta[2 + bands : 2 + 2 * bands])[0]
    plan[SLOT_OF : SLOT_OF + 1, :LANES] = jnp.maximum(slot - 1.0, 0.0).astype(jnp.int32)
    live = (slot > 0.0).astype(F32)
    hot = (iota((num_slots, none), 0).astype(F32) == kernel).astype(F32) * live
    upto = (iota((none, none), 0) <= iota((none, none), 1)).astype(F32).astype(BF16)
    rank = dot(hot.astype(BF16), upto)
    size = jnp.max(rank, axis=1, keepdims=True)
    filled = ((size.astype(jnp.int32) + (GROUP - 1)) // GROUP).astype(F32)
    before = (iota((num_slots, num_slots), 1) < iota((num_slots, num_slots), 0)).astype(F32).astype(BF16)
    start = dot(before, jnp.broadcast_to(filled, (num_slots, none)).astype(BF16))
    place = jnp.sum(hot * (GROUP * start + rank), axis=0, keepdims=True) - 1.0
    eight = iota((8, none), 0)
    names = jnp.where(eight == 0, iota((8, none), 1).astype(F32) - none, 0.0).astype(BF16)
    for part in range(plan.shape[1] // LANES):
        at = (iota((LANES, none), 0) + part * LANES).astype(F32)
        hit = (at == place).astype(F32) * live
        found = dot_nt(names, hit.astype(BF16))[:1] + none
        plan[ORDER : ORDER + 1, part * LANES : (part + 1) * LANES] = found.astype(jnp.int32)
    chunk = iota((num_slots, LANES), 1).astype(F32)
    row = iota((num_slots, LANES), 0).astype(F32)
    inside = (chunk >= start[:, :LANES]) & (chunk < start[:, :LANES] + filled)
    kernels = jnp.sum(jnp.where(inside, row, 0.0), axis=0, keepdims=True)
    plan[KERNEL_OF : KERNEL_OF + 1, :LANES] = kernels.astype(jnp.int32)
    total = jnp.sum(filled, axis=0, keepdims=True)
    plan[COUNT : COUNT + 1, :LANES] = jnp.broadcast_to(total, (1, LANES)).astype(jnp.int32)


def quarter_start(quarter, held):
    parity, line = lax.axis_index("ra") % 2, lax.axis_index("dec") % 2
    shard = parity if quarter % 2 == 0 else 1 - parity
    half = line if quarter < 2 else 1 - line
    return (2 * shard + half) * held


def tables_kernel(bands, earlier, *refs):
    shards, (first_t, left, left_t, right, packed) = refs[: len(refs) - 5 - 4 * earlier], refs[-5:]
    held = shards[0].shape[1]
    for turn, ref in enumerate(shards):
        for band in range(bands):
            for r in range(ROWS):
                rows = pl.ds(turn * held * ROWS + r, held, stride=ROWS)
                packed[band, rows, :] = ref[band, :, r * LANES : (r + 1) * LANES].astype(F32)
    starts = [quarter_start(2 + turn, held) if earlier else turn * held for turn in range(len(shards))]
    if earlier:
        old_first, old_left, old_left_t, old_right = refs[len(shards) : len(shards) + 4]
        for turn in range(2):
            old, new = pl.ds(turn * held, held), pl.ds(quarter_start(turn, held), held)
            first_t[new] = old_first[old]
            right[new] = old_right[old]
            for band in range(bands):
                left[band, new] = old_left[band, old]
                left_t[band, new] = old_left_t[band, old]
    eye = (iota((SIDE, SIDE), 0) == iota((SIDE, SIDE), 1)).astype(F32).astype(BF16)
    row, col = iota((SIDE, SIDE), 0), iota((SIDE, SIDE), 1)
    even = (col == 2 * (row % ROWS) + row // ROWS).astype(F32).astype(BF16)
    even_t = (row == 2 * (col % ROWS) + col // ROWS).astype(F32).astype(BF16)
    rest = [jnp.zeros((SIDE * (4 - bands), SIDE), BF16)] if bands < 4 else []
    for turn, start in enumerate(starts):

        def step(place, carry, turn=turn, start=start):
            k = start + place
            at = pl.multiple_of((turn * held + place) * ROWS, ROWS)
            parts = [twofold(packed[band, pl.ds(at, ROWS), :]).astype(BF16) for band in range(bands)]
            lefts = dot_nt(jnp.concatenate([part[:, :SIDE] for part in parts], axis=0), even).astype(BF16)
            natural = []
            for band, part in enumerate(parts):
                rows = slice(band * SIDE, (band + 1) * SIDE)
                left[band, k] = lefts[rows]
                left_t[band, k] = dot_nt(eye, lefts[rows]).astype(BF16)
                both = dot(even_t, part).astype(BF16)
                right[k, rows, :] = both
                natural.append(both[:, :SIDE])
            if rest:
                right[k, bands * SIDE :, :] = jnp.zeros((SIDE * (4 - bands), LANES), BF16)
            first_t[k] = dot_nt(eye, jnp.concatenate(natural + rest, axis=0)).astype(BF16)
            return carry

        lax.fori_loop(0, held, step, 0, unroll=min(held, 4))


def make_tables(shards, bands, earlier=()):
    count = sum(x.shape[1] for x in shards)
    total = count + sum(x.shape[0] for x in earlier[:1])
    square = ((bands, total, SIDE, SIDE), BF16, False)
    return call(
        functools.partial(tables_kernel, bands, bool(earlier)),
        "tables",
        (*shards, *earlier),
        0,
        [((total, SIDE, WIDE), BF16, False), square, square, ((total, WIDE, LANES), BF16, False)],
        [((bands, count * ROWS, LANES), F32)],
        flops=2 * 10**9,
        moved=5 * 2**20,
    )


def home_sums_kernel(bands, lists, amps, morph, sums):
    first = lax.axis_index("band") * bands
    sums[...] = jnp.zeros_like(sums)

    def add(s, carry):
        q = lists[0, s]
        stamp = morph[s].astype(F32)
        for band in range(bands):
            sums[band, q] += amps[first + band, s] * stamp
        return carry

    lax.fori_loop(0, lists.shape[1], add, 0, unroll=4)


def home_forward_kernel(bands, sums, first_t, left, total, inner_all):
    num_slots = total.shape[1]
    masks = half_masks(SIDE)

    def inner_products(q, carry):
        images = []
        for band in range(bands):
            both = sums[band, q]
            images += [both[:, :SIDE], turned(both)[:, :SIDE]]
        inners = dot(jnp.concatenate(images, axis=0).astype(BF16), first_t[q])
        for band in range(bands):
            lanes = slice(band // 2 * LANES, (band // 2 + 1) * LANES)
            inner_all[band, q] = inners[band * SIDE : (band + 1) * SIDE, lanes].astype(BF16)
        return carry

    def slot(q, carry):
        for band in range(bands):
            total[band, q] = jnp.where(masks[band % 2], dot(left[band, q], inner_all[band, q]), 0.0)
        return carry

    lax.fori_loop(0, num_slots, inner_products, 0, unroll=4)
    lax.fori_loop(0, num_slots, slot, 0, unroll=4)


def chunk_reader(bands, plan, amps):
    none = NEAR * CAP

    def read(c):
        members = [plan[ORDER, c * GROUP + u] for u in range(GROUP)]
        held = [jnp.minimum(v, none - 1) for v in members]
        values = [[jnp.where(v < none, amps[band, h], 0.0) for v, h in zip(members, held)] for band in range(bands)]
        return plan[KERNEL_OF, c], members, [plan[SLOT_OF, h] for h in held], values

    return read, (plan[COUNT, 0] + STRIDE - 1) // STRIDE


def forward_kernel(bands, plan, amps, *refs):
    home, observed, first_t, left = refs[NEAR : NEAR + 4]
    residual, inner_all, stamps, *totals = refs[NEAR + 4 :]
    totals = [totals[2 * band : 2 * band + 2] for band in range(bands)]
    num_slots = home.shape[1]
    none = NEAR * CAP
    core = lax.axis_index("band")
    for source, near in enumerate((core, 2 + core, 1 - core, 3 - core)):
        group = pl.ds(near * CAP, CAP)
        even = refs[source][pl.ds(0, CAP)].astype(F32)
        odd = turned(even.reshape(CAP * ROWS, LANES)).reshape(CAP, ROWS, LANES)
        stamps[group, pl.ds(0, ROWS), :] = even.astype(BF16)
        stamps[group, pl.ds(ROWS, ROWS), :] = odd.astype(BF16)
    stamps[none] = jnp.zeros((SIDE, LANES), BF16)
    for band in range(bands):
        totals[band][band % 2][...] = home[band]
        totals[band][1 - band % 2][...] = jnp.zeros_like(home[band])
    masks, row_masks = half_masks(SIDE), half_masks(1)
    read, rounds = chunk_reader(bands, plan, amps)

    def inner_products(turn, carry):
        for c in [STRIDE * turn + i for i in range(STRIDE)]:
            k, members, _, _ = read(c)
            stack = jnp.concatenate([stamps[v] for v in members], axis=0)
            inners = dot(stack[:, :SIDE], first_t[k])
            for band in range(bands):
                lanes = slice(band // 2 * LANES, (band // 2 + 1) * LANES)
                pairs = []
                for u in range(0, GROUP, 2):
                    x = inners[u * SIDE : (u + 1) * SIDE, lanes]
                    y = inners[(u + 1) * SIDE : (u + 2) * SIDE, lanes]
                    x, y = (x, turned(y)) if band % 2 == 0 else (turned(x), y)
                    pairs.append(jnp.where(masks[0], x, y))
                inner_all[c, band] = jnp.concatenate(pairs, axis=1).astype(BF16)
        return carry

    def images(turn, carry):
        for c in [STRIDE * turn + i for i in range(STRIDE)]:
            k, _, slots, values = read(c)
            for band in range(bands):
                image = dot(left[band, k], inner_all[c, band])
                for u in range(0, GROUP, 2):
                    lanes = slice(u // 2 * LANES, (u // 2 + 1) * LANES)
                    scale = jnp.where(row_masks[0], values[band][u], values[band][u + 1])
                    pair = image[:, lanes] * scale
                    for part in (0, 1):
                        totals[band][part][slots[u + part]] += pair
        return carry

    lax.fori_loop(0, rounds, inner_products, 0)
    lax.fori_loop(0, rounds, images, 0)

    def slot(q, carry):
        for band in range(bands):
            model = jnp.where(masks[0], totals[band][0][q], totals[band][1][q])
            seen = twofold(observed[band, q].astype(F32))
            residual[band, q] = (model + turned(model) - seen).astype(BF16)
        return carry

    lax.fori_loop(0, num_slots, slot, 0, unroll=8)


def backward_kernel(bands, plan, amps, *refs):
    residual, inner_all, left_t, right, keep, send, stacks, sums = refs
    none = NEAR * CAP
    sums[...] = jnp.zeros_like(sums)
    masks, row_masks, packed_low = half_masks(SIDE), half_masks(1), half_masks(ROWS)[0]
    read, rounds = chunk_reader(bands, plan, amps)
    spare = none // 2
    core = lax.axis_index("band")

    def outer_products(turn, carry):
        for c in [STRIDE * turn + i for i in range(STRIDE)]:
            k, members, slots, values = read(c)
            outers = []
            for band in range(bands):
                pairs = [
                    jnp.where(masks[0], residual[band, slots[u]], residual[band, slots[u + 1]])
                    for u in range(0, GROUP, 2)
                ]
                outer = dot(left_t[band, k], jnp.concatenate(pairs, axis=1))
                along = jnp.sum(inner_all[c, band].astype(F32) * outer, axis=0, keepdims=True)
                scaled = []
                for u in range(0, GROUP, 2):
                    lanes = slice(u // 2 * LANES, (u // 2 + 1) * LANES)
                    for part in (0, 1):
                        row = jnp.where(row_masks[part], along[:, lanes], 0.0)
                        sums[band, pl.ds(members[u + part], 1), :] = row
                    scale = jnp.where(row_masks[0], values[band][u], values[band][u + 1])
                    scaled.append(outer[:, lanes] * scale)
                outers.append(scaled)
            outers += [[jnp.zeros((SIDE, LANES), F32)] * (GROUP // 2)] * (4 - bands)
            for pair in range(GROUP // 2):
                b0, b1, b2, b3 = [outers[band][pair] for band in range(4)]
                if bands > 3:
                    last = [jnp.where(masks[0], b2, turned(b3)), jnp.where(masks[0], turned(b2), b3)]
                else:
                    last = [b2, turned(b2)]
                first = [jnp.where(masks[0], b0, turned(b1)), jnp.where(masks[0], turned(b0), b1)]
                for part in (0, 1):
                    rows = slice((2 * pair + part) * SIDE, (2 * pair + part + 1) * SIDE)
                    stacks[c, rows, :] = jnp.concatenate([first[part], last[part]], axis=1).astype(BF16)
        return carry

    def gradients(turn, carry):
        for c in [STRIDE * turn + i for i in range(STRIDE)]:
            k, members, _, _ = read(c)
            grads = dot(stacks[c], right[k])
            for u, v in enumerate(members):
                top = grads[u * SIDE : u * SIDE + ROWS]
                low = grads[u * SIDE + ROWS : (u + 1) * SIDE]
                stamp = jnp.where(packed_low, top, low).astype(BF16)
                side, place = v // CAP % 2, v // (2 * CAP) * CAP + v % CAP
                keep[jnp.where(side == core, place, spare)] = stamp
                send[jnp.where(side == 1 - core, place, spare)] = stamp
        return carry

    lax.fori_loop(0, rounds, outer_products, 0)
    lax.fori_loop(0, rounds, gradients, 0)
    meta = amp_rows([lane_sums(sums[band, :none, :]) for band in range(bands)])
    keep[spare] = meta
    send[spare] = meta


def home_slots_kernel(bands, residual, left_t, right, back):
    num_slots = residual.shape[1]
    back[:, num_slots] = jnp.zeros((bands, ROWS, LANES), BF16)
    packed_low = half_masks(ROWS)[0]

    def slot(q, carry):
        for band in range(bands):
            outer = dot(left_t[band, q], residual[band, q]).astype(BF16)
            grad = dot(outer[:, :SIDE], right[q, band * SIDE : (band + 1) * SIDE, :])
            back[band, q] = jnp.where(packed_low, grad[:ROWS], grad[ROWS:]).astype(BF16)
        return carry

    lax.fori_loop(0, num_slots, slot, 0, unroll=8)


def home_gather_kernel(bands, last, lists, amps, morph, back, received, keep, grad_a, sums):
    core = lax.axis_index("band")
    mine = pl.ds(half_rows(), HALF) if last else pl.ds(0, ROWS)

    def gather(s, carry):
        q = lists[0, s]
        stamp = morph[s].astype(F32)
        grad = jnp.zeros((HALF if last else ROWS, LANES), F32)
        for ref, side in ((back, core), (received, 1 - core)):
            for band in range(bands):
                amp = amps[side * bands + band, s]
                if last:
                    grad = grad + amp * ref[band, q, mine, :].astype(F32)
                    if ref is received:
                        continue
                seen = ref[band, q].astype(F32)
                if not last:
                    grad = grad + amp * seen
                along = jnp.sum(seen * stamp, axis=0, keepdims=True)
                sums[side * bands + band, pl.ds(s, 1), :] = along
        keep[s] = grad
        return carry

    lax.fori_loop(0, lists.shape[1], gather, 0, unroll=4)
    for band in range(grad_a.shape[0]):
        rows = sums[core * bands + band] if last else sums[band]
        grad_a[band : band + 1, :] = lane_sums(rows)[:1]


def amp_rows(sums):
    eight = iota((8, LANES), 0)
    total = jnp.zeros((8, LANES), F32)
    for band, row in enumerate(sums):
        total = jnp.where(eight == band, row, total)
    coarse = total.astype(BF16).astype(F32)
    return jnp.concatenate([coarse, total - coarse, jnp.zeros((HALF, LANES), F32)], axis=0).astype(BF16)


def reduce_kernel(keep, received, *messages):
    for turn in range(2):
        part = pl.ds(turn * CAP, CAP)
        total = keep[part].astype(F32) + received[part].astype(F32)
        messages[turn][pl.ds(0, CAP)] = total.astype(BF16)
        pair = by_core(keep[2 * CAP].astype(F32), received[2 * CAP].astype(F32))
        meta = jnp.concatenate([pair[0][:HALF], pair[1][:HALF]], axis=0)
        messages[turn][CAP] = meta.astype(BF16)


def update_kernel(first, last, places, eta_m, slots_ref, eta_a, hots, amps_ref, grad_a, morph, home, *refs):
    grads, out = refs[:NEAR], refs[NEAR:]
    state, amps_out, work = out[0], out[1], out[-1]
    sources = slots_ref.shape[1]
    core = lax.axis_index("band")
    mine = pl.ds(half_rows(), HALF) if last else pl.ds(0, ROWS)
    nears = (core, 2 + core, 1 - core, 3 - core)
    work[...] = home[...]
    for ref, near in zip(grads, nears):

        def add(n, carry, ref=ref, near=near):
            work[places[near, n]] += ref[n, mine, :].astype(F32)
            return carry

        lax.fori_loop(0, places[NEAR + near, 0], add, 0)

    def step(s, carry):
        new = jnp.maximum(morph[s, mine, :].astype(F32) - eta_m[0, s] * work[s], 0.0)
        if last:
            work[s] = new
        else:
            state[s] = new
            out[2][s] = new.astype(BF16)
        return carry

    lax.fori_loop(0, sources, step, 0, unroll=8)
    if last:
        for r in range(HALF):
            state[:, r * LANES : (r + 1) * LANES] = work[:, r, :]
    lane = iota((ROWS, LANES), 1) // CAP
    meta = jnp.zeros((ROWS, LANES), F32)
    for ref, near in zip(grads, nears):
        meta = jnp.where(lane == near, ref[CAP].astype(F32), meta)
    all_hots = jnp.concatenate([hots[near, :CAP] for near in range(NEAR)], axis=0)
    from_near = dot(meta.astype(BF16), all_hots)
    bands = amps_ref.shape[0] // 2
    sides = [from_near[r : r + bands] + from_near[r + 8 : r + 8 + bands] for r in (0, HALF)]
    if last:
        amps = by_core(amps_ref[:bands], amps_ref[bands:])[0]
        total = grad_a[...] + by_core(sides[0], sides[1])[0]
    else:
        amps = amps_ref[...]
        total = grad_a[...] + jnp.concatenate(sides, axis=0)
    amps = jnp.maximum(amps - eta_a[...] * total, 0.0)
    amps_out[...] = amps
    if last:
        return
    stamps, amps_q, messages = out[2], out[3], out[4:6]
    amps_q[...] = amps.astype(BF16).astype(F32)
    write_messages(messages, slots_ref[...], amps, hots, places, stamps)


def call(body, name, operands, scalars, outs, scratch=(), smem_scratch=(), flops=0, moved=0):
    vmem, smem = pl.BlockSpec(memory_space=pltpu.VMEM), pl.BlockSpec(memory_space=pltpu.SMEM)
    return pl.pallas_call(
        body,
        out_shape=[jax.ShapeDtypeStruct(shape, dtype) for shape, dtype, _ in outs],
        in_specs=[smem if i < scalars else vmem for i in range(len(operands))],
        out_specs=[smem if flag else vmem for _, _, flag in outs],
        scratch_shapes=[pltpu.VMEM(shape, dtype) for shape, dtype in scratch]
        + [pltpu.SMEM(shape, dtype) for shape, dtype in smem_scratch],
        compiler_params=pltpu.CompilerParams(vmem_limit_bytes=40 * 2**20),
        cost_estimate=pl.CostEstimate(flops=flops, bytes_accessed=moved, transcendentals=0),
        name=name,
    )(*operands)


def stepped(value, axis, step):
    shape = [lax.axis_size(name) for name in ("ra", "dec", "band")]

    def device(ra, dec, band):
        return (ra * shape[1] + dec) * shape[2] + band

    pairs = []
    for ra in range(shape[0]):
        for dec in range(shape[1]):
            for band, by in ((0, step), (1, -step)):
                if axis == "ra":
                    pairs.append((device(ra, dec, band), device((ra + by) % shape[0], dec, band)))
                elif 0 <= dec + by < shape[1]:
                    pairs.append((device(ra, dec, band), device(ra, dec + by, band)))
    return lax.ppermute(value, ("ra", "dec", "band"), pairs)


def swapped(value):
    return lax.ppermute(value, "band", [(0, 1), (1, 0)])


def all_tables(psf, num_slots, messages, morph):
    bands, held = psf.shape[:2]
    lines = lax.axis_size("dec")
    if lax.axis_size("ra") == 4 and 2 * held == num_slots and held % 2 == 0 and lines % 2 == 0:
        across = [(i, i + 1 - 2 * (i % 2)) for i in range(lines)]
        along = [(0, 1), (1, 0), (2, 3), (3, 2)]
        mine = jnp.where(lax.axis_index("dec") % 2 == 0, psf[:, : held // 2], psf[:, held // 2 :])
        far = lax.ppermute(mine, "ra", [(0, 2), (1, 3)])
        here = jnp.where(lax.axis_index("ra") < 2, mine, far)
        here, *messages = lax.optimization_barrier((here, *messages))
        near = lax.ppermute(here, "ra", along)
        near, morph, messages[1] = lax.optimization_barrier((near, morph, messages[1]))
        halves = make_tables((here, near), bands)
        others = (lax.ppermute(here, "dec", across), lax.ppermute(near, "dec", across))
        return make_tables(others, bands, halves), messages, morph
    return make_tables((lax.all_gather(psf, "ra", axis=1, tiled=True)[:, :num_slots],), bands), messages, morph


def shards(morphology, sed_amps, slot_lists, morph_step, sed_step, psf_kernels, observed):
    bands, num_slots, sources = sed_amps.shape[2], observed.shape[3], morphology.shape[2]
    lists, amps = slot_lists[0, 0], sed_amps[0, 0]
    eta_m, eta_a = morph_step[0], sed_step[0]
    full = morphology[0, 0].reshape(sources, ROWS, LANES)
    seen = observed[0, 0].reshape(bands, num_slots, ROWS, LANES)
    stamp = ((CAP + 1, ROWS, LANES), BF16, False)
    all_stamps = (sources, ROWS, LANES)
    near_all = NEAR * CAP
    chunks = -(-(near_all // GROUP + num_slots) // STRIDE) * STRIDE
    amps_theirs = swapped(amps)
    hots, places = call(
        functools.partial(lists_kernel, num_slots),
        "lists",
        (lists,),
        0,
        [
            ((NEAR, LANES, sources), BF16, False),
            ((2 * NEAR, LANES), jnp.int32, False),
        ],
        moved=2**20,
    )
    *messages, amps, amps_q = call(
        pack_kernel,
        "pack",
        (places, lists, amps, amps_theirs, hots, full),
        1,
        [stamp] * 2 + [((2 * bands, sources), F32, False)] * 2,
        moved=2**20,
    )
    (first_t, left, left_t, right), messages, morph = all_tables(psf_kernels, num_slots, messages, full)
    state = full
    for sweep in range(ITERS):
        last = sweep == ITERS - 1
        own = [stepped(messages[0], "ra", 1), stepped(messages[1], "dec", 1)]
        sums = call(
            functools.partial(home_sums_kernel, bands),
            "home_sums",
            (lists, amps_q, morph),
            2,
            [((bands, num_slots + 1, ROWS, LANES), F32, False)],
            moved=4 * 2**20,
        )[0]
        home = call(
            functools.partial(home_forward_kernel, bands),
            "home_forward",
            (sums, first_t, left),
            0,
            [((bands, num_slots, SIDE, LANES), F32, False)],
            [((bands, num_slots, SIDE, LANES), BF16)],
            flops=2 * 10**9,
            moved=4 * 2**20,
        )[0]
        home, *own = lax.optimization_barrier((home, *own))
        other = [swapped(x) for x in own]
        order = call(
            functools.partial(order_kernel, num_slots),
            "order",
            (*own, *other),
            0,
            [
                ((8, -(-chunks * GROUP // LANES) * LANES), jnp.int32, False),
                ((bands, LANES), F32, False),
            ],
            moved=2**20,
        )
        residual, inner_all = call(
            functools.partial(forward_kernel, bands),
            "forward",
            (*order, *own, *other, home, seen, first_t, left),
            2,
            [
                ((bands, num_slots, SIDE, LANES), BF16, False),
                ((chunks, bands, SIDE, WIDE), BF16, False),
            ],
            [((near_all + 1, SIDE, LANES), BF16)] + [((num_slots, SIDE, LANES), F32)] * (2 * bands),
            flops=3 * 10**9,
            moved=8 * 2**20,
        )
        half_of_near = ((near_all // 2 + 1, ROWS, LANES), BF16, False)
        keep, send = call(
            functools.partial(backward_kernel, bands),
            "backward",
            (*order, residual, inner_all, left_t, right),
            2,
            [half_of_near] * 2,
            [((chunks, WIDE, WIDE), BF16), ((bands, near_all + 8, LANES), F32)],
            flops=3 * 10**9,
            moved=8 * 2**20,
        )
        received = swapped(send)
        back = call(
            functools.partial(home_slots_kernel, bands),
            "home_slots",
            (residual, left_t, right),
            0,
            [((bands, num_slots + 1, ROWS, LANES), BF16, False)],
            flops=2 * 10**9,
            moved=4 * 2**20,
        )[0]
        back_received = swapped(back)
        received, back_received = lax.optimization_barrier((received, back_received))
        grads = call(reduce_kernel, "reduce", (keep, received), 0, [stamp] * 2, moved=2 * 2**20)
        grads = [stepped(grads[0], "ra", -1), stepped(grads[1], "dec", -1)]
        bands_here = bands if last else 2 * bands
        part = (sources, HALF, LANES) if last else all_stamps
        home_grad, grad_a = call(
            functools.partial(home_gather_kernel, bands, last),
            "home_gather",
            (lists, amps_q, morph, back, back_received),
            2,
            [(part, F32, False), ((bands_here, sources), F32, False)],
            [((2 * bands, sources, LANES), F32)],
            moved=4 * 2**20,
        )
        home_grad, *grads = lax.optimization_barrier((home_grad, *grads))
        grads += [swapped(x) for x in grads]
        outs = [((sources, HALF * LANES) if last else all_stamps, F32, False), ((bands_here, sources), F32, False)]
        if not last:
            outs += [(all_stamps, BF16, False), ((bands_here, sources), F32, False)] + [stamp] * 2
        state, amps, *more = call(
            functools.partial(update_kernel, sweep == 0, last),
            "update",
            (places, eta_m, lists, eta_a, hots, amps, grad_a, state, home_grad, *grads),
            2,
            outs,
            [(part, F32)],
            moved=3 * 2**20,
        )
        if not last:
            morph, amps_q, *messages = more
    return state[None, None], amps[None, None]


def solution(mesh):
    in_specs = (
        P("ra", "dec", None, None),
        P("ra", "dec", "band", None),
        P("ra", "dec", None, None),
        P("ra", "dec", None),
        P("ra", "dec", None),
        P("band", "ra", None),
        P("ra", "dec", "band", None, None),
    )
    out_specs = (P("ra", "dec", None, "band"), P("ra", "dec", "band", None))
    return jax.shard_map(shards, mesh=mesh, in_specs=in_specs, out_specs=out_specs, check_vma=False)
```

```python
import functools

import jax
import jax.numpy as jnp
from jax import lax
from jax.experimental import pallas as pl
from jax.experimental.pallas import tpu as pltpu
from jax.sharding import PartitionSpec as P

SIDE = 64
KERN = 32
ITERS = 2
CAP = 32
LANES = 128
ROWS = SIDE * SIDE // LANES
HALF = ROWS // 2
WIDE = 4 * SIDE
ORDER, KERNEL_OF, SLOT_OF, COUNT = range(4)
NEAR = 4
GROUP = 4
STRIDE = 4
F32 = jnp.float32
BF16 = jnp.bfloat16


def dot(a, b):
    return lax.dot_general(a, b, (((1,), (0,)), ((), ())), preferred_element_type=F32)


def dot_nt(a, b):
    return lax.dot_general(a, b, (((1,), (1,)), ((), ())), preferred_element_type=F32)


def iota(shape, dim):
    return lax.broadcasted_iota(jnp.int32, shape, dim)


def low_lanes(rows, dtype=F32):
    return (iota((rows, LANES), 1) < SIDE).astype(F32).astype(dtype)


def lane_sums(rows):
    coarse = rows.astype(BF16)
    fine = (rows - coarse.astype(F32)).astype(BF16)
    ones = jnp.ones((8, rows.shape[1]), BF16)
    return dot_nt(ones, coarse) + dot_nt(ones, fine)


def half_masks(rows):
    low = iota((rows, LANES), 1) < SIDE
    return low, jnp.logical_not(low)


def turned(value):
    return pltpu.roll(value, SIDE, 1)


def twofold(packed):
    low, flip = half_masks(ROWS)[0], turned(packed)
    return jnp.concatenate([jnp.where(low, packed, flip), jnp.where(low, flip, packed)], axis=0)


def half_rows():
    return pl.multiple_of(lax.axis_index("band") * HALF, HALF)


def rows_of(ref):
    return jnp.concatenate([ref[i] for i in range(ref.shape[0])], axis=0)


def by_core(mine, theirs):
    first = lax.axis_index("band") == 0
    return jnp.where(first, mine, theirs), jnp.where(first, theirs, mine)


def lists_kernel(num_slots, slots_ref, hots, places):
    slots = rows_of(slots_ref)
    sources = slots.shape[1]
    valid = (slots < num_slots).astype(F32)
    upper = (iota((sources, sources), 0) <= iota((sources, sources), 1)).astype(F32)
    rank = dot(valid.astype(BF16), upper.astype(BF16))
    place = iota((LANES, sources), 0).astype(F32)
    names = iota((8, sources), 1).astype(F32).astype(BF16)
    for near in range(NEAR):
        row = slice(near + 1, near + 2)
        hot = ((place == rank[row] - 1.0).astype(F32) * valid[row]).astype(BF16)
        hots[near] = hot
        places[near : near + 1, :] = dot_nt(names, hot)[:1].astype(jnp.int32)
        count = jnp.broadcast_to(rank[row, sources - 1 :], (1, LANES))
        places[NEAR + near : NEAR + near + 1, :] = count.astype(jnp.int32)


def write_messages(messages, slots, amps, hots, places, stamps):
    first = lax.axis_index("band") == 0
    row = iota((ROWS, slots.shape[1]), 0)
    for turn in range(2):
        near = 2 * turn + lax.axis_index("band")

        def pick(n, carry, near=near, turn=turn):
            messages[turn][n] = stamps[places[near, n]]
            return carry

        lax.fori_loop(0, CAP, pick, 0, unroll=8)
        slot = jnp.where(first, slots[2 * turn + 1 : 2 * turn + 2], slots[2 * turn + 2 : 2 * turn + 3]).astype(F32)
        meta = jnp.where(row == 0, slot + 1.0, 0.0)
        meta = jnp.where(row == 1, slots[0:1].astype(F32), meta)
        for band in range(amps.shape[0]):
            meta = jnp.where(row == 2 + band, amps[band : band + 1], meta)
        hot = jnp.where(first, hots[2 * turn].astype(F32), hots[2 * turn + 1].astype(F32)).astype(BF16)
        messages[turn][CAP] = dot_nt(meta.astype(BF16), hot).astype(BF16)


def pack_kernel(places, slots_ref, amps_mine, amps_theirs, hots, morph, *out):
    messages, amps_out, amps_q = out[:2], out[2], out[3]
    amps = jnp.concatenate(by_core(rows_of(amps_mine), rows_of(amps_theirs)), axis=0)
    write_messages(messages, rows_of(slots_ref), amps, hots, places, morph)
    amps_out[...] = amps
    amps_q[...] = amps.astype(BF16).astype(F32)


def order_kernel(num_slots, *refs):
    plan, amps = refs[NEAR:]
    none = NEAR * CAP
    bands = amps.shape[0]
    meta = jnp.zeros((ROWS, LANES), F32)
    for turn in range(2):
        pair = by_core(refs[turn][CAP].astype(F32), refs[2 + turn][CAP].astype(F32))
        for core in range(2):
            meta = meta + pltpu.roll(pair[core], (2 * turn + core) * CAP, 1)
    slot, kernel = meta[0:1], meta[1:2]
    amps[...] = by_core(meta[2 : 2 + bands], meta[2 + bands : 2 + 2 * bands])[0]
    plan[SLOT_OF : SLOT_OF + 1, :LANES] = jnp.maximum(slot - 1.0, 0.0).astype(jnp.int32)
    live = (slot > 0.0).astype(F32)
    hot = (iota((num_slots, none), 0).astype(F32) == kernel).astype(F32) * live
    upto = (iota((none, none), 0) <= iota((none, none), 1)).astype(F32).astype(BF16)
    rank = dot(hot.astype(BF16), upto)
    size = jnp.max(rank, axis=1, keepdims=True)
    filled = ((size.astype(jnp.int32) + (GROUP - 1)) // GROUP).astype(F32)
    before = (iota((num_slots, num_slots), 1) < iota((num_slots, num_slots), 0)).astype(F32).astype(BF16)
    start = dot(before, jnp.broadcast_to(filled, (num_slots, none)).astype(BF16))
    place = jnp.sum(hot * (GROUP * start + rank), axis=0, keepdims=True) - 1.0
    eight = iota((8, none), 0)
    names = jnp.where(eight == 0, iota((8, none), 1).astype(F32) - none, 0.0).astype(BF16)
    for part in range(plan.shape[1] // LANES):
        at = (iota((LANES, none), 0) + part * LANES).astype(F32)
        hit = (at == place).astype(F32) * live
        found = dot_nt(names, hit.astype(BF16))[:1] + none
        plan[ORDER : ORDER + 1, part * LANES : (part + 1) * LANES] = found.astype(jnp.int32)
    chunk = iota((num_slots, LANES), 1).astype(F32)
    row = iota((num_slots, LANES), 0).astype(F32)
    inside = (chunk >= start[:, :LANES]) & (chunk < start[:, :LANES] + filled)
    kernels = jnp.sum(jnp.where(inside, row, 0.0), axis=0, keepdims=True)
    plan[KERNEL_OF : KERNEL_OF + 1, :LANES] = kernels.astype(jnp.int32)
    total = jnp.sum(filled, axis=0, keepdims=True)
    plan[COUNT : COUNT + 1, :LANES] = jnp.broadcast_to(total, (1, LANES)).astype(jnp.int32)


def quarter_start(quarter, held):
    parity, line = lax.axis_index("ra") % 2, lax.axis_index("dec") % 2
    shard = parity if quarter % 2 == 0 else 1 - parity
    half = line if quarter < 2 else 1 - line
    return (2 * shard + half) * held


def tables_kernel(bands, earlier, *refs):
    shards, (first_t, left, left_t, right, packed) = refs[: len(refs) - 5 - 4 * earlier], refs[-5:]
    held = shards[0].shape[1]
    for turn, ref in enumerate(shards):
        for band in range(bands):
            for r in range(ROWS):
                rows = pl.ds(turn * held * ROWS + r, held, stride=ROWS)
                packed[band, rows, :] = ref[band, :, r * LANES : (r + 1) * LANES].astype(F32)
    starts = [quarter_start(2 + turn, held) if earlier else turn * held for turn in range(len(shards))]
    if earlier:
        old_first, old_left, old_left_t, old_right = refs[len(shards) : len(shards) + 4]
        for turn in range(2):
            old, new = pl.ds(turn * held, held), pl.ds(quarter_start(turn, held), held)
            first_t[new] = old_first[old]
            right[new] = old_right[old]
            for band in range(bands):
                left[band, new] = old_left[band, old]
                left_t[band, new] = old_left_t[band, old]
    eye = (iota((SIDE, SIDE), 0) == iota((SIDE, SIDE), 1)).astype(F32).astype(BF16)
    row, col = iota((SIDE, SIDE), 0), iota((SIDE, SIDE), 1)
    even = (col == 2 * (row % ROWS) + row // ROWS).astype(F32).astype(BF16)
    even_t = (row == 2 * (col % ROWS) + col // ROWS).astype(F32).astype(BF16)
    rest = [jnp.zeros((SIDE * (4 - bands), SIDE), BF16)] if bands < 4 else []
    for turn, start in enumerate(starts):

        def step(place, carry, turn=turn, start=start):
            k = start + place
            at = pl.multiple_of((turn * held + place) * ROWS, ROWS)
            parts = [twofold(packed[band, pl.ds(at, ROWS), :]).astype(BF16) for band in range(bands)]
            lefts = dot_nt(jnp.concatenate([part[:, :SIDE] for part in parts], axis=0), even).astype(BF16)
            natural = []
            for band, part in enumerate(parts):
                rows = slice(band * SIDE, (band + 1) * SIDE)
                left[band, k] = lefts[rows]
                left_t[band, k] = dot_nt(eye, lefts[rows]).astype(BF16)
                both = dot(even_t, part).astype(BF16)
                right[k, rows, :] = both
                natural.append(both[:, :SIDE])
            if rest:
                right[k, bands * SIDE :, :] = jnp.zeros((SIDE * (4 - bands), LANES), BF16)
            first_t[k] = dot_nt(eye, jnp.concatenate(natural + rest, axis=0)).astype(BF16)
            return carry

        lax.fori_loop(0, held, step, 0, unroll=min(held, 4))


def make_tables(shards, bands, earlier=()):
    count = sum(x.shape[1] for x in shards)
    total = count + sum(x.shape[0] for x in earlier[:1])
    square = ((bands, total, SIDE, SIDE), BF16)
    return call(
        functools.partial(tables_kernel, bands, bool(earlier)),
        "tables",
        (*shards, *earlier),
        0,
        [((total, SIDE, WIDE), BF16), square, square, ((total, WIDE, LANES), BF16)],
        [((bands, count * ROWS, LANES), F32)],
        flops=2 * 10**9,
        moved=5 * 2**20,
    )


def home_sums_kernel(bands, lists, amps, morph, sums):
    first = lax.axis_index("band") * bands
    sums[...] = jnp.zeros_like(sums)

    def add(s, carry):
        q = lists[0, 0, s]
        stamp = morph[s].astype(F32)
        for band in range(bands):
            sums[band, q] += amps[first + band, s] * stamp
        return carry

    lax.fori_loop(0, lists.shape[2], add, 0, unroll=4)


def home_forward_kernel(bands, sums, first_t, left, total, inner_all):
    num_slots = total.shape[1]
    masks = half_masks(SIDE)

    def inner_products(q, carry):
        images = []
        for band in range(bands):
            both = sums[band, q]
            images += [both[:, :SIDE], turned(both)[:, :SIDE]]
        inners = dot(jnp.concatenate(images, axis=0).astype(BF16), first_t[q])
        for band in range(bands):
            lanes = slice(band // 2 * LANES, (band // 2 + 1) * LANES)
            inner_all[band, q] = inners[band * SIDE : (band + 1) * SIDE, lanes].astype(BF16)
        return carry

    def slot(q, carry):
        for band in range(bands):
            total[band, q] = jnp.where(masks[band % 2], dot(left[band, q], inner_all[band, q]), 0.0)
        return carry

    lax.fori_loop(0, num_slots, inner_products, 0, unroll=4)
    lax.fori_loop(0, num_slots, slot, 0, unroll=4)


def chunk_reader(bands, plan, amps):
    none = NEAR * CAP

    def read(c):
        members = [plan[ORDER, c * GROUP + u] for u in range(GROUP)]
        held = [jnp.minimum(v, none - 1) for v in members]
        values = [[jnp.where(v < none, amps[band, h], 0.0) for v, h in zip(members, held)] for band in range(bands)]
        return plan[KERNEL_OF, c], members, [plan[SLOT_OF, h] for h in held], values

    return read, (plan[COUNT, 0] + STRIDE - 1) // STRIDE


def forward_kernel(bands, plan, amps, *refs):
    home, observed, first_t, left = refs[NEAR : NEAR + 4]
    residual, inner_all, stamps, *totals = refs[NEAR + 4 :]
    totals = [totals[2 * band : 2 * band + 2] for band in range(bands)]
    num_slots = home.shape[1]
    none = NEAR * CAP
    core = lax.axis_index("band")
    for source, near in enumerate((core, 2 + core, 1 - core, 3 - core)):
        group = pl.ds(near * CAP, CAP)
        even = refs[source][pl.ds(0, CAP)].astype(F32)
        odd = turned(even.reshape(CAP * ROWS, LANES)).reshape(CAP, ROWS, LANES)
        stamps[group, pl.ds(0, ROWS), :] = even.astype(BF16)
        stamps[group, pl.ds(ROWS, ROWS), :] = odd.astype(BF16)
    stamps[none] = jnp.zeros((SIDE, LANES), BF16)
    for band in range(bands):
        totals[band][band % 2][...] = home[band]
        totals[band][1 - band % 2][...] = jnp.zeros_like(home[band])
    masks, row_masks = half_masks(SIDE), half_masks(1)
    read, rounds = chunk_reader(bands, plan, amps)

    def inner_products(turn, carry):
        for c in [STRIDE * turn + i for i in range(STRIDE)]:
            k, members, _, _ = read(c)
            stack = jnp.concatenate([stamps[v] for v in members], axis=0)
            inners = dot(stack[:, :SIDE], first_t[k])
            for band in range(bands):
                lanes = slice(band // 2 * LANES, (band // 2 + 1) * LANES)
                pairs = []
                for u in range(0, GROUP, 2):
                    x = inners[u * SIDE : (u + 1) * SIDE, lanes]
                    y = inners[(u + 1) * SIDE : (u + 2) * SIDE, lanes]
                    x, y = (x, turned(y)) if band % 2 == 0 else (turned(x), y)
                    pairs.append(jnp.where(masks[0], x, y))
                inner_all[c, band] = jnp.concatenate(pairs, axis=1).astype(BF16)
        return carry

    def images(turn, carry):
        for c in [STRIDE * turn + i for i in range(STRIDE)]:
            k, _, slots, values = read(c)
            for band in range(bands):
                image = dot(left[band, k], inner_all[c, band])
                for u in range(0, GROUP, 2):
                    lanes = slice(u // 2 * LANES, (u // 2 + 1) * LANES)
                    scale = jnp.where(row_masks[0], values[band][u], values[band][u + 1])
                    pair = image[:, lanes] * scale
                    for part in (0, 1):
                        totals[band][part][slots[u + part]] += pair
        return carry

    lax.fori_loop(0, rounds, inner_products, 0)
    lax.fori_loop(0, rounds, images, 0)

    def slot(q, carry):
        for band in range(bands):
            model = jnp.where(masks[0], totals[band][0][q], totals[band][1][q])
            seen = twofold(observed[band, q].astype(F32))
            residual[band, q] = (model + turned(model) - seen).astype(BF16)
        return carry

    lax.fori_loop(0, num_slots, slot, 0, unroll=8)


def backward_kernel(bands, plan, amps, *refs):
    residual, inner_all, left_t, right, keep, send, stacks, sums = refs
    none = NEAR * CAP
    sums[...] = jnp.zeros_like(sums)
    keep[...] = jnp.zeros_like(keep)
    send[...] = jnp.zeros_like(send)
    masks, row_masks, packed_low = half_masks(SIDE), half_masks(1), half_masks(ROWS)[0]
    read, rounds = chunk_reader(bands, plan, amps)
    spare = none // 2
    core = lax.axis_index("band")

    def outer_products(turn, carry):
        for c in [STRIDE * turn + i for i in range(STRIDE)]:
            k, members, slots, values = read(c)
            outers = []
            for band in range(bands):
                pairs = [
                    jnp.where(masks[0], residual[band, slots[u]], residual[band, slots[u + 1]])
                    for u in range(0, GROUP, 2)
                ]
                outer = dot(left_t[band, k], jnp.concatenate(pairs, axis=1))
                along = jnp.sum(inner_all[c, band].astype(F32) * outer, axis=0, keepdims=True)
                scaled = []
                for u in range(0, GROUP, 2):
                    lanes = slice(u // 2 * LANES, (u // 2 + 1) * LANES)
                    for part in (0, 1):
                        row = jnp.where(row_masks[part], along[:, lanes], 0.0)
                        sums[band, pl.ds(members[u + part], 1), :] = row
                    scale = jnp.where(row_masks[0], values[band][u], values[band][u + 1])
                    scaled.append(outer[:, lanes] * scale)
                outers.append(scaled)
            outers += [[jnp.zeros((SIDE, LANES), F32)] * (GROUP // 2)] * (4 - bands)
            for pair in range(GROUP // 2):
                b0, b1, b2, b3 = [outers[band][pair] for band in range(4)]
                if bands > 3:
                    last = [jnp.where(masks[0], b2, turned(b3)), jnp.where(masks[0], turned(b2), b3)]
                else:
                    last = [b2, turned(b2)]
                first = [jnp.where(masks[0], b0, turned(b1)), jnp.where(masks[0], turned(b0), b1)]
                for part in (0, 1):
                    rows = slice((2 * pair + part) * SIDE, (2 * pair + part + 1) * SIDE)
                    stacks[c, rows, :] = jnp.concatenate([first[part], last[part]], axis=1).astype(BF16)
        return carry

    def gradients(turn, carry):
        for c in [STRIDE * turn + i for i in range(STRIDE)]:
            k, members, _, _ = read(c)
            grads = dot(stacks[c], right[k])
            for u, v in enumerate(members):
                top = grads[u * SIDE : u * SIDE + ROWS]
                low = grads[u * SIDE + ROWS : (u + 1) * SIDE]
                stamp = jnp.where(packed_low, top, low).astype(BF16)
                side, place = v // CAP % 2, v // (2 * CAP) * CAP + v % CAP
                keep[jnp.where(side == core, place, spare)] = stamp
                send[jnp.where(side == 1 - core, place, spare)] = stamp
        return carry

    lax.fori_loop(0, rounds, outer_products, 0)
    lax.fori_loop(0, rounds, gradients, 0)
    meta = amp_rows([lane_sums(sums[band, :none, :]) for band in range(bands)])
    keep[spare] = meta
    send[spare] = meta


def home_slots_kernel(bands, residual, left_t, right, back):
    num_slots = residual.shape[1]
    back[:, num_slots] = jnp.zeros((bands, ROWS, LANES), BF16)
    packed_low = half_masks(ROWS)[0]

    def slot(q, carry):
        for band in range(bands):
            outer = dot(left_t[band, q], residual[band, q]).astype(BF16)
            grad = dot(outer[:, :SIDE], right[q, band * SIDE : (band + 1) * SIDE, :])
            back[band, q] = jnp.where(packed_low, grad[:ROWS], grad[ROWS:]).astype(BF16)
        return carry

    lax.fori_loop(0, num_slots, slot, 0, unroll=8)


def home_gather_kernel(bands, last, lists, amps, morph, back, received, keep, grad_a, sums):
    core = lax.axis_index("band")
    mine = pl.ds(half_rows(), HALF) if last else pl.ds(0, ROWS)

    def gather(s, carry):
        q = lists[0, 0, s]
        stamp = morph[s].astype(F32)
        grad = jnp.zeros((HALF if last else ROWS, LANES), F32)
        for ref, side in ((back, core), (received, 1 - core)):
            for band in range(bands):
                amp = amps[side * bands + band, s]
                if last:
                    grad = grad + amp * ref[band, q, mine, :].astype(F32)
                    if ref is received:
                        continue
                seen = ref[band, q].astype(F32)
                if not last:
                    grad = grad + amp * seen
                along = jnp.sum(seen * stamp, axis=0, keepdims=True)
                sums[side * bands + band, pl.ds(s, 1), :] = along
        keep[s] = grad
        return carry

    lax.fori_loop(0, lists.shape[2], gather, 0, unroll=4)
    for band in range(grad_a.shape[0]):
        rows = sums[core * bands + band] if last else sums[band]
        grad_a[band : band + 1, :] = lane_sums(rows)[:1]


def amp_rows(sums):
    eight = iota((8, LANES), 0)
    total = jnp.zeros((8, LANES), F32)
    for band, row in enumerate(sums):
        total = jnp.where(eight == band, row, total)
    coarse = total.astype(BF16).astype(F32)
    return jnp.concatenate([coarse, total - coarse, jnp.zeros((HALF, LANES), F32)], axis=0).astype(BF16)


def reduce_kernel(keep, received, *messages):
    for turn in range(2):
        part = pl.ds(turn * CAP, CAP)
        total = keep[part].astype(F32) + received[part].astype(F32)
        messages[turn][pl.ds(0, CAP)] = total.astype(BF16)
        pair = by_core(keep[2 * CAP].astype(F32), received[2 * CAP].astype(F32))
        meta = jnp.concatenate([pair[0][:HALF], pair[1][:HALF]], axis=0)
        messages[turn][CAP] = meta.astype(BF16)


def update_kernel(first, last, places, eta_m, slots_ref, eta_a, hots, amps_ref, grad_a, morph, home, *refs):
    grads, out = refs[:NEAR], refs[NEAR:]
    state, amps_out, work = out[0], out[1], out[-1]
    sources = slots_ref.shape[2]
    core = lax.axis_index("band")
    mine = pl.ds(half_rows(), HALF) if last else pl.ds(0, ROWS)
    nears = (core, 2 + core, 1 - core, 3 - core)
    lane = iota((ROWS, LANES), 1) // CAP
    meta = jnp.zeros((ROWS, LANES), F32)
    for ref, near in zip(grads, nears):
        meta = jnp.where(lane == near, ref[CAP].astype(F32), meta)
    all_hots = jnp.concatenate([hots[near, :CAP] for near in range(NEAR)], axis=0)
    from_near = dot(meta.astype(BF16), all_hots)
    bands = amps_ref.shape[0] // 2
    sides = [from_near[r : r + bands] + from_near[r + 8 : r + 8 + bands] for r in (0, HALF)]
    if last:
        amps = by_core(amps_ref[:bands], amps_ref[bands:])[0]
        total = grad_a[...] + by_core(sides[0], sides[1])[0]
    else:
        amps = amps_ref[...]
        total = grad_a[...] + jnp.concatenate(sides, axis=0)
    amps = jnp.maximum(amps - eta_a[...] * total, 0.0)
    if last:
        for band in range(bands):
            amps_out[band] = amps[band : band + 1]
    else:
        amps_out[...] = amps
    work[...] = home[...]
    for ref, near in zip(grads, nears):

        def add(n, carry, ref=ref, near=near):
            work[places[near, n]] += ref[n, mine, :].astype(F32)
            return carry

        lax.fori_loop(0, CAP, add, 0, unroll=8)

    def step(s, carry):
        new = jnp.maximum(morph[s, mine, :].astype(F32) - eta_m[0, s] * work[s], 0.0)
        if last:
            work[s] = new
        else:
            state[s] = new
            out[2][s] = new.astype(BF16)
        return carry

    lax.fori_loop(0, sources, step, 0, unroll=8)
    if last:
        for r in range(HALF):
            state[:, r * LANES : (r + 1) * LANES] = work[:, r, :]
        return
    stamps, amps_q, messages = out[2], out[3], out[4:6]
    amps_q[...] = amps.astype(BF16).astype(F32)
    write_messages(messages, rows_of(slots_ref), amps, hots, places, stamps)


def call(body, name, operands, scalars, outs, scratch=(), flops=0, moved=0):
    vmem, smem = pl.BlockSpec(memory_space=pltpu.VMEM), pl.BlockSpec(memory_space=pltpu.SMEM)
    return pl.pallas_call(
        body,
        out_shape=[jax.ShapeDtypeStruct(shape, dtype) for shape, dtype in outs],
        in_specs=[smem if i < scalars else vmem for i in range(len(operands))],
        out_specs=[vmem] * len(outs),
        scratch_shapes=[pltpu.VMEM(shape, dtype) for shape, dtype in scratch],
        compiler_params=pltpu.CompilerParams(vmem_limit_bytes=40 * 2**20),
        cost_estimate=pl.CostEstimate(flops=flops, bytes_accessed=moved, transcendentals=0),
        name=name,
    )(*operands)


def stepped(value, axis, step):
    shape = [lax.axis_size(name) for name in ("ra", "dec", "band")]

    def device(ra, dec, band):
        return (ra * shape[1] + dec) * shape[2] + band

    pairs = []
    for ra in range(shape[0]):
        for dec in range(shape[1]):
            for band, by in ((0, step), (1, -step)):
                if axis == "ra":
                    pairs.append((device(ra, dec, band), device((ra + by) % shape[0], dec, band)))
                elif 0 <= dec + by < shape[1]:
                    pairs.append((device(ra, dec, band), device(ra, dec + by, band)))
    return lax.ppermute(value, ("ra", "dec", "band"), pairs)


def swapped(value):
    return lax.ppermute(value, "band", [(0, 1), (1, 0)])


def all_tables(psf, num_slots, messages, sums):
    bands, held = psf.shape[:2]
    lines = lax.axis_size("dec")
    if lax.axis_size("ra") == 4 and 2 * held == num_slots and held % 2 == 0 and lines % 2 == 0:
        across = [(i, i + 1 - 2 * (i % 2)) for i in range(lines)]
        along = [(0, 1), (1, 0), (2, 3), (3, 2)]
        mine = jnp.where(lax.axis_index("dec") % 2 == 0, psf[:, : held // 2], psf[:, held // 2 :])
        far = lax.ppermute(mine, "ra", [(0, 2), (1, 3)])
        here = jnp.where(lax.axis_index("ra") < 2, mine, far)
        here, messages[0] = lax.optimization_barrier((here, messages[0]))
        near = lax.ppermute(here, "ra", along)
        near, sums = lax.optimization_barrier((near, sums))
        halves = make_tables((here, near), bands)
        others = (lax.ppermute(here, "dec", across), lax.ppermute(near, "dec", across))
        messages[1], *halves = lax.optimization_barrier((messages[1], *halves))
        return make_tables(others, bands, halves), messages, sums
    return make_tables((lax.all_gather(psf, "ra", axis=1, tiled=True)[:, :num_slots],), bands), messages, sums


def shards(morphology, sed_amps, slot_lists, morph_step, sed_step, psf_kernels, observed):
    bands, num_slots, sources = sed_amps.shape[2], observed.shape[3], morphology.shape[2]
    lists, amps = slot_lists[0, 0][:, None, :], sed_amps[0, 0][:, None, :]
    eta_m, eta_a = morph_step[0], sed_step[0]
    full = morphology[0, 0].reshape(sources, ROWS, LANES)
    seen = observed[0, 0].reshape(bands, num_slots, ROWS, LANES)
    stamp = ((CAP + 1, ROWS, LANES), BF16)
    all_stamps = (sources, ROWS, LANES)
    near_all = NEAR * CAP
    chunks = -(-(near_all // GROUP + num_slots) // STRIDE) * STRIDE
    amps_theirs = swapped(amps)
    hots, places = call(
        functools.partial(lists_kernel, num_slots),
        "lists",
        (lists,),
        0,
        [
            ((NEAR, LANES, sources), BF16),
            ((2 * NEAR, LANES), jnp.int32),
        ],
        moved=2**20,
    )
    *messages, amps, amps_q = call(
        pack_kernel,
        "pack",
        (places, lists, amps, amps_theirs, hots, full),
        1,
        [stamp] * 2 + [((2 * bands, sources), F32)] * 2,
        moved=2**20,
    )
    def home_sums(amps_q, morph):
        return call(
            functools.partial(home_sums_kernel, bands),
            "home_sums",
            (lists, amps_q, morph),
            2,
            [((bands, num_slots + 1, ROWS, LANES), F32)],
            moved=4 * 2**20,
        )[0]

    sums = home_sums(amps_q, full)
    tables, messages, sums = all_tables(psf_kernels, num_slots, messages, sums)
    first_t, left, left_t, right = tables
    morph = state = full
    for sweep in range(ITERS):
        last = sweep == ITERS - 1
        own = [stepped(messages[0], "ra", 1), stepped(messages[1], "dec", 1)]
        if sweep == 0:
            left, *own = lax.optimization_barrier((left, *own))
        else:
            sums = home_sums(amps_q, morph)
        home = call(
            functools.partial(home_forward_kernel, bands),
            "home_forward",
            (sums, first_t, left),
            0,
            [((bands, num_slots, SIDE, LANES), F32)],
            [((bands, num_slots, SIDE, LANES), BF16)],
            flops=2 * 10**9,
            moved=4 * 2**20,
        )[0]
        if sweep > 0:
            own = [lax.optimization_barrier((home, x))[1] for x in own]
        other = [swapped(x) for x in own]
        order = call(
            functools.partial(order_kernel, num_slots),
            "order",
            (*own, *other),
            0,
            [
                ((8, -(-chunks * GROUP // LANES) * LANES), jnp.int32),
                ((bands, LANES), F32),
            ],
            moved=2**20,
        )
        residual, inner_all = call(
            functools.partial(forward_kernel, bands),
            "forward",
            (*order, *own, *other, home, seen, first_t, left),
            2,
            [
                ((bands, num_slots, SIDE, LANES), BF16),
                ((chunks, bands, SIDE, WIDE), BF16),
            ],
            [((near_all + 1, SIDE, LANES), BF16)] + [((num_slots, SIDE, LANES), F32)] * (2 * bands),
            flops=3 * 10**9,
            moved=8 * 2**20,
        )
        half_of_near = ((near_all // 2 + 1, ROWS, LANES), BF16)
        keep, send = call(
            functools.partial(backward_kernel, bands),
            "backward",
            (*order, residual, inner_all, left_t, right),
            2,
            [half_of_near] * 2,
            [((chunks, WIDE, WIDE), BF16), ((bands, near_all + 8, LANES), F32)],
            flops=3 * 10**9,
            moved=8 * 2**20,
        )
        received = swapped(send)
        back = call(
            functools.partial(home_slots_kernel, bands),
            "home_slots",
            (residual, left_t, right),
            0,
            [((bands, num_slots + 1, ROWS, LANES), BF16)],
            flops=2 * 10**9,
            moved=4 * 2**20,
        )[0]
        received, back = lax.optimization_barrier((received, back))
        grads = call(reduce_kernel, "reduce", (keep, received), 0, [stamp] * 2, moved=2 * 2**20)
        grads = [stepped(grads[0], "ra", -1), stepped(grads[1], "dec", -1)]
        back_received = swapped(back)
        bands_here = bands if last else 2 * bands
        part = (sources, HALF, LANES) if last else all_stamps
        home_grad, grad_a = call(
            functools.partial(home_gather_kernel, bands, last),
            "home_gather",
            (lists, amps_q, morph, back, back_received),
            2,
            [(part, F32), ((bands_here, sources), F32)],
            [((2 * bands, sources, LANES), F32)],
            moved=4 * 2**20,
        )
        grads = [lax.optimization_barrier((home_grad, x))[1] for x in grads]
        grads += [swapped(x) for x in grads]
        outs = [((sources, HALF * LANES) if last else all_stamps, F32)]
        outs += [((bands, 1, sources) if last else (2 * bands, sources), F32)]
        if not last:
            outs += [(all_stamps, BF16), ((bands_here, sources), F32)] + [stamp] * 2
        state, amps, *more = call(
            functools.partial(update_kernel, sweep == 0, last),
            "update",
            (places, eta_m, lists, eta_a, hots, amps, grad_a, state, home_grad, *grads),
            2,
            outs,
            [(part, F32)],
            moved=3 * 2**20,
        )
        if not last:
            morph, amps_q, *messages = more
    return state[None, None], amps.reshape(1, 1, bands, sources)


def solution(mesh):
    in_specs = (
        P("ra", "dec", None, None),
        P("ra", "dec", "band", None),
        P("ra", "dec", None, None),
        P("ra", "dec", None),
        P("ra", "dec", None),
        P("band", "ra", None),
        P("ra", "dec", "band", None, None),
    )
    out_specs = (P("ra", "dec", None, "band"), P("ra", "dec", "band", None))
    return jax.shard_map(shards, mesh=mesh, in_specs=in_specs, out_specs=out_specs, check_vma=False)
```

```python
import functools

import jax
import jax.numpy as jnp
from jax import lax
from jax.experimental import pallas as pl
from jax.experimental.pallas import tpu as pltpu
from jax.sharding import PartitionSpec as P

SIDE = 64
KERN = 32
ITERS = 2
CAP = 32
LANES = 128
ROWS = SIDE * SIDE // LANES
HALF = ROWS // 2
WIDE = 4 * SIDE
ORDER, KERNEL_OF, SLOT_OF, COUNT = range(4)
NEAR = 4
GROUP = 4
STRIDE = 4
F32 = jnp.float32
BF16 = jnp.bfloat16


def dot(a, b):
    return lax.dot_general(a, b, (((1,), (0,)), ((), ())), preferred_element_type=F32)


def dot_nt(a, b):
    return lax.dot_general(a, b, (((1,), (1,)), ((), ())), preferred_element_type=F32)


def iota(shape, dim):
    return lax.broadcasted_iota(jnp.int32, shape, dim)


def low_lanes(rows, dtype=F32):
    return (iota((rows, LANES), 1) < SIDE).astype(F32).astype(dtype)


def lane_sums(rows):
    coarse = rows.astype(BF16)
    fine = (rows - coarse.astype(F32)).astype(BF16)
    ones = jnp.ones((8, rows.shape[1]), BF16)
    return dot_nt(ones, coarse) + dot_nt(ones, fine)


def half_masks(rows):
    low = iota((rows, LANES), 1) < SIDE
    return low, jnp.logical_not(low)


def turned(value):
    return pltpu.roll(value, SIDE, 1)


def twofold(packed):
    low, flip = half_masks(ROWS)[0], turned(packed)
    return jnp.concatenate([jnp.where(low, packed, flip), jnp.where(low, flip, packed)], axis=0)


def rounded(stamp):
    if stamp.dtype == F32:
        stamp = jnp.maximum(stamp, 0.0).astype(BF16)
    return stamp.astype(F32)


def half_rows():
    return pl.multiple_of(lax.axis_index("band") * HALF, HALF)


def rows_of(ref):
    return jnp.concatenate([ref[i] for i in range(ref.shape[0])], axis=0)


def by_core(mine, theirs):
    first = lax.axis_index("band") == 0
    return jnp.where(first, mine, theirs), jnp.where(first, theirs, mine)


def lists_kernel(num_slots, slots_ref, hots, places):
    slots = rows_of(slots_ref)
    sources = slots.shape[1]
    valid = (slots < num_slots).astype(F32)
    upper = (iota((sources, sources), 0) <= iota((sources, sources), 1)).astype(F32)
    rank = dot(valid.astype(BF16), upper.astype(BF16))
    place = iota((LANES, sources), 0).astype(F32)
    names = iota((8, sources), 1).astype(F32).astype(BF16)
    for near in range(NEAR):
        row = slice(near + 1, near + 2)
        hot = ((place == rank[row] - 1.0).astype(F32) * valid[row]).astype(BF16)
        hots[near] = hot
        places[near : near + 1, :] = dot_nt(names, hot)[:1].astype(jnp.int32)
        count = jnp.broadcast_to(rank[row, sources - 1 :], (1, LANES))
        places[NEAR + near : NEAR + near + 1, :] = count.astype(jnp.int32)


def write_messages(messages, slots, amps, hots, places, stamp_of):
    first = lax.axis_index("band") == 0
    row = iota((ROWS, slots.shape[1]), 0)
    for turn in range(2):
        near = 2 * turn + lax.axis_index("band")

        def pick(n, carry, near=near, turn=turn):
            messages[turn][n] = stamp_of(places[near, n])
            return carry

        lax.fori_loop(0, CAP, pick, 0, unroll=8)
        slot = jnp.where(first, slots[2 * turn + 1 : 2 * turn + 2], slots[2 * turn + 2 : 2 * turn + 3]).astype(F32)
        meta = jnp.where(row == 0, slot + 1.0, 0.0)
        meta = jnp.where(row == 1, slots[0:1].astype(F32), meta)
        for band in range(amps.shape[0]):
            meta = jnp.where(row == 2 + band, amps[band : band + 1], meta)
        hot = jnp.where(first, hots[2 * turn].astype(F32), hots[2 * turn + 1].astype(F32)).astype(BF16)
        messages[turn][CAP] = dot_nt(meta.astype(BF16), hot).astype(BF16)


def pack_kernel(places, slots_ref, amps_mine, amps_theirs, hots, morph, *out):
    messages, amps_out, amps_q = out[:2], out[2], out[3]
    amps = jnp.concatenate(by_core(rows_of(amps_mine), rows_of(amps_theirs)), axis=0)
    write_messages(messages, rows_of(slots_ref), amps, hots, places, lambda s: morph[s])
    amps_out[...] = amps
    amps_q[...] = amps.astype(BF16).astype(F32)


def order_kernel(num_slots, again, *refs):
    amps, none = refs[NEAR], NEAR * CAP
    bands = amps.shape[0]
    meta = jnp.zeros((ROWS, LANES), F32)
    for turn in range(2):
        pair = by_core(refs[turn][CAP].astype(F32), refs[2 + turn][CAP].astype(F32))
        for core in range(2):
            meta = meta + pltpu.roll(pair[core], (2 * turn + core) * CAP, 1)
    amps[...] = by_core(meta[2 : 2 + bands], meta[2 + bands : 2 + 2 * bands])[0]
    if again:
        return
    plan, slot, kernel = refs[NEAR + 1], meta[0:1], meta[1:2]
    plan[SLOT_OF : SLOT_OF + 1, :LANES] = jnp.maximum(slot - 1.0, 0.0).astype(jnp.int32)
    live = (slot > 0.0).astype(F32)
    hot = (iota((num_slots, none), 0).astype(F32) == kernel).astype(F32) * live
    upto = (iota((none, none), 0) <= iota((none, none), 1)).astype(F32).astype(BF16)
    rank = dot(hot.astype(BF16), upto)
    size = jnp.max(rank, axis=1, keepdims=True)
    filled = ((size.astype(jnp.int32) + (GROUP - 1)) // GROUP).astype(F32)
    before = (iota((num_slots, num_slots), 1) < iota((num_slots, num_slots), 0)).astype(F32).astype(BF16)
    start = dot(before, jnp.broadcast_to(filled, (num_slots, none)).astype(BF16))
    place = jnp.sum(hot * (GROUP * start + rank), axis=0, keepdims=True) - 1.0
    eight = iota((8, none), 0)
    names = jnp.where(eight == 0, iota((8, none), 1).astype(F32) - none, 0.0).astype(BF16)
    for part in range(plan.shape[1] // LANES):
        at = (iota((LANES, none), 0) + part * LANES).astype(F32)
        hit = (at == place).astype(F32) * live
        found = dot_nt(names, hit.astype(BF16))[:1] + none
        plan[ORDER : ORDER + 1, part * LANES : (part + 1) * LANES] = found.astype(jnp.int32)
    chunk = iota((num_slots, LANES), 1).astype(F32)
    row = iota((num_slots, LANES), 0).astype(F32)
    inside = (chunk >= start[:, :LANES]) & (chunk < start[:, :LANES] + filled)
    kernels = jnp.sum(jnp.where(inside, row, 0.0), axis=0, keepdims=True)
    plan[KERNEL_OF : KERNEL_OF + 1, :LANES] = kernels.astype(jnp.int32)
    total = jnp.sum(filled, axis=0, keepdims=True)
    plan[COUNT : COUNT + 1, :LANES] = jnp.broadcast_to(total, (1, LANES)).astype(jnp.int32)


def quarter_start(quarter, held):
    parity, line = lax.axis_index("ra") % 2, lax.axis_index("dec") % 2
    shard = parity if quarter % 2 == 0 else 1 - parity
    half = line if quarter < 2 else 1 - line
    return (2 * shard + half) * held


def tables_kernel(bands, earlier, *refs):
    shards, (first_t, left, left_t, right, packed) = refs[: len(refs) - 5 - 4 * earlier], refs[-5:]
    held = shards[0].shape[1]
    for turn, ref in enumerate(shards):
        for band in range(bands):
            for r in range(ROWS):
                rows = pl.ds(turn * held * ROWS + r, held, stride=ROWS)
                packed[band, rows, :] = ref[band, :, r * LANES : (r + 1) * LANES].astype(F32)
    starts = [quarter_start(2 + turn, held) if earlier else turn * held for turn in range(len(shards))]
    if earlier:
        old_first, old_left, old_left_t, old_right = refs[len(shards) : len(shards) + 4]
        for turn in range(2):
            old, new = pl.ds(turn * held, held), pl.ds(quarter_start(turn, held), held)
            first_t[new] = old_first[old]
            right[new] = old_right[old]
            for band in range(bands):
                left[band, new] = old_left[band, old]
                left_t[band, new] = old_left_t[band, old]
    eye = (iota((SIDE, SIDE), 0) == iota((SIDE, SIDE), 1)).astype(F32).astype(BF16)
    row, col = iota((SIDE, SIDE), 0), iota((SIDE, SIDE), 1)
    even = (col == 2 * (row % ROWS) + row // ROWS).astype(F32).astype(BF16)
    even_t = (row == 2 * (col % ROWS) + col // ROWS).astype(F32).astype(BF16)
    rest = [jnp.zeros((SIDE * (4 - bands), SIDE), BF16)] if bands < 4 else []
    for turn, start in enumerate(starts):

        def step(place, carry, turn=turn, start=start):
            k = start + place
            at = pl.multiple_of((turn * held + place) * ROWS, ROWS)
            parts = [twofold(packed[band, pl.ds(at, ROWS), :]).astype(BF16) for band in range(bands)]
            lefts = dot_nt(jnp.concatenate([part[:, :SIDE] for part in parts], axis=0), even).astype(BF16)
            natural = []
            for band, part in enumerate(parts):
                rows = slice(band * SIDE, (band + 1) * SIDE)
                left[band, k] = lefts[rows]
                left_t[band, k] = dot_nt(eye, lefts[rows]).astype(BF16)
                both = dot(even_t, part).astype(BF16)
                right[k, rows, :] = both
                natural.append(both[:, :SIDE])
            if rest:
                right[k, bands * SIDE :, :] = jnp.zeros((SIDE * (4 - bands), LANES), BF16)
            first_t[k] = dot_nt(eye, jnp.concatenate(natural + rest, axis=0)).astype(BF16)
            return carry

        lax.fori_loop(0, held, step, 0, unroll=min(held, 4))


def make_tables(shards, bands, earlier=()):
    count = sum(x.shape[1] for x in shards)
    total = count + sum(x.shape[0] for x in earlier[:1])
    square = ((bands, total, SIDE, SIDE), BF16)
    return call(
        functools.partial(tables_kernel, bands, bool(earlier)),
        "tables",
        (*shards, *earlier),
        0,
        [((total, SIDE, WIDE), BF16), square, square, ((total, WIDE, LANES), BF16)],
        [((bands, count * ROWS, LANES), F32)],
        flops=2 * 10**9,
        moved=5 * 2**20,
    )


def home_sums_kernel(bands, lists, amps, morph, sums):
    first = lax.axis_index("band") * bands
    sums[...] = jnp.zeros_like(sums)

    def add(s, carry):
        q = lists[0, 0, s]
        stamp = rounded(morph[s])
        for band in range(bands):
            sums[band, q] += amps[first + band, s] * stamp
        return carry

    lax.fori_loop(0, lists.shape[2], add, 0, unroll=4)


def home_forward_kernel(bands, sums, observed, first_t, left, total, inner_all):
    num_slots = total.shape[1]
    masks = half_masks(SIDE)

    def inner_products(q, carry):
        images = []
        for band in range(bands):
            both = sums[band, q]
            images += [both[:, :SIDE], turned(both)[:, :SIDE]]
        inners = dot(jnp.concatenate(images, axis=0).astype(BF16), first_t[q])
        for band in range(bands):
            lanes = slice(band // 2 * LANES, (band // 2 + 1) * LANES)
            inner_all[band, q] = inners[band * SIDE : (band + 1) * SIDE, lanes].astype(BF16)
        return carry

    def slot(q, carry):
        for band in range(bands):
            image = dot(left[band, q], inner_all[band, q]) - twofold(observed[band, q].astype(F32))
            total[band, q] = jnp.where(masks[band % 2], image, 0.0)
        return carry

    lax.fori_loop(0, num_slots, inner_products, 0, unroll=4)
    lax.fori_loop(0, num_slots, slot, 0, unroll=4)


def chunk_reader(bands, plan, amps):
    none = NEAR * CAP

    def read(c):
        members = [plan[ORDER, c * GROUP + u] for u in range(GROUP)]
        held = [jnp.minimum(v, none - 1) for v in members]
        values = [[jnp.where(v < none, amps[band, h], 0.0) for v, h in zip(members, held)] for band in range(bands)]
        return plan[KERNEL_OF, c], members, [plan[SLOT_OF, h] for h in held], values

    return read, (plan[COUNT, 0] + STRIDE - 1) // STRIDE


def forward_kernel(bands, plan, amps, *refs):
    home, first_t, left = refs[NEAR : NEAR + 3]
    residual, inner_all, stamps, *totals = refs[NEAR + 3 :]
    totals = [totals[2 * band : 2 * band + 2] for band in range(bands)]
    num_slots = home.shape[1]
    none = NEAR * CAP
    core = lax.axis_index("band")
    for source, near in enumerate((core, 2 + core, 1 - core, 3 - core)):
        group = pl.ds(near * CAP, CAP)
        even = refs[source][pl.ds(0, CAP)].astype(F32)
        odd = turned(even.reshape(CAP * ROWS, LANES)).reshape(CAP, ROWS, LANES)
        stamps[group, pl.ds(0, ROWS), :] = even.astype(BF16)
        stamps[group, pl.ds(ROWS, ROWS), :] = odd.astype(BF16)
    stamps[none] = jnp.zeros((SIDE, LANES), BF16)
    for band in range(bands):
        totals[band][band % 2][...] = home[band]
        totals[band][1 - band % 2][...] = jnp.zeros_like(home[band])
    masks, row_masks = half_masks(SIDE), half_masks(1)
    read, rounds = chunk_reader(bands, plan, amps)

    def inner_products(turn, carry):
        for c in [STRIDE * turn + i for i in range(STRIDE)]:
            k, members, _, _ = read(c)
            stack = jnp.concatenate([stamps[v] for v in members], axis=0)
            inners = dot(stack[:, :SIDE], first_t[k])
            for band in range(bands):
                lanes = slice(band // 2 * LANES, (band // 2 + 1) * LANES)
                pairs = []
                for u in range(0, GROUP, 2):
                    x = inners[u * SIDE : (u + 1) * SIDE, lanes]
                    y = inners[(u + 1) * SIDE : (u + 2) * SIDE, lanes]
                    x, y = (x, turned(y)) if band % 2 == 0 else (turned(x), y)
                    pairs.append(jnp.where(masks[0], x, y))
                inner_all[c, band] = jnp.concatenate(pairs, axis=1).astype(BF16)
        return carry

    def images(turn, carry):
        for c in [STRIDE * turn + i for i in range(STRIDE)]:
            k, _, slots, values = read(c)
            for band in range(bands):
                image = dot(left[band, k], inner_all[c, band])
                for u in range(0, GROUP, 2):
                    lanes = slice(u // 2 * LANES, (u // 2 + 1) * LANES)
                    scale = jnp.where(row_masks[0], values[band][u], values[band][u + 1])
                    pair = image[:, lanes] * scale
                    for part in (0, 1):
                        totals[band][part][slots[u + part]] += pair
        return carry

    lax.fori_loop(0, rounds, inner_products, 0)
    lax.fori_loop(0, rounds, images, 0)

    def slot(q, carry):
        for band in range(bands):
            model = jnp.where(masks[0], totals[band][0][q], totals[band][1][q])
            residual[band, q] = (model + turned(model)).astype(BF16)
        return carry

    lax.fori_loop(0, num_slots, slot, 0, unroll=8)


def backward_kernel(bands, plan, amps, *refs):
    residual, inner_all, left_t, right, keep, send, stacks, sums = refs
    none = NEAR * CAP
    sums[...] = jnp.zeros_like(sums)
    keep[...] = jnp.zeros_like(keep)
    send[...] = jnp.zeros_like(send)
    masks, row_masks, packed_low = half_masks(SIDE), half_masks(1), half_masks(ROWS)[0]
    read, rounds = chunk_reader(bands, plan, amps)
    spare = none // 2
    core = lax.axis_index("band")

    def outer_products(turn, carry):
        for c in [STRIDE * turn + i for i in range(STRIDE)]:
            k, members, slots, values = read(c)
            outers = []
            for band in range(bands):
                pairs = [
                    jnp.where(masks[0], residual[band, slots[u]], residual[band, slots[u + 1]])
                    for u in range(0, GROUP, 2)
                ]
                outer = dot(left_t[band, k], jnp.concatenate(pairs, axis=1))
                along = jnp.sum(inner_all[c, band].astype(F32) * outer, axis=0, keepdims=True)
                scaled = []
                for u in range(0, GROUP, 2):
                    lanes = slice(u // 2 * LANES, (u // 2 + 1) * LANES)
                    for part in (0, 1):
                        row = jnp.where(row_masks[part], along[:, lanes], 0.0)
                        sums[band, pl.ds(members[u + part], 1), :] = row
                    scale = jnp.where(row_masks[0], values[band][u], values[band][u + 1])
                    scaled.append(outer[:, lanes] * scale)
                outers.append(scaled)
            outers += [[jnp.zeros((SIDE, LANES), F32)] * (GROUP // 2)] * (4 - bands)
            for pair in range(GROUP // 2):
                b0, b1, b2, b3 = [outers[band][pair] for band in range(4)]
                if bands > 3:
                    last = [jnp.where(masks[0], b2, turned(b3)), jnp.where(masks[0], turned(b2), b3)]
                else:
                    last = [b2, turned(b2)]
                first = [jnp.where(masks[0], b0, turned(b1)), jnp.where(masks[0], turned(b0), b1)]
                for part in (0, 1):
                    rows = slice((2 * pair + part) * SIDE, (2 * pair + part + 1) * SIDE)
                    stacks[c, rows, :] = jnp.concatenate([first[part], last[part]], axis=1).astype(BF16)
        return carry

    def gradients(turn, carry):
        for c in [STRIDE * turn + i for i in range(STRIDE)]:
            k, members, _, _ = read(c)
            grads = dot(stacks[c], right[k])
            for u, v in enumerate(members):
                top = grads[u * SIDE : u * SIDE + ROWS]
                low = grads[u * SIDE + ROWS : (u + 1) * SIDE]
                stamp = jnp.where(packed_low, top, low).astype(BF16)
                side, place = v // CAP % 2, v // (2 * CAP) * CAP + v % CAP
                keep[jnp.where(side == core, place, spare)] = stamp
                send[jnp.where(side == 1 - core, place, spare)] = stamp
        return carry

    lax.fori_loop(0, rounds, outer_products, 0)
    lax.fori_loop(0, rounds, gradients, 0)
    meta = amp_rows([lane_sums(sums[band, :none, :]) for band in range(bands)])
    keep[spare] = meta
    send[spare] = meta


def home_slots_kernel(bands, residual, left_t, right, back):
    num_slots = residual.shape[1]
    back[:, num_slots] = jnp.zeros((bands, ROWS, LANES), BF16)
    packed_low = half_masks(ROWS)[0]

    def slot(q, carry):
        for band in range(bands):
            outer = dot(left_t[band, q], residual[band, q]).astype(BF16)
            grad = dot(outer[:, :SIDE], right[q, band * SIDE : (band + 1) * SIDE, :])
            back[band, q] = jnp.where(packed_low, grad[:ROWS], grad[ROWS:]).astype(BF16)
        return carry

    lax.fori_loop(0, num_slots, slot, 0, unroll=8)


def home_gather_kernel(bands, last, lists, amps, eta_m, morph, back, received, keep, grad_a, sums):
    core = lax.axis_index("band")
    mine = pl.ds(half_rows(), HALF) if last else pl.ds(0, ROWS)

    def gather(s, carry):
        q = lists[0, 0, s]
        stamp = rounded(morph[s])
        grad = jnp.zeros((HALF if last else ROWS, LANES), F32)
        for ref, side in ((back, core), (received, 1 - core)):
            for band in range(bands):
                amp = amps[side * bands + band, s]
                if last:
                    grad = grad + amp * ref[band, q, mine, :].astype(F32)
                    if ref is received:
                        continue
                seen = ref[band, q].astype(F32)
                if not last:
                    grad = grad + amp * seen
                along = jnp.sum(seen * stamp, axis=0, keepdims=True)
                sums[side * bands + band, pl.ds(s, 1), :] = along
        keep[s] = jnp.maximum(morph[s, mine, :].astype(F32), 0.0) - eta_m[0, s] * grad
        return carry

    lax.fori_loop(0, lists.shape[2], gather, 0, unroll=4)
    for band in range(grad_a.shape[0]):
        rows = sums[core * bands + band] if last else sums[band]
        grad_a[band : band + 1, :] = lane_sums(rows)[:1]


def amp_rows(sums):
    eight = iota((8, LANES), 0)
    total = jnp.zeros((8, LANES), F32)
    for band, row in enumerate(sums):
        total = jnp.where(eight == band, row, total)
    coarse = total.astype(BF16).astype(F32)
    return jnp.concatenate([coarse, total - coarse, jnp.zeros((HALF, LANES), F32)], axis=0).astype(BF16)


def reduce_kernel(keep, received, *messages):
    for turn in range(2):
        part = pl.ds(turn * CAP, CAP)
        total = keep[part].astype(F32) + received[part].astype(F32)
        messages[turn][pl.ds(0, CAP)] = total.astype(BF16)
        pair = by_core(keep[2 * CAP].astype(F32), received[2 * CAP].astype(F32))
        meta = jnp.concatenate([pair[0][:HALF], pair[1][:HALF]], axis=0)
        messages[turn][CAP] = meta.astype(BF16)


def update_kernel(last, places, eta_m, slots_ref, eta_a, hots, amps_ref, grad_a, home, *refs):
    grads, out = refs[:NEAR], refs[NEAR:]
    state, amps_out, work = out[0], out[1], out[-1] if last else out[0]
    core = lax.axis_index("band")
    mine = pl.ds(half_rows(), HALF) if last else pl.ds(0, ROWS)
    nears = (core, 2 + core, 1 - core, 3 - core)
    lane = iota((ROWS, LANES), 1) // CAP
    meta = jnp.zeros((ROWS, LANES), F32)
    for ref, near in zip(grads, nears):
        meta = jnp.where(lane == near, ref[CAP].astype(F32), meta)
    all_hots = jnp.concatenate([hots[near, :CAP] for near in range(NEAR)], axis=0)
    from_near = dot(meta.astype(BF16), all_hots)
    bands = amps_ref.shape[0] // 2
    sides = [from_near[r : r + bands] + from_near[r + 8 : r + 8 + bands] for r in (0, HALF)]
    if last:
        amps = by_core(amps_ref[:bands], amps_ref[bands:])[0]
        total = grad_a[...] + by_core(sides[0], sides[1])[0]
    else:
        amps = amps_ref[...]
        total = grad_a[...] + jnp.concatenate(sides, axis=0)
    amps = jnp.maximum(amps - eta_a[...] * total, 0.0)
    if last:
        for band in range(bands):
            amps_out[band] = amps[band : band + 1]
    else:
        amps_out[...] = amps
    work[...] = home[...]
    for ref, near in zip(grads, nears):

        def add(n, carry, ref=ref, near=near):
            s = places[near, n]
            work[s] -= eta_m[0, s] * ref[n, mine, :].astype(F32)
            return carry

        lax.fori_loop(0, CAP, add, 0, unroll=8)

    if last:
        for r in range(HALF):
            state[:, r * LANES : (r + 1) * LANES] = jnp.maximum(work[:, r, :], 0.0)
        return
    amps_q, messages = out[2], out[3:5]
    amps_q[...] = amps.astype(BF16).astype(F32)

    def stamp_of(s):
        return jnp.maximum(state[s], 0.0).astype(BF16)

    write_messages(messages, rows_of(slots_ref), amps, hots, places, stamp_of)


def call(body, name, operands, scalars, outs, scratch=(), flops=0, moved=0):
    vmem, smem = pl.BlockSpec(memory_space=pltpu.VMEM), pl.BlockSpec(memory_space=pltpu.SMEM)
    return pl.pallas_call(
        body,
        out_shape=[jax.ShapeDtypeStruct(shape, dtype) for shape, dtype in outs],
        in_specs=[smem if i < scalars else vmem for i in range(len(operands))],
        out_specs=[vmem] * len(outs),
        scratch_shapes=[pltpu.VMEM(shape, dtype) for shape, dtype in scratch],
        compiler_params=pltpu.CompilerParams(vmem_limit_bytes=40 * 2**20),
        cost_estimate=pl.CostEstimate(flops=flops, bytes_accessed=moved, transcendentals=0),
        name=name,
    )(*operands)


def stepped(value, axis, step):
    shape = [lax.axis_size(name) for name in ("ra", "dec", "band")]

    def device(ra, dec, band):
        return (ra * shape[1] + dec) * shape[2] + band

    pairs = []
    for ra in range(shape[0]):
        for dec in range(shape[1]):
            for band, by in ((0, step), (1, -step)):
                if axis == "ra":
                    pairs.append((device(ra, dec, band), device((ra + by) % shape[0], dec, band)))
                elif 0 <= dec + by < shape[1]:
                    pairs.append((device(ra, dec, band), device(ra, dec + by, band)))
    return lax.ppermute(value, ("ra", "dec", "band"), pairs)


def swapped(value):
    return lax.ppermute(value, "band", [(0, 1), (1, 0)])


def all_tables(psf, num_slots, messages, sums):
    bands, held = psf.shape[:2]
    lines = lax.axis_size("dec")
    if lax.axis_size("ra") == 4 and 2 * held == num_slots and held % 2 == 0 and lines % 2 == 0:
        across = [(i, i + 1 - 2 * (i % 2)) for i in range(lines)]
        along = [(0, 1), (1, 0), (2, 3), (3, 2)]
        mine = jnp.where(lax.axis_index("dec") % 2 == 0, psf[:, : held // 2], psf[:, held // 2 :])
        far = lax.ppermute(mine, "ra", [(0, 2), (1, 3)])
        far, sums = lax.optimization_barrier((far, sums))
        here = jnp.where(lax.axis_index("ra") < 2, mine, far)
        here, messages[0] = lax.optimization_barrier((here, messages[0]))
        near = lax.ppermute(here, "ra", along)
        halves = make_tables((here, near), bands)
        others = (lax.ppermute(here, "dec", across), lax.ppermute(near, "dec", across))
        return make_tables(others, bands, halves), messages, sums
    return make_tables((lax.all_gather(psf, "ra", axis=1, tiled=True)[:, :num_slots],), bands), messages, sums


def shards(morphology, sed_amps, slot_lists, morph_step, sed_step, psf_kernels, observed):
    bands, num_slots, sources = sed_amps.shape[2], observed.shape[3], morphology.shape[2]
    lists, amps = slot_lists[0, 0][:, None, :], sed_amps[0, 0][:, None, :]
    eta_m, eta_a = morph_step[0], sed_step[0]
    full = morphology[0, 0].reshape(sources, ROWS, LANES)
    seen = observed[0, 0].reshape(bands, num_slots, ROWS, LANES)
    stamp = ((CAP + 1, ROWS, LANES), BF16)
    all_stamps = (sources, ROWS, LANES)
    near_all = NEAR * CAP
    chunks = -(-(near_all // GROUP + num_slots) // STRIDE) * STRIDE
    amps_theirs = swapped(amps)
    hots, places = call(
        functools.partial(lists_kernel, num_slots),
        "lists",
        (lists,),
        0,
        [
            ((NEAR, LANES, sources), BF16),
            ((2 * NEAR, LANES), jnp.int32),
        ],
        moved=2**20,
    )
    *messages, amps, amps_q = call(
        pack_kernel,
        "pack",
        (places, lists, amps, amps_theirs, hots, full),
        1,
        [stamp] * 2 + [((2 * bands, sources), F32)] * 2,
        moved=2**20,
    )
    def home_sums(amps_q, morph):
        return call(
            functools.partial(home_sums_kernel, bands),
            "home_sums",
            (lists, amps_q, morph),
            2,
            [((bands, num_slots + 1, ROWS, LANES), F32)],
            moved=4 * 2**20,
        )[0]

    sums = home_sums(amps_q, full)
    tables, messages, sums = all_tables(psf_kernels, num_slots, messages, sums)
    first_t, left, left_t, right = tables
    morph, plan = full, None
    for sweep in range(ITERS):
        last = sweep == ITERS - 1
        own = [stepped(messages[0], "ra", 1), stepped(messages[1], "dec", 1)]
        if sweep == 0:
            left, *own = lax.optimization_barrier((left, *own))
        else:
            sums = home_sums(amps_q, morph)
        home = call(
            functools.partial(home_forward_kernel, bands),
            "home_forward",
            (sums, seen, first_t, left),
            0,
            [((bands, num_slots, SIDE, LANES), F32)],
            [((bands, num_slots, SIDE, LANES), BF16)],
            flops=2 * 10**9,
            moved=4 * 2**20,
        )[0]
        if sweep > 0:
            own = [lax.optimization_barrier((home, x))[1] for x in own]
        other = [swapped(x) for x in own]
        amps_near, *new_plan = call(
            functools.partial(order_kernel, num_slots, sweep > 0),
            "order",
            (*own, *other),
            0,
            [((bands, LANES), F32)] + [((8, -(-chunks * GROUP // LANES) * LANES), jnp.int32)] * (sweep == 0),
            moved=2**20,
        )
        plan = new_plan[0] if new_plan else plan
        residual, inner_all = call(
            functools.partial(forward_kernel, bands),
            "forward",
            (plan, amps_near, *own, *other, home, first_t, left),
            2,
            [
                ((bands, num_slots, SIDE, LANES), BF16),
                ((chunks, bands, SIDE, WIDE), BF16),
            ],
            [((near_all + 1, SIDE, LANES), BF16)] + [((num_slots, SIDE, LANES), F32)] * (2 * bands),
            flops=3 * 10**9,
            moved=8 * 2**20,
        )
        half_of_near = ((near_all // 2 + 1, ROWS, LANES), BF16)
        keep, send = call(
            functools.partial(backward_kernel, bands),
            "backward",
            (plan, amps_near, residual, inner_all, left_t, right),
            2,
            [half_of_near] * 2,
            [((chunks, WIDE, WIDE), BF16), ((bands, near_all + 8, LANES), F32)],
            flops=3 * 10**9,
            moved=8 * 2**20,
        )
        received = swapped(send)
        back = call(
            functools.partial(home_slots_kernel, bands),
            "home_slots",
            (residual, left_t, right),
            0,
            [((bands, num_slots + 1, ROWS, LANES), BF16)],
            flops=2 * 10**9,
            moved=4 * 2**20,
        )[0]
        received, back = lax.optimization_barrier((received, back))
        grads = call(reduce_kernel, "reduce", (keep, received), 0, [stamp] * 2, moved=2 * 2**20)
        grads = [stepped(grads[0], "ra", -1), stepped(grads[1], "dec", -1)]
        back_received = swapped(back)
        bands_here = bands if last else 2 * bands
        part = (sources, HALF, LANES) if last else all_stamps
        home_grad, grad_a = call(
            functools.partial(home_gather_kernel, bands, last),
            "home_gather",
            (lists, amps_q, eta_m, morph, back, back_received),
            3,
            [(part, F32), ((bands_here, sources), F32)],
            [((2 * bands, sources, LANES), F32)],
            moved=4 * 2**20,
        )
        grads = [lax.optimization_barrier((home_grad, x))[1] for x in grads]
        grads += [swapped(x) for x in grads]
        outs = [((sources, HALF * LANES) if last else all_stamps, F32)]
        outs += [((bands, 1, sources) if last else (2 * bands, sources), F32)]
        if not last:
            outs += [((bands_here, sources), F32)] + [stamp] * 2
        state, amps, *more = call(
            functools.partial(update_kernel, last),
            "update",
            (places, eta_m, lists, eta_a, hots, amps, grad_a, home_grad, *grads),
            2,
            outs,
            [(part, F32)] if last else (),
            moved=3 * 2**20,
        )
        if not last:
            morph = state
            amps_q, *messages = more
    return state[None, None], amps.reshape(1, 1, bands, sources)


def solution(mesh):
    in_specs = (
        P("ra", "dec", None, None),
        P("ra", "dec", "band", None),
        P("ra", "dec", None, None),
        P("ra", "dec", None),
        P("ra", "dec", None),
        P("band", "ra", None),
        P("ra", "dec", "band", None, None),
    )
    out_specs = (P("ra", "dec", None, "band"), P("ra", "dec", "band", None))
    return jax.shard_map(shards, mesh=mesh, in_specs=in_specs, out_specs=out_specs, check_vma=False)
```

```python
import functools

import jax
import jax.numpy as jnp
from jax import lax
from jax.experimental import pallas as pl
from jax.experimental.pallas import tpu as pltpu
from jax.sharding import PartitionSpec as P

SIDE = 64
KERN = 32
ITERS = 2
CAP = 32
LANES = 128
ROWS = SIDE * SIDE // LANES
HALF = ROWS // 2
WIDE = 4 * SIDE
ORDER, KERNEL_OF, SLOT_OF, COUNT = range(4)
NEAR = 4
GROUP = 4
STRIDE = 4
F32 = jnp.float32
BF16 = jnp.bfloat16


def dot(a, b):
    return lax.dot_general(a, b, (((1,), (0,)), ((), ())), preferred_element_type=F32)


def dot_nt(a, b):
    return lax.dot_general(a, b, (((1,), (1,)), ((), ())), preferred_element_type=F32)


def iota(shape, dim):
    return lax.broadcasted_iota(jnp.int32, shape, dim)


def low_lanes(rows, dtype=F32):
    return (iota((rows, LANES), 1) < SIDE).astype(F32).astype(dtype)


def lane_sums(rows):
    coarse = rows.astype(BF16)
    fine = (rows - coarse.astype(F32)).astype(BF16)
    ones = jnp.ones((8, rows.shape[1]), BF16)
    return dot_nt(ones, coarse) + dot_nt(ones, fine)


def half_masks(rows):
    low = iota((rows, LANES), 1) < SIDE
    return low, jnp.logical_not(low)


def turned(value):
    return pltpu.roll(value, SIDE, 1)


def twofold(packed):
    low, flip = half_masks(ROWS)[0], turned(packed)
    return jnp.concatenate([jnp.where(low, packed, flip), jnp.where(low, flip, packed)], axis=0)


def rounded(stamp):
    if stamp.dtype == F32:
        stamp = jnp.maximum(stamp, 0.0).astype(BF16)
    return stamp.astype(F32)


def half_rows():
    return pl.multiple_of(lax.axis_index("band") * HALF, HALF)


def rows_of(ref):
    return jnp.concatenate([ref[i] for i in range(ref.shape[0])], axis=0)


def by_core(mine, theirs):
    first = lax.axis_index("band") == 0
    return jnp.where(first, mine, theirs), jnp.where(first, theirs, mine)


def lists_kernel(num_slots, slots_ref, hots, places):
    slots = rows_of(slots_ref)
    sources = slots.shape[1]
    valid = (slots < num_slots).astype(F32)
    upper = (iota((sources, sources), 0) <= iota((sources, sources), 1)).astype(F32)
    rank = dot(valid.astype(BF16), upper.astype(BF16))
    place = iota((LANES, sources), 0).astype(F32)
    names = iota((8, sources), 1).astype(F32).astype(BF16)
    for near in range(NEAR):
        row = slice(near + 1, near + 2)
        hot = ((place == rank[row] - 1.0).astype(F32) * valid[row]).astype(BF16)
        hots[near] = hot
        places[near : near + 1, :] = dot_nt(names, hot)[:1].astype(jnp.int32)
        count = jnp.broadcast_to(rank[row, sources - 1 :], (1, LANES))
        places[NEAR + near : NEAR + near + 1, :] = count.astype(jnp.int32)


def write_messages(messages, slots, amps, hots, places, stamp_of):
    first = lax.axis_index("band") == 0
    row = iota((ROWS, slots.shape[1]), 0)
    for turn in range(2):
        near = 2 * turn + lax.axis_index("band")

        def pick(n, carry, near=near, turn=turn):
            messages[turn][n] = stamp_of(places[near, n])
            return carry

        lax.fori_loop(0, CAP, pick, 0, unroll=8)
        slot = jnp.where(first, slots[2 * turn + 1 : 2 * turn + 2], slots[2 * turn + 2 : 2 * turn + 3]).astype(F32)
        meta = jnp.where(row == 0, slot + 1.0, 0.0)
        meta = jnp.where(row == 1, slots[0:1].astype(F32), meta)
        for band in range(amps.shape[0]):
            meta = jnp.where(row == 2 + band, amps[band : band + 1], meta)
        hot = jnp.where(first, hots[2 * turn].astype(F32), hots[2 * turn + 1].astype(F32)).astype(BF16)
        messages[turn][CAP] = dot_nt(meta.astype(BF16), hot).astype(BF16)


def pack_kernel(places, slots_ref, amps_mine, amps_theirs, hots, morph, *out):
    messages, amps_out, amps_q = out[:2], out[2], out[3]
    amps = jnp.concatenate(by_core(rows_of(amps_mine), rows_of(amps_theirs)), axis=0)
    write_messages(messages, rows_of(slots_ref), amps, hots, places, lambda s: morph[s])
    amps_out[...] = amps
    amps_q[...] = amps.astype(BF16).astype(F32)


def order_kernel(num_slots, again, *refs):
    amps, none = refs[NEAR], NEAR * CAP
    bands = amps.shape[0]
    meta = jnp.zeros((ROWS, LANES), F32)
    for turn in range(2):
        pair = by_core(refs[turn][CAP].astype(F32), refs[2 + turn][CAP].astype(F32))
        for core in range(2):
            meta = meta + pltpu.roll(pair[core], (2 * turn + core) * CAP, 1)
    amps[...] = by_core(meta[2 : 2 + bands], meta[2 + bands : 2 + 2 * bands])[0]
    if again:
        return
    plan, slot, kernel = refs[NEAR + 1], meta[0:1], meta[1:2]
    plan[SLOT_OF : SLOT_OF + 1, :LANES] = jnp.maximum(slot - 1.0, 0.0).astype(jnp.int32)
    live = (slot > 0.0).astype(F32)
    hot = (iota((num_slots, none), 0).astype(F32) == kernel).astype(F32) * live
    upto = (iota((none, none), 0) <= iota((none, none), 1)).astype(F32).astype(BF16)
    rank = dot(hot.astype(BF16), upto)
    size = jnp.max(rank, axis=1, keepdims=True)
    filled = ((size.astype(jnp.int32) + (GROUP - 1)) // GROUP).astype(F32)
    before = (iota((num_slots, num_slots), 1) < iota((num_slots, num_slots), 0)).astype(F32).astype(BF16)
    start = dot(before, jnp.broadcast_to(filled, (num_slots, none)).astype(BF16))
    place = jnp.sum(hot * (GROUP * start + rank), axis=0, keepdims=True) - 1.0
    eight = iota((8, none), 0)
    names = jnp.where(eight == 0, iota((8, none), 1).astype(F32) - none, 0.0).astype(BF16)
    for part in range(plan.shape[1] // LANES):
        at = (iota((LANES, none), 0) + part * LANES).astype(F32)
        hit = (at == place).astype(F32) * live
        found = dot_nt(names, hit.astype(BF16))[:1] + none
        plan[ORDER : ORDER + 1, part * LANES : (part + 1) * LANES] = found.astype(jnp.int32)
    chunk = iota((num_slots, LANES), 1).astype(F32)
    row = iota((num_slots, LANES), 0).astype(F32)
    inside = (chunk >= start[:, :LANES]) & (chunk < start[:, :LANES] + filled)
    kernels = jnp.sum(jnp.where(inside, row, 0.0), axis=0, keepdims=True)
    plan[KERNEL_OF : KERNEL_OF + 1, :LANES] = kernels.astype(jnp.int32)
    total = jnp.sum(filled, axis=0, keepdims=True)
    plan[COUNT : COUNT + 1, :LANES] = jnp.broadcast_to(total, (1, LANES)).astype(jnp.int32)


def quarter_start(quarter, held):
    parity, line = lax.axis_index("ra") % 2, lax.axis_index("dec") // (lax.axis_size("dec") // 2)
    shard = parity if quarter % 2 == 0 else 1 - parity
    half = line if quarter < 2 else 1 - line
    return (2 * shard + half) * held


def tables_kernel(bands, earlier, *refs):
    shards, (first_t, left, left_t, right, packed) = refs[: len(refs) - 5 - 4 * earlier], refs[-5:]
    held = shards[0].shape[1]
    for turn, ref in enumerate(shards):
        for band in range(bands):
            for r in range(ROWS):
                rows = pl.ds(turn * held * ROWS + r, held, stride=ROWS)
                packed[band, rows, :] = ref[band, :, r * LANES : (r + 1) * LANES].astype(F32)
    starts = [quarter_start(2 + turn, held) if earlier else turn * held for turn in range(len(shards))]
    if earlier:
        old_first, old_left, old_left_t, old_right = refs[len(shards) : len(shards) + 4]
        for turn in range(2):
            old, new = pl.ds(turn * held, held), pl.ds(quarter_start(turn, held), held)
            first_t[new] = old_first[old]
            right[new] = old_right[old]
            for band in range(bands):
                left[band, new] = old_left[band, old]
                left_t[band, new] = old_left_t[band, old]
    eye = (iota((SIDE, SIDE), 0) == iota((SIDE, SIDE), 1)).astype(F32).astype(BF16)
    row, col = iota((SIDE, SIDE), 0), iota((SIDE, SIDE), 1)
    even = (col == 2 * (row % ROWS) + row // ROWS).astype(F32).astype(BF16)
    even_t = (row == 2 * (col % ROWS) + col // ROWS).astype(F32).astype(BF16)
    rest = [jnp.zeros((SIDE * (4 - bands), SIDE), BF16)] if bands < 4 else []

    def step(place, carry):
        for turn, start in enumerate(starts):
            k = start + place
            at = pl.multiple_of((turn * held + place) * ROWS, ROWS)
            parts = [twofold(packed[band, pl.ds(at, ROWS), :]).astype(BF16) for band in range(bands)]
            lefts = dot_nt(jnp.concatenate([part[:, :SIDE] for part in parts], axis=0), even).astype(BF16)
            natural = []
            for band, part in enumerate(parts):
                rows = slice(band * SIDE, (band + 1) * SIDE)
                left[band, k] = lefts[rows]
                left_t[band, k] = dot_nt(even, part[:, :SIDE]).astype(BF16)
                both = dot(even_t, part).astype(BF16)
                right[k, rows, :] = both
                natural.append(both[:, :SIDE])
            if rest:
                right[k, bands * SIDE :, :] = jnp.zeros((SIDE * (4 - bands), LANES), BF16)
            first_t[k] = dot_nt(eye, jnp.concatenate(natural + rest, axis=0)).astype(BF16)
        return carry

    lax.fori_loop(0, held, step, 0, unroll=min(held, 4))


def make_tables(shards, bands, earlier=()):
    count = sum(x.shape[1] for x in shards)
    total = count + sum(x.shape[0] for x in earlier[:1])
    square = ((bands, total, SIDE, SIDE), BF16)
    return call(
        functools.partial(tables_kernel, bands, bool(earlier)),
        "tables",
        (*shards, *earlier),
        0,
        [((total, SIDE, WIDE), BF16), square, square, ((total, WIDE, LANES), BF16)],
        [((bands, count * ROWS, LANES), F32)],
        flops=2 * 10**9,
        moved=5 * 2**20,
    )


def home_sums_kernel(bands, lists, amps, morph, sums):
    first = lax.axis_index("band") * bands
    sums[...] = jnp.zeros_like(sums)

    def add(s, carry):
        q = lists[0, 0, s]
        stamp = rounded(morph[s])
        for band in range(bands):
            sums[band, q] += amps[first + band, s] * stamp
        return carry

    lax.fori_loop(0, lists.shape[2], add, 0, unroll=4)


def home_forward_kernel(bands, sums, observed, first_t, left, total, inner_all):
    num_slots = total.shape[1]
    masks = half_masks(SIDE)

    def inner_products(q, carry):
        images = []
        for band in range(bands):
            both = sums[band, q]
            images += [both[:, :SIDE], turned(both)[:, :SIDE]]
        inners = dot(jnp.concatenate(images, axis=0).astype(BF16), first_t[q])
        for band in range(bands):
            lanes = slice(band // 2 * LANES, (band // 2 + 1) * LANES)
            inner_all[band, q] = inners[band * SIDE : (band + 1) * SIDE, lanes].astype(BF16)
        return carry

    def slot(q, carry):
        for band in range(bands):
            image = dot(left[band, q], inner_all[band, q]) - twofold(observed[band, q].astype(F32))
            total[band, q] = jnp.where(masks[band % 2], image, 0.0)
        return carry

    lax.fori_loop(0, num_slots, inner_products, 0, unroll=4)
    lax.fori_loop(0, num_slots, slot, 0, unroll=4)


def chunk_reader(bands, plan, amps):
    none = NEAR * CAP

    def read(c):
        members = [plan[ORDER, c * GROUP + u] for u in range(GROUP)]
        held = [jnp.minimum(v, none - 1) for v in members]
        values = [[jnp.where(v < none, amps[band, h], 0.0) for v, h in zip(members, held)] for band in range(bands)]
        return plan[KERNEL_OF, c], members, [plan[SLOT_OF, h] for h in held], values

    return read, (plan[COUNT, 0] + STRIDE - 1) // STRIDE


def forward_kernel(bands, plan, amps, *refs):
    home, first_t, left = refs[NEAR : NEAR + 3]
    residual, inner_all, stamps, *totals = refs[NEAR + 3 :]
    totals = [totals[2 * band : 2 * band + 2] for band in range(bands)]
    num_slots = home.shape[1]
    none = NEAR * CAP
    core = lax.axis_index("band")
    for source, near in enumerate((core, 2 + core, 1 - core, 3 - core)):
        group = pl.ds(near * CAP, CAP)
        even = refs[source][pl.ds(0, CAP)].astype(F32)
        odd = turned(even.reshape(CAP * ROWS, LANES)).reshape(CAP, ROWS, LANES)
        stamps[group, pl.ds(0, ROWS), :] = even.astype(BF16)
        stamps[group, pl.ds(ROWS, ROWS), :] = odd.astype(BF16)
    stamps[none] = jnp.zeros((SIDE, LANES), BF16)
    for band in range(bands):
        totals[band][band % 2][...] = home[band]
        totals[band][1 - band % 2][...] = jnp.zeros_like(home[band])
    masks, row_masks = half_masks(SIDE), half_masks(1)
    read, rounds = chunk_reader(bands, plan, amps)

    def inner_products(turn, carry):
        for c in [STRIDE * turn + i for i in range(STRIDE)]:
            k, members, _, _ = read(c)
            stack = jnp.concatenate([stamps[v] for v in members], axis=0)
            inners = dot(stack[:, :SIDE], first_t[k])
            for band in range(bands):
                lanes = slice(band // 2 * LANES, (band // 2 + 1) * LANES)
                pairs = []
                for u in range(0, GROUP, 2):
                    x = inners[u * SIDE : (u + 1) * SIDE, lanes]
                    y = inners[(u + 1) * SIDE : (u + 2) * SIDE, lanes]
                    x, y = (x, turned(y)) if band % 2 == 0 else (turned(x), y)
                    pairs.append(jnp.where(masks[0], x, y))
                inner_all[c, band] = jnp.concatenate(pairs, axis=1).astype(BF16)
        return carry

    def images(turn, carry):
        for c in [STRIDE * turn + i for i in range(STRIDE)]:
            k, _, slots, values = read(c)
            for band in range(bands):
                image = dot(left[band, k], inner_all[c, band])
                for u in range(0, GROUP, 2):
                    lanes = slice(u // 2 * LANES, (u // 2 + 1) * LANES)
                    scale = jnp.where(row_masks[0], values[band][u], values[band][u + 1])
                    pair = image[:, lanes] * scale
                    for part in (0, 1):
                        totals[band][part][slots[u + part]] += pair
        return carry

    lax.fori_loop(0, rounds, inner_products, 0)
    lax.fori_loop(0, rounds, images, 0)

    def slot(q, carry):
        for band in range(bands):
            model = jnp.where(masks[0], totals[band][0][q], totals[band][1][q])
            residual[band, q] = (model + turned(model)).astype(BF16)
        return carry

    lax.fori_loop(0, num_slots, slot, 0, unroll=8)


def backward_kernel(bands, plan, amps, *refs):
    residual, inner_all, left_t, right, keep, send, stacks, sums = refs
    none = NEAR * CAP
    sums[...] = jnp.zeros_like(sums)
    keep[...] = jnp.zeros_like(keep)
    send[...] = jnp.zeros_like(send)
    masks, row_masks, packed_low = half_masks(SIDE), half_masks(1), half_masks(ROWS)[0]
    read, rounds = chunk_reader(bands, plan, amps)
    spare = none // 2
    core = lax.axis_index("band")

    def outer_products(turn, carry):
        for c in [STRIDE * turn + i for i in range(STRIDE)]:
            k, members, slots, values = read(c)
            outers = []
            for band in range(bands):
                pairs = [
                    jnp.where(masks[0], residual[band, slots[u]], residual[band, slots[u + 1]])
                    for u in range(0, GROUP, 2)
                ]
                outer = dot(left_t[band, k], jnp.concatenate(pairs, axis=1))
                along = jnp.sum(inner_all[c, band].astype(F32) * outer, axis=0, keepdims=True)
                scaled = []
                for u in range(0, GROUP, 2):
                    lanes = slice(u // 2 * LANES, (u // 2 + 1) * LANES)
                    for part in (0, 1):
                        row = jnp.where(row_masks[part], along[:, lanes], 0.0)
                        sums[band, pl.ds(members[u + part], 1), :] = row
                    scale = jnp.where(row_masks[0], values[band][u], values[band][u + 1])
                    scaled.append(outer[:, lanes] * scale)
                outers.append(scaled)
            outers += [[jnp.zeros((SIDE, LANES), F32)] * (GROUP // 2)] * (4 - bands)
            for pair in range(GROUP // 2):
                b0, b1, b2, b3 = [outers[band][pair] for band in range(4)]
                if bands > 3:
                    last = [jnp.where(masks[0], b2, turned(b3)), jnp.where(masks[0], turned(b2), b3)]
                else:
                    last = [b2, turned(b2)]
                first = [jnp.where(masks[0], b0, turned(b1)), jnp.where(masks[0], turned(b0), b1)]
                for part in (0, 1):
                    rows = slice((2 * pair + part) * SIDE, (2 * pair + part + 1) * SIDE)
                    stacks[c, rows, :] = jnp.concatenate([first[part], last[part]], axis=1).astype(BF16)
        return carry

    def gradients(turn, carry):
        for c in [STRIDE * turn + i for i in range(STRIDE)]:
            k, members, _, _ = read(c)
            grads = dot(stacks[c], right[k])
            for u, v in enumerate(members):
                top = grads[u * SIDE : u * SIDE + ROWS]
                low = grads[u * SIDE + ROWS : (u + 1) * SIDE]
                stamp = jnp.where(packed_low, top, low).astype(BF16)
                side, place = v // CAP % 2, v // (2 * CAP) * CAP + v % CAP
                keep[jnp.where(side == core, place, spare)] = stamp
                send[jnp.where(side == 1 - core, place, spare)] = stamp
        return carry

    lax.fori_loop(0, rounds, outer_products, 0)
    lax.fori_loop(0, rounds, gradients, 0)
    meta = amp_rows([lane_sums(sums[band, :none, :]) for band in range(bands)])
    keep[spare] = meta
    send[spare] = meta


def home_slots_kernel(bands, residual, left_t, right, back):
    num_slots = residual.shape[1]
    back[:, num_slots] = jnp.zeros((bands, ROWS, LANES), BF16)
    packed_low = half_masks(ROWS)[0]

    def slot(q, carry):
        for band in range(bands):
            outer = dot(left_t[band, q], residual[band, q]).astype(BF16)
            grad = dot(outer[:, :SIDE], right[q, band * SIDE : (band + 1) * SIDE, :])
            back[band, q] = jnp.where(packed_low, grad[:ROWS], grad[ROWS:]).astype(BF16)
        return carry

    lax.fori_loop(0, num_slots, slot, 0, unroll=8)


def home_gather_kernel(bands, last, lists, amps, eta_m, morph, back, received, keep, grad_a, sums):
    core = lax.axis_index("band")
    mine = pl.ds(half_rows(), HALF) if last else pl.ds(0, ROWS)

    def gather(s, carry):
        q = lists[0, 0, s]
        stamp = rounded(morph[s])
        grad = jnp.zeros((HALF if last else ROWS, LANES), F32)
        for ref, side in ((back, core), (received, 1 - core)):
            for band in range(bands):
                amp = amps[side * bands + band, s]
                if last:
                    grad = grad + amp * ref[band, q, mine, :].astype(F32)
                    if ref is received:
                        continue
                seen = ref[band, q].astype(F32)
                if not last:
                    grad = grad + amp * seen
                along = jnp.sum(seen * stamp, axis=0, keepdims=True)
                sums[side * bands + band, pl.ds(s, 1), :] = along
        keep[s] = jnp.maximum(morph[s, mine, :].astype(F32), 0.0) - eta_m[0, s] * grad
        return carry

    lax.fori_loop(0, lists.shape[2], gather, 0, unroll=4)
    for band in range(grad_a.shape[0]):
        rows = sums[core * bands + band] if last else sums[band]
        grad_a[band : band + 1, :] = lane_sums(rows)[:1]


def amp_rows(sums):
    eight = iota((8, LANES), 0)
    total = jnp.zeros((8, LANES), F32)
    for band, row in enumerate(sums):
        total = jnp.where(eight == band, row, total)
    coarse = total.astype(BF16).astype(F32)
    return jnp.concatenate([coarse, total - coarse, jnp.zeros((HALF, LANES), F32)], axis=0).astype(BF16)


def reduce_kernel(keep, received, *messages):
    for turn in range(2):
        part = pl.ds(turn * CAP, CAP)
        total = keep[part].astype(F32) + received[part].astype(F32)
        messages[turn][pl.ds(0, CAP)] = total.astype(BF16)
        pair = by_core(keep[2 * CAP].astype(F32), received[2 * CAP].astype(F32))
        meta = jnp.concatenate([pair[0][:HALF], pair[1][:HALF]], axis=0)
        messages[turn][CAP] = meta.astype(BF16)


def update_kernel(last, places, eta_m, slots_ref, eta_a, hots, amps_ref, grad_a, home, *refs):
    grads, out = refs[:NEAR], refs[NEAR:]
    state, amps_out, work = out[0], out[1], out[-1] if last else out[0]
    core = lax.axis_index("band")
    mine = pl.ds(half_rows(), HALF) if last else pl.ds(0, ROWS)
    nears = (core, 2 + core, 1 - core, 3 - core)
    lane = iota((ROWS, LANES), 1) // CAP
    meta = jnp.zeros((ROWS, LANES), F32)
    for ref, near in zip(grads, nears):
        meta = jnp.where(lane == near, ref[CAP].astype(F32), meta)
    all_hots = jnp.concatenate([hots[near, :CAP] for near in range(NEAR)], axis=0)
    from_near = dot(meta.astype(BF16), all_hots)
    bands = amps_ref.shape[0] // 2
    sides = [from_near[r : r + bands] + from_near[r + 8 : r + 8 + bands] for r in (0, HALF)]
    if last:
        amps = by_core(amps_ref[:bands], amps_ref[bands:])[0]
        total = grad_a[...] + by_core(sides[0], sides[1])[0]
    else:
        amps = amps_ref[...]
        total = grad_a[...] + jnp.concatenate(sides, axis=0)
    amps = jnp.maximum(amps - eta_a[...] * total, 0.0)
    if last:
        for band in range(bands):
            amps_out[band] = amps[band : band + 1]
    else:
        amps_out[...] = amps
    work[...] = home[...]
    for ref, near in zip(grads, nears):

        def add(n, carry, ref=ref, near=near):
            s = places[near, n]
            work[s] -= eta_m[0, s] * ref[n, mine, :].astype(F32)
            return carry

        lax.fori_loop(0, CAP, add, 0, unroll=8)

    if last:
        for r in range(HALF):
            state[:, r * LANES : (r + 1) * LANES] = jnp.maximum(work[:, r, :], 0.0)
        return
    amps_q, messages = out[2], out[3:5]
    amps_q[...] = amps.astype(BF16).astype(F32)

    def stamp_of(s):
        return jnp.maximum(state[s], 0.0).astype(BF16)

    write_messages(messages, rows_of(slots_ref), amps, hots, places, stamp_of)


def call(body, name, operands, scalars, outs, scratch=(), flops=0, moved=0):
    vmem, smem = pl.BlockSpec(memory_space=pltpu.VMEM), pl.BlockSpec(memory_space=pltpu.SMEM)
    return pl.pallas_call(
        body,
        out_shape=[jax.ShapeDtypeStruct(shape, dtype) for shape, dtype in outs],
        in_specs=[smem if i < scalars else vmem for i in range(len(operands))],
        out_specs=[vmem] * len(outs),
        scratch_shapes=[pltpu.VMEM(shape, dtype) for shape, dtype in scratch],
        compiler_params=pltpu.CompilerParams(vmem_limit_bytes=40 * 2**20),
        cost_estimate=pl.CostEstimate(flops=flops, bytes_accessed=moved, transcendentals=0),
        name=name,
    )(*operands)


def stepped(value, axis, step):
    shape = [lax.axis_size(name) for name in ("ra", "dec", "band")]

    def device(ra, dec, band):
        return (ra * shape[1] + dec) * shape[2] + band

    pairs = []
    for ra in range(shape[0]):
        for dec in range(shape[1]):
            for band, by in ((0, step), (1, -step)):
                if axis == "ra":
                    pairs.append((device(ra, dec, band), device((ra + by) % shape[0], dec, band)))
                elif 0 <= dec + by < shape[1]:
                    pairs.append((device(ra, dec, band), device(ra, dec + by, band)))
    return lax.ppermute(value, ("ra", "dec", "band"), pairs)


def swapped(value):
    return lax.ppermute(value, "band", [(0, 1), (1, 0)])


def all_tables(psf, num_slots, messages, sums):
    bands, held = psf.shape[:2]
    lines = lax.axis_size("dec")
    if lax.axis_size("ra") == 4 and 2 * held == num_slots and held % 2 == 0 and lines % 2 == 0:
        across = [(i, (i + lines // 2) % lines) for i in range(lines)]
        along = [(0, 1), (1, 0), (2, 3), (3, 2)]
        mine = jnp.where(lax.axis_index("dec") < lines // 2, psf[:, : held // 2], psf[:, held // 2 :])
        far = lax.ppermute(mine, "ra", [(0, 2), (1, 3)])
        far, sums = lax.optimization_barrier((far, sums))
        here = jnp.where(lax.axis_index("ra") < 2, mine, far)
        here, messages[0] = lax.optimization_barrier((here, messages[0]))
        near = lax.ppermute(here, "ra", along)
        halves = make_tables((here, near), bands)
        others = (lax.ppermute(here, "dec", across), lax.ppermute(near, "dec", across))
        return make_tables(others, bands, halves), messages, sums
    return make_tables((lax.all_gather(psf, "ra", axis=1, tiled=True)[:, :num_slots],), bands), messages, sums


def shards(morphology, sed_amps, slot_lists, morph_step, sed_step, psf_kernels, observed):
    bands, num_slots, sources = sed_amps.shape[2], observed.shape[3], morphology.shape[2]
    lists, amps = slot_lists[0, 0][:, None, :], sed_amps[0, 0][:, None, :]
    eta_m, eta_a = morph_step[0], sed_step[0]
    full = morphology[0, 0].reshape(sources, ROWS, LANES)
    seen = observed[0, 0].reshape(bands, num_slots, ROWS, LANES)
    stamp = ((CAP + 1, ROWS, LANES), BF16)
    all_stamps = (sources, ROWS, LANES)
    near_all = NEAR * CAP
    chunks = -(-(near_all // GROUP + num_slots) // STRIDE) * STRIDE
    amps_theirs = swapped(amps)
    hots, places = call(
        functools.partial(lists_kernel, num_slots),
        "lists",
        (lists,),
        0,
        [
            ((NEAR, LANES, sources), BF16),
            ((2 * NEAR, LANES), jnp.int32),
        ],
        moved=2**20,
    )
    *messages, amps, amps_q = call(
        pack_kernel,
        "pack",
        (places, lists, amps, amps_theirs, hots, full),
        1,
        [stamp] * 2 + [((2 * bands, sources), F32)] * 2,
        moved=2**20,
    )
    def home_sums(amps_q, morph):
        return call(
            functools.partial(home_sums_kernel, bands),
            "home_sums",
            (lists, amps_q, morph),
            2,
            [((bands, num_slots + 1, ROWS, LANES), F32)],
            moved=4 * 2**20,
        )[0]

    sums = home_sums(amps_q, full)
    tables, messages, sums = all_tables(psf_kernels, num_slots, messages, sums)
    first_t, left, left_t, right = tables
    morph, plan = full, None
    for sweep in range(ITERS):
        last = sweep == ITERS - 1
        own = [stepped(messages[0], "ra", 1), stepped(messages[1], "dec", 1)]
        if sweep == 0:
            left, *own = lax.optimization_barrier((left, *own))
        else:
            sums = home_sums(amps_q, morph)
        home = call(
            functools.partial(home_forward_kernel, bands),
            "home_forward",
            (sums, seen, first_t, left),
            0,
            [((bands, num_slots, SIDE, LANES), F32)],
            [((bands, num_slots, SIDE, LANES), BF16)],
            flops=2 * 10**9,
            moved=4 * 2**20,
        )[0]
        if sweep > 0:
            own = [lax.optimization_barrier((home, x))[1] for x in own]
        other = [swapped(x) for x in own]
        amps_near, *new_plan = call(
            functools.partial(order_kernel, num_slots, sweep > 0),
            "order",
            (*own, *other),
            0,
            [((bands, LANES), F32)] + [((8, -(-chunks * GROUP // LANES) * LANES), jnp.int32)] * (sweep == 0),
            moved=2**20,
        )
        plan = new_plan[0] if new_plan else plan
        residual, inner_all = call(
            functools.partial(forward_kernel, bands),
            "forward",
            (plan, amps_near, *own, *other, home, first_t, left),
            2,
            [
                ((bands, num_slots, SIDE, LANES), BF16),
                ((chunks, bands, SIDE, WIDE), BF16),
            ],
            [((near_all + 1, SIDE, LANES), BF16)] + [((num_slots, SIDE, LANES), F32)] * (2 * bands),
            flops=3 * 10**9,
            moved=8 * 2**20,
        )
        half_of_near = ((near_all // 2 + 1, ROWS, LANES), BF16)
        keep, send = call(
            functools.partial(backward_kernel, bands),
            "backward",
            (plan, amps_near, residual, inner_all, left_t, right),
            2,
            [half_of_near] * 2,
            [((chunks, WIDE, WIDE), BF16), ((bands, near_all + 8, LANES), F32)],
            flops=3 * 10**9,
            moved=8 * 2**20,
        )
        received = swapped(send)
        back = call(
            functools.partial(home_slots_kernel, bands),
            "home_slots",
            (residual, left_t, right),
            0,
            [((bands, num_slots + 1, ROWS, LANES), BF16)],
            flops=2 * 10**9,
            moved=4 * 2**20,
        )[0]
        received, back = lax.optimization_barrier((received, back))
        grads = call(reduce_kernel, "reduce", (keep, received), 0, [stamp] * 2, moved=2 * 2**20)
        grads = [stepped(grads[0], "ra", -1), stepped(grads[1], "dec", -1)]
        back_received = swapped(back)
        bands_here = bands if last else 2 * bands
        part = (sources, HALF, LANES) if last else all_stamps
        home_grad, grad_a = call(
            functools.partial(home_gather_kernel, bands, last),
            "home_gather",
            (lists, amps_q, eta_m, morph, back, back_received),
            3,
            [(part, F32), ((bands_here, sources), F32)],
            [((2 * bands, sources, LANES), F32)],
            moved=4 * 2**20,
        )
        grads = [lax.optimization_barrier((home_grad, x))[1] for x in grads]
        grads += [swapped(x) for x in grads]
        outs = [((sources, HALF * LANES) if last else all_stamps, F32)]
        outs += [((bands, 1, sources) if last else (2 * bands, sources), F32)]
        if not last:
            outs += [((bands_here, sources), F32)] + [stamp] * 2
        state, amps, *more = call(
            functools.partial(update_kernel, last),
            "update",
            (places, eta_m, lists, eta_a, hots, amps, grad_a, home_grad, *grads),
            2,
            outs,
            [(part, F32)] if last else (),
            moved=3 * 2**20,
        )
        if not last:
            morph = state
            amps_q, *messages = more
    return state[None, None], amps.reshape(1, 1, bands, sources)


def solution(mesh):
    in_specs = (
        P("ra", "dec", None, None),
        P("ra", "dec", "band", None),
        P("ra", "dec", None, None),
        P("ra", "dec", None),
        P("ra", "dec", None),
        P("band", "ra", None),
        P("ra", "dec", "band", None, None),
    )
    out_specs = (P("ra", "dec", None, "band"), P("ra", "dec", "band", None))
    return jax.shard_map(shards, mesh=mesh, in_specs=in_specs, out_specs=out_specs, check_vma=False)
```

```python
import functools

import jax
import jax.numpy as jnp
from jax import lax
from jax.experimental import pallas as pl
from jax.experimental.pallas import tpu as pltpu
from jax.sharding import PartitionSpec as P

SIDE = 64
KERN = 32
ITERS = 2
CAP = 32
LANES = 128
ROWS = SIDE * SIDE // LANES
HALF = ROWS // 2
WIDE = 4 * SIDE
ORDER, KERNEL_OF, SLOT_OF, COUNT = range(4)
NEAR = 4
GROUP = 4
STRIDE = 8
F32 = jnp.float32
BF16 = jnp.bfloat16


def dot(a, b):
    return lax.dot_general(a, b, (((1,), (0,)), ((), ())), preferred_element_type=F32)


def dot_nt(a, b):
    return lax.dot_general(a, b, (((1,), (1,)), ((), ())), preferred_element_type=F32)


def iota(shape, dim):
    return lax.broadcasted_iota(jnp.int32, shape, dim)


def low_lanes(rows, dtype=F32):
    return (iota((rows, LANES), 1) < SIDE).astype(F32).astype(dtype)


def lane_sums(rows):
    coarse = rows.astype(BF16)
    fine = (rows - coarse.astype(F32)).astype(BF16)
    ones = jnp.ones((8, rows.shape[1]), BF16)
    return dot_nt(ones, coarse) + dot_nt(ones, fine)


def half_masks(rows):
    low = iota((rows, LANES), 1) < SIDE
    return low, jnp.logical_not(low)


def turned(value):
    return pltpu.roll(value, SIDE, 1)


def twofold(packed):
    low, flip = half_masks(ROWS)[0], turned(packed)
    return jnp.concatenate([jnp.where(low, packed, flip), jnp.where(low, flip, packed)], axis=0)


def rounded(stamp):
    if stamp.dtype == F32:
        stamp = jnp.maximum(stamp, 0.0).astype(BF16)
    return stamp.astype(F32)


def half_rows():
    return pl.multiple_of(lax.axis_index("band") * HALF, HALF)


def rows_of(ref):
    return jnp.concatenate([ref[i] for i in range(ref.shape[0])], axis=0)


def by_core(mine, theirs):
    first = lax.axis_index("band") == 0
    return jnp.where(first, mine, theirs), jnp.where(first, theirs, mine)


def lists_kernel(num_slots, slots_ref, hots, places):
    slots = rows_of(slots_ref)
    sources = slots.shape[1]
    valid = (slots < num_slots).astype(F32)
    upper = (iota((sources, sources), 0) <= iota((sources, sources), 1)).astype(F32)
    rank = dot(valid.astype(BF16), upper.astype(BF16))
    place = iota((LANES, sources), 0).astype(F32)
    names = iota((8, sources), 1).astype(F32).astype(BF16)
    for near in range(NEAR):
        row = slice(near + 1, near + 2)
        hot = ((place == rank[row] - 1.0).astype(F32) * valid[row]).astype(BF16)
        hots[near] = hot
        places[near : near + 1, :] = dot_nt(names, hot)[:1].astype(jnp.int32)
        count = jnp.broadcast_to(rank[row, sources - 1 :], (1, LANES))
        places[NEAR + near : NEAR + near + 1, :] = count.astype(jnp.int32)


def write_messages(messages, slots, amps, hots, places, stamp_of):
    first = lax.axis_index("band") == 0
    row = iota((ROWS, slots.shape[1]), 0)
    for turn in range(2):
        near = 2 * turn + lax.axis_index("band")

        def pick(n, carry, near=near, turn=turn):
            messages[turn][n] = stamp_of(places[near, n])
            return carry

        lax.fori_loop(0, CAP, pick, 0, unroll=8)
        slot = jnp.where(first, slots[2 * turn + 1 : 2 * turn + 2], slots[2 * turn + 2 : 2 * turn + 3]).astype(F32)
        meta = jnp.where(row == 0, slot + 1.0, 0.0)
        meta = jnp.where(row == 1, slots[0:1].astype(F32), meta)
        for band in range(amps.shape[0]):
            meta = jnp.where(row == 2 + band, amps[band : band + 1], meta)
        hot = jnp.where(first, hots[2 * turn].astype(F32), hots[2 * turn + 1].astype(F32)).astype(BF16)
        messages[turn][CAP] = dot_nt(meta.astype(BF16), hot).astype(BF16)


def pack_kernel(places, slots_ref, amps_mine, amps_theirs, hots, morph, *out):
    messages, amps_out, amps_q = out[:2], out[2], out[3]
    amps = jnp.concatenate(by_core(rows_of(amps_mine), rows_of(amps_theirs)), axis=0)
    write_messages(messages, rows_of(slots_ref), amps, hots, places, lambda s: morph[s])
    amps_out[...] = amps
    amps_q[...] = amps.astype(BF16).astype(F32)


def order_kernel(num_slots, again, *refs):
    amps, none = refs[NEAR], NEAR * CAP
    bands = amps.shape[0]
    meta = jnp.zeros((ROWS, LANES), F32)
    for turn in range(2):
        pair = by_core(refs[turn][CAP].astype(F32), refs[2 + turn][CAP].astype(F32))
        for core in range(2):
            meta = meta + pltpu.roll(pair[core], (2 * turn + core) * CAP, 1)
    amps[...] = by_core(meta[2 : 2 + bands], meta[2 + bands : 2 + 2 * bands])[0]
    if again:
        return
    plan, slot, kernel = refs[NEAR + 1], meta[0:1], meta[1:2]
    plan[SLOT_OF : SLOT_OF + 1, :LANES] = jnp.maximum(slot - 1.0, 0.0).astype(jnp.int32)
    live = (slot > 0.0).astype(F32)
    hot = (iota((num_slots, none), 0).astype(F32) == kernel).astype(F32) * live
    upto = (iota((none, none), 0) <= iota((none, none), 1)).astype(F32).astype(BF16)
    rank = dot(hot.astype(BF16), upto)
    size = jnp.max(rank, axis=1, keepdims=True)
    filled = ((size.astype(jnp.int32) + (GROUP - 1)) // GROUP).astype(F32)
    before = (iota((num_slots, num_slots), 1) < iota((num_slots, num_slots), 0)).astype(F32).astype(BF16)
    start = dot(before, jnp.broadcast_to(filled, (num_slots, none)).astype(BF16))
    place = jnp.sum(hot * (GROUP * start + rank), axis=0, keepdims=True) - 1.0
    eight = iota((8, none), 0)
    names = jnp.where(eight == 0, iota((8, none), 1).astype(F32) - none, 0.0).astype(BF16)
    for part in range(plan.shape[1] // LANES):
        at = (iota((LANES, none), 0) + part * LANES).astype(F32)
        hit = (at == place).astype(F32) * live
        found = dot_nt(names, hit.astype(BF16))[:1] + none
        plan[ORDER : ORDER + 1, part * LANES : (part + 1) * LANES] = found.astype(jnp.int32)
    chunk = iota((num_slots, LANES), 1).astype(F32)
    row = iota((num_slots, LANES), 0).astype(F32)
    inside = (chunk >= start[:, :LANES]) & (chunk < start[:, :LANES] + filled)
    kernels = jnp.sum(jnp.where(inside, row, 0.0), axis=0, keepdims=True)
    plan[KERNEL_OF : KERNEL_OF + 1, :LANES] = kernels.astype(jnp.int32)
    total = jnp.sum(filled, axis=0, keepdims=True)
    plan[COUNT : COUNT + 1, :LANES] = jnp.broadcast_to(total, (1, LANES)).astype(jnp.int32)


def quarter_start(quarter, held):
    parity, line = lax.axis_index("ra") % 2, lax.axis_index("dec") // (lax.axis_size("dec") // 2)
    shard = parity if quarter % 2 == 0 else 1 - parity
    half = line if quarter < 2 else 1 - line
    return (2 * shard + half) * held


def tables_kernel(bands, earlier, *refs):
    shards, (first_t, left, left_t, right, packed) = refs[: len(refs) - 5 - 4 * earlier], refs[-5:]
    held = shards[0].shape[1]
    for turn, ref in enumerate(shards):
        for band in range(bands):
            for r in range(ROWS):
                rows = pl.ds(turn * held * ROWS + r, held, stride=ROWS)
                packed[band, rows, :] = ref[band, :, r * LANES : (r + 1) * LANES].astype(F32)
    starts = [quarter_start(2 + turn, held) if earlier else turn * held for turn in range(len(shards))]
    if earlier:
        old_first, old_left, old_left_t, old_right = refs[len(shards) : len(shards) + 4]
        for turn in range(2):
            old, new = pl.ds(turn * held, held), pl.ds(quarter_start(turn, held), held)
            first_t[new] = old_first[old]
            right[new] = old_right[old]
            for band in range(bands):
                left[band, new] = old_left[band, old]
                left_t[band, new] = old_left_t[band, old]
    eye = (iota((SIDE, SIDE), 0) == iota((SIDE, SIDE), 1)).astype(F32).astype(BF16)
    row, col = iota((SIDE, SIDE), 0), iota((SIDE, SIDE), 1)
    even = (col == 2 * (row % ROWS) + row // ROWS).astype(F32).astype(BF16)
    even_t = (row == 2 * (col % ROWS) + col // ROWS).astype(F32).astype(BF16)
    rest = [jnp.zeros((SIDE * (4 - bands), SIDE), BF16)] if bands < 4 else []

    def step(place, carry):
        for turn, start in enumerate(starts):
            k = start + place
            at = pl.multiple_of((turn * held + place) * ROWS, ROWS)
            parts = [twofold(packed[band, pl.ds(at, ROWS), :]).astype(BF16) for band in range(bands)]
            lefts = dot_nt(jnp.concatenate([part[:, :SIDE] for part in parts], axis=0), even).astype(BF16)
            natural = []
            for band, part in enumerate(parts):
                rows = slice(band * SIDE, (band + 1) * SIDE)
                left[band, k] = lefts[rows]
                left_t[band, k] = dot_nt(even, part[:, :SIDE]).astype(BF16)
                both = dot(even_t, part).astype(BF16)
                right[k, rows, :] = both
                natural.append(both[:, :SIDE])
            if rest:
                right[k, bands * SIDE :, :] = jnp.zeros((SIDE * (4 - bands), LANES), BF16)
            first_t[k] = dot_nt(eye, jnp.concatenate(natural + rest, axis=0)).astype(BF16)
        return carry

    lax.fori_loop(0, held, step, 0, unroll=min(held, 4))


def make_tables(shards, bands, earlier=()):
    count = sum(x.shape[1] for x in shards)
    total = count + sum(x.shape[0] for x in earlier[:1])
    square = ((bands, total, SIDE, SIDE), BF16)
    return call(
        functools.partial(tables_kernel, bands, bool(earlier)),
        "tables",
        (*shards, *earlier),
        0,
        [((total, SIDE, WIDE), BF16), square, square, ((total, WIDE, LANES), BF16)],
        [((bands, count * ROWS, LANES), F32)],
        flops=2 * 10**9,
        moved=5 * 2**20,
    )


def home_sums_kernel(bands, lists, amps, morph, sums):
    first = lax.axis_index("band") * bands
    sums[...] = jnp.zeros_like(sums)

    def add(s, carry):
        q = lists[0, 0, s]
        stamp = rounded(morph[s])
        for band in range(bands):
            sums[band, q] += amps[first + band, s] * stamp
        return carry

    lax.fori_loop(0, lists.shape[2], add, 0, unroll=4)


def home_forward_kernel(bands, sums, observed, first_t, left, total, inner_all):
    num_slots = total.shape[1]
    masks = half_masks(SIDE)

    def inner_products(q, carry):
        images = []
        for band in range(bands):
            both = sums[band, q]
            images += [both[:, :SIDE], turned(both)[:, :SIDE]]
        inners = dot(jnp.concatenate(images, axis=0).astype(BF16), first_t[q])
        for band in range(bands):
            lanes = slice(band // 2 * LANES, (band // 2 + 1) * LANES)
            inner_all[band, q] = inners[band * SIDE : (band + 1) * SIDE, lanes].astype(BF16)
        return carry

    def slot(q, carry):
        for band in range(bands):
            image = dot(left[band, q], inner_all[band, q]) - twofold(observed[band, q].astype(F32))
            total[band, q] = jnp.where(masks[band % 2], image, 0.0)
        return carry

    lax.fori_loop(0, num_slots, inner_products, 0, unroll=4)
    lax.fori_loop(0, num_slots, slot, 0, unroll=4)


def chunk_reader(bands, plan, amps):
    none = NEAR * CAP

    def read(c):
        members = [plan[ORDER, c * GROUP + u] for u in range(GROUP)]
        held = [jnp.minimum(v, none - 1) for v in members]
        values = [[jnp.where(v < none, amps[band, h], 0.0) for v, h in zip(members, held)] for band in range(bands)]
        return plan[KERNEL_OF, c], members, [plan[SLOT_OF, h] for h in held], values

    return read, (plan[COUNT, 0] + STRIDE - 1) // STRIDE


def forward_kernel(bands, plan, amps, *refs):
    home, first_t, left = refs[NEAR : NEAR + 3]
    residual, inner_all, stamps, *totals = refs[NEAR + 3 :]
    totals = [totals[2 * band : 2 * band + 2] for band in range(bands)]
    num_slots = home.shape[1]
    none = NEAR * CAP
    core = lax.axis_index("band")
    for source, near in enumerate((core, 2 + core, 1 - core, 3 - core)):
        group = pl.ds(near * CAP, CAP)
        even = refs[source][pl.ds(0, CAP)].astype(F32)
        odd = turned(even.reshape(CAP * ROWS, LANES)).reshape(CAP, ROWS, LANES)
        stamps[group, pl.ds(0, ROWS), :] = even.astype(BF16)
        stamps[group, pl.ds(ROWS, ROWS), :] = odd.astype(BF16)
    stamps[none] = jnp.zeros((SIDE, LANES), BF16)
    for band in range(bands):
        totals[band][band % 2][...] = home[band]
        totals[band][1 - band % 2][...] = jnp.zeros_like(home[band])
    masks, row_masks = half_masks(SIDE), half_masks(1)
    read, rounds = chunk_reader(bands, plan, amps)

    def inner_products(turn, carry):
        for c in [STRIDE * turn + i for i in range(STRIDE)]:
            k, members, _, _ = read(c)
            stack = jnp.concatenate([stamps[v] for v in members], axis=0)
            inners = dot(stack[:, :SIDE], first_t[k])
            for band in range(bands):
                lanes = slice(band // 2 * LANES, (band // 2 + 1) * LANES)
                pairs = []
                for u in range(0, GROUP, 2):
                    x = inners[u * SIDE : (u + 1) * SIDE, lanes]
                    y = inners[(u + 1) * SIDE : (u + 2) * SIDE, lanes]
                    x, y = (x, turned(y)) if band % 2 == 0 else (turned(x), y)
                    pairs.append(jnp.where(masks[0], x, y))
                inner_all[c, band] = jnp.concatenate(pairs, axis=1).astype(BF16)
        return carry

    def images(turn, carry):
        for c in [STRIDE * turn + i for i in range(STRIDE)]:
            k, _, slots, values = read(c)
            for band in range(bands):
                image = dot(left[band, k], inner_all[c, band])
                for u in range(0, GROUP, 2):
                    lanes = slice(u // 2 * LANES, (u // 2 + 1) * LANES)
                    scale = jnp.where(row_masks[0], values[band][u], values[band][u + 1])
                    pair = image[:, lanes] * scale
                    for part in (0, 1):
                        totals[band][part][slots[u + part]] += pair
        return carry

    lax.fori_loop(0, rounds, inner_products, 0)
    lax.fori_loop(0, rounds, images, 0)

    def slot(q, carry):
        for band in range(bands):
            model = jnp.where(masks[0], totals[band][0][q], totals[band][1][q])
            residual[band, q] = (model + turned(model)).astype(BF16)
        return carry

    lax.fori_loop(0, num_slots, slot, 0, unroll=8)


def backward_kernel(bands, plan, amps, *refs):
    residual, inner_all, left_t, right, keep, send, stacks, sums = refs
    none = NEAR * CAP
    sums[...] = jnp.zeros_like(sums)
    keep[...] = jnp.zeros_like(keep)
    send[...] = jnp.zeros_like(send)
    masks, row_masks, packed_low = half_masks(SIDE), half_masks(1), half_masks(ROWS)[0]
    read, rounds = chunk_reader(bands, plan, amps)
    spare = none // 2
    core = lax.axis_index("band")

    def outer_products(turn, carry):
        for c in [STRIDE * turn + i for i in range(STRIDE)]:
            k, members, slots, values = read(c)
            outers = []
            for band in range(bands):
                pairs = [
                    jnp.where(masks[0], residual[band, slots[u]], residual[band, slots[u + 1]])
                    for u in range(0, GROUP, 2)
                ]
                outer = dot(left_t[band, k], jnp.concatenate(pairs, axis=1))
                along = jnp.sum(inner_all[c, band].astype(F32) * outer, axis=0, keepdims=True)
                scaled = []
                for u in range(0, GROUP, 2):
                    lanes = slice(u // 2 * LANES, (u // 2 + 1) * LANES)
                    for part in (0, 1):
                        row = jnp.where(row_masks[part], along[:, lanes], 0.0)
                        sums[band, pl.ds(members[u + part], 1), :] = row
                    scale = jnp.where(row_masks[0], values[band][u], values[band][u + 1])
                    scaled.append(outer[:, lanes] * scale)
                outers.append(scaled)
            outers += [[jnp.zeros((SIDE, LANES), F32)] * (GROUP // 2)] * (4 - bands)
            for pair in range(GROUP // 2):
                b0, b1, b2, b3 = [outers[band][pair] for band in range(4)]
                if bands > 3:
                    last = [jnp.where(masks[0], b2, turned(b3)), jnp.where(masks[0], turned(b2), b3)]
                else:
                    last = [b2, turned(b2)]
                first = [jnp.where(masks[0], b0, turned(b1)), jnp.where(masks[0], turned(b0), b1)]
                for part in (0, 1):
                    rows = slice((2 * pair + part) * SIDE, (2 * pair + part + 1) * SIDE)
                    stacks[c, rows, :] = jnp.concatenate([first[part], last[part]], axis=1).astype(BF16)
        return carry

    def gradients(turn, carry):
        for c in [STRIDE * turn + i for i in range(STRIDE)]:
            k, members, _, _ = read(c)
            grads = dot(stacks[c], right[k])
            for u, v in enumerate(members):
                top = grads[u * SIDE : u * SIDE + ROWS]
                low = grads[u * SIDE + ROWS : (u + 1) * SIDE]
                stamp = jnp.where(packed_low, top, low).astype(BF16)
                side, place = v // CAP % 2, v // (2 * CAP) * CAP + v % CAP
                keep[jnp.where(side == core, place, spare)] = stamp
                send[jnp.where(side == 1 - core, place, spare)] = stamp
        return carry

    lax.fori_loop(0, rounds, outer_products, 0)
    lax.fori_loop(0, rounds, gradients, 0)
    meta = amp_rows([lane_sums(sums[band, :none, :]) for band in range(bands)])
    keep[spare] = meta
    send[spare] = meta


def home_slots_kernel(bands, residual, left_t, right, back):
    num_slots = residual.shape[1]
    back[:, num_slots] = jnp.zeros((bands, ROWS, LANES), BF16)
    packed_low = half_masks(ROWS)[0]

    def slot(q, carry):
        for band in range(bands):
            outer = dot(left_t[band, q], residual[band, q]).astype(BF16)
            grad = dot(outer[:, :SIDE], right[q, band * SIDE : (band + 1) * SIDE, :])
            back[band, q] = jnp.where(packed_low, grad[:ROWS], grad[ROWS:]).astype(BF16)
        return carry

    lax.fori_loop(0, num_slots, slot, 0, unroll=8)


def home_gather_kernel(bands, last, lists, amps, eta_m, morph, back, received, keep, grad_a, sums):
    core = lax.axis_index("band")
    mine = pl.ds(half_rows(), HALF) if last else pl.ds(0, ROWS)

    def gather(s, carry):
        q = lists[0, 0, s]
        stamp = rounded(morph[s])
        grad = jnp.zeros((HALF if last else ROWS, LANES), F32)
        for ref, side in ((back, core), (received, 1 - core)):
            for band in range(bands):
                amp = amps[side * bands + band, s]
                if last:
                    grad = grad + amp * ref[band, q, mine, :].astype(F32)
                    if ref is received:
                        continue
                seen = ref[band, q].astype(F32)
                if not last:
                    grad = grad + amp * seen
                along = jnp.sum(seen * stamp, axis=0, keepdims=True)
                sums[side * bands + band, pl.ds(s, 1), :] = along
        keep[s] = jnp.maximum(morph[s, mine, :].astype(F32), 0.0) - eta_m[0, s] * grad
        return carry

    lax.fori_loop(0, lists.shape[2], gather, 0, unroll=4)
    for band in range(grad_a.shape[0]):
        rows = sums[core * bands + band] if last else sums[band]
        grad_a[band : band + 1, :] = lane_sums(rows)[:1]


def amp_rows(sums):
    eight = iota((8, LANES), 0)
    total = jnp.zeros((8, LANES), F32)
    for band, row in enumerate(sums):
        total = jnp.where(eight == band, row, total)
    coarse = total.astype(BF16).astype(F32)
    return jnp.concatenate([coarse, total - coarse, jnp.zeros((HALF, LANES), F32)], axis=0).astype(BF16)


def reduce_kernel(keep, received, *messages):
    for turn in range(2):
        part = pl.ds(turn * CAP, CAP)
        total = keep[part].astype(F32) + received[part].astype(F32)
        messages[turn][pl.ds(0, CAP)] = total.astype(BF16)
        pair = by_core(keep[2 * CAP].astype(F32), received[2 * CAP].astype(F32))
        meta = jnp.concatenate([pair[0][:HALF], pair[1][:HALF]], axis=0)
        messages[turn][CAP] = meta.astype(BF16)


def update_kernel(last, places, eta_m, slots_ref, eta_a, hots, amps_ref, grad_a, home, *refs):
    grads, out = refs[:NEAR], refs[NEAR:]
    state, amps_out, work = out[0], out[1], out[-1] if last else out[0]
    core = lax.axis_index("band")
    mine = pl.ds(half_rows(), HALF) if last else pl.ds(0, ROWS)
    nears = (core, 2 + core, 1 - core, 3 - core)
    lane = iota((ROWS, LANES), 1) // CAP
    meta = jnp.zeros((ROWS, LANES), F32)
    for ref, near in zip(grads, nears):
        meta = jnp.where(lane == near, ref[CAP].astype(F32), meta)
    all_hots = jnp.concatenate([hots[near, :CAP] for near in range(NEAR)], axis=0)
    from_near = dot(meta.astype(BF16), all_hots)
    bands = amps_ref.shape[0] // 2
    sides = [from_near[r : r + bands] + from_near[r + 8 : r + 8 + bands] for r in (0, HALF)]
    if last:
        amps = by_core(amps_ref[:bands], amps_ref[bands:])[0]
        total = grad_a[...] + by_core(sides[0], sides[1])[0]
    else:
        amps = amps_ref[...]
        total = grad_a[...] + jnp.concatenate(sides, axis=0)
    amps = jnp.maximum(amps - eta_a[...] * total, 0.0)
    if last:
        for band in range(bands):
            amps_out[band] = amps[band : band + 1]
    else:
        amps_out[...] = amps
    work[...] = home[...]
    for ref, near in zip(grads, nears):

        def add(n, carry, ref=ref, near=near):
            s = places[near, n]
            work[s] -= eta_m[0, s] * ref[n, mine, :].astype(F32)
            return carry

        lax.fori_loop(0, CAP, add, 0, unroll=8)

    if last:
        for r in range(HALF):
            state[:, r * LANES : (r + 1) * LANES] = jnp.maximum(work[:, r, :], 0.0)
        return
    amps_q, messages = out[2], out[3:5]
    amps_q[...] = amps.astype(BF16).astype(F32)

    def stamp_of(s):
        return jnp.maximum(state[s], 0.0).astype(BF16)

    write_messages(messages, rows_of(slots_ref), amps, hots, places, stamp_of)


def call(body, name, operands, scalars, outs, scratch=(), flops=0, moved=0):
    vmem, smem = pl.BlockSpec(memory_space=pltpu.VMEM), pl.BlockSpec(memory_space=pltpu.SMEM)
    return pl.pallas_call(
        body,
        out_shape=[jax.ShapeDtypeStruct(shape, dtype) for shape, dtype in outs],
        in_specs=[smem if i < scalars else vmem for i in range(len(operands))],
        out_specs=[vmem] * len(outs),
        scratch_shapes=[pltpu.VMEM(shape, dtype) for shape, dtype in scratch],
        compiler_params=pltpu.CompilerParams(vmem_limit_bytes=40 * 2**20),
        cost_estimate=pl.CostEstimate(flops=flops, bytes_accessed=moved, transcendentals=0),
        name=name,
    )(*operands)


def stepped(value, axis, step):
    shape = [lax.axis_size(name) for name in ("ra", "dec", "band")]

    def device(ra, dec, band):
        return (ra * shape[1] + dec) * shape[2] + band

    pairs = []
    for ra in range(shape[0]):
        for dec in range(shape[1]):
            for band, by in ((0, step), (1, -step)):
                if axis == "ra":
                    pairs.append((device(ra, dec, band), device((ra + by) % shape[0], dec, band)))
                elif 0 <= dec + by < shape[1]:
                    pairs.append((device(ra, dec, band), device(ra, dec + by, band)))
    return lax.ppermute(value, ("ra", "dec", "band"), pairs)


def swapped(value):
    return lax.ppermute(value, "band", [(0, 1), (1, 0)])


def all_tables(psf, num_slots, messages, sums):
    bands, held = psf.shape[:2]
    lines = lax.axis_size("dec")
    if lax.axis_size("ra") == 4 and 2 * held == num_slots and held % 2 == 0 and lines % 2 == 0:
        across = [(i, (i + lines // 2) % lines) for i in range(lines)]
        along = [(0, 1), (1, 0), (2, 3), (3, 2)]
        mine = jnp.where(lax.axis_index("dec") < lines // 2, psf[:, : held // 2], psf[:, held // 2 :])
        far = lax.ppermute(mine, "ra", [(0, 2), (1, 3)])
        far, sums = lax.optimization_barrier((far, sums))
        here = jnp.where(lax.axis_index("ra") < 2, mine, far)
        here, *messages = lax.optimization_barrier((here, *messages))
        near = lax.ppermute(here, "ra", along)
        halves = make_tables((here, near), bands)
        others = (lax.ppermute(here, "dec", across), lax.ppermute(near, "dec", across))
        return make_tables(others, bands, halves), messages, sums
    return make_tables((lax.all_gather(psf, "ra", axis=1, tiled=True)[:, :num_slots],), bands), messages, sums


def shards(morphology, sed_amps, slot_lists, morph_step, sed_step, psf_kernels, observed):
    bands, num_slots, sources = sed_amps.shape[2], observed.shape[3], morphology.shape[2]
    lists, amps = slot_lists[0, 0][:, None, :], sed_amps[0, 0][:, None, :]
    eta_m, eta_a = morph_step[0], sed_step[0]
    full = morphology[0, 0].reshape(sources, ROWS, LANES)
    seen = observed[0, 0].reshape(bands, num_slots, ROWS, LANES)
    stamp = ((CAP + 1, ROWS, LANES), BF16)
    all_stamps = (sources, ROWS, LANES)
    near_all = NEAR * CAP
    chunks = -(-(near_all // GROUP + num_slots) // STRIDE) * STRIDE
    amps_theirs = swapped(amps)
    hots, places = call(
        functools.partial(lists_kernel, num_slots),
        "lists",
        (lists,),
        0,
        [
            ((NEAR, LANES, sources), BF16),
            ((2 * NEAR, LANES), jnp.int32),
        ],
        moved=2**20,
    )
    *messages, amps, amps_q = call(
        pack_kernel,
        "pack",
        (places, lists, amps, amps_theirs, hots, full),
        1,
        [stamp] * 2 + [((2 * bands, sources), F32)] * 2,
        moved=2**20,
    )
    def home_sums(amps_q, morph):
        return call(
            functools.partial(home_sums_kernel, bands),
            "home_sums",
            (lists, amps_q, morph),
            2,
            [((bands, num_slots + 1, ROWS, LANES), F32)],
            moved=4 * 2**20,
        )[0]

    sums = home_sums(amps_q, full)
    tables, messages, sums = all_tables(psf_kernels, num_slots, messages, sums)
    first_t, left, left_t, right = tables
    morph, plan = full, None
    for sweep in range(ITERS):
        last = sweep == ITERS - 1
        own = [stepped(messages[0], "ra", 1), stepped(messages[1], "dec", 1)]
        if sweep == 0:
            left, *own = lax.optimization_barrier((left, *own))
        else:
            sums = home_sums(amps_q, morph)
        home = call(
            functools.partial(home_forward_kernel, bands),
            "home_forward",
            (sums, seen, first_t, left),
            0,
            [((bands, num_slots, SIDE, LANES), F32)],
            [((bands, num_slots, SIDE, LANES), BF16)],
            flops=2 * 10**9,
            moved=4 * 2**20,
        )[0]
        if sweep > 0:
            own = [lax.optimization_barrier((home, x))[1] for x in own]
        other = [swapped(x) for x in own]
        amps_near, *new_plan = call(
            functools.partial(order_kernel, num_slots, sweep > 0),
            "order",
            (*own, *other),
            0,
            [((bands, LANES), F32)] + [((8, -(-chunks * GROUP // LANES) * LANES), jnp.int32)] * (sweep == 0),
            moved=2**20,
        )
        plan = new_plan[0] if new_plan else plan
        residual, inner_all = call(
            functools.partial(forward_kernel, bands),
            "forward",
            (plan, amps_near, *own, *other, home, first_t, left),
            2,
            [
                ((bands, num_slots, SIDE, LANES), BF16),
                ((chunks, bands, SIDE, WIDE), BF16),
            ],
            [((near_all + 1, SIDE, LANES), BF16)] + [((num_slots, SIDE, LANES), F32)] * (2 * bands),
            flops=3 * 10**9,
            moved=8 * 2**20,
        )
        half_of_near = ((near_all // 2 + 1, ROWS, LANES), BF16)
        keep, send = call(
            functools.partial(backward_kernel, bands),
            "backward",
            (plan, amps_near, residual, inner_all, left_t, right),
            2,
            [half_of_near] * 2,
            [((chunks, WIDE, WIDE), BF16), ((bands, near_all + 8, LANES), F32)],
            flops=3 * 10**9,
            moved=8 * 2**20,
        )
        received = swapped(send)
        back = call(
            functools.partial(home_slots_kernel, bands),
            "home_slots",
            (residual, left_t, right),
            0,
            [((bands, num_slots + 1, ROWS, LANES), BF16)],
            flops=2 * 10**9,
            moved=4 * 2**20,
        )[0]
        received, back = lax.optimization_barrier((received, back))
        grads = call(reduce_kernel, "reduce", (keep, received), 0, [stamp] * 2, moved=2 * 2**20)
        grads = [stepped(grads[0], "ra", -1), stepped(grads[1], "dec", -1)]
        back_received = swapped(back)
        bands_here = bands if last else 2 * bands
        part = (sources, HALF, LANES) if last else all_stamps
        home_grad, grad_a = call(
            functools.partial(home_gather_kernel, bands, last),
            "home_gather",
            (lists, amps_q, eta_m, morph, back, back_received),
            3,
            [(part, F32), ((bands_here, sources), F32)],
            [((2 * bands, sources, LANES), F32)],
            moved=4 * 2**20,
        )
        grads = [lax.optimization_barrier((home_grad, x))[1] for x in grads]
        grads += [swapped(x) for x in grads]
        outs = [((sources, HALF * LANES) if last else all_stamps, F32)]
        outs += [((bands, 1, sources) if last else (2 * bands, sources), F32)]
        if not last:
            outs += [((bands_here, sources), F32)] + [stamp] * 2
        state, amps, *more = call(
            functools.partial(update_kernel, last),
            "update",
            (places, eta_m, lists, eta_a, hots, amps, grad_a, home_grad, *grads),
            2,
            outs,
            [(part, F32)] if last else (),
            moved=3 * 2**20,
        )
        if not last:
            morph = state
            amps_q, *messages = more
    return state[None, None], amps.reshape(1, 1, bands, sources)


def solution(mesh):
    in_specs = (
        P("ra", "dec", None, None),
        P("ra", "dec", "band", None),
        P("ra", "dec", None, None),
        P("ra", "dec", None),
        P("ra", "dec", None),
        P("band", "ra", None),
        P("ra", "dec", "band", None, None),
    )
    out_specs = (P("ra", "dec", None, "band"), P("ra", "dec", "band", None))
    return jax.shard_map(shards, mesh=mesh, in_specs=in_specs, out_specs=out_specs, check_vma=False)
```

```python
import functools

import jax
import jax.numpy as jnp
from jax import lax
from jax.experimental import pallas as pl
from jax.experimental.pallas import tpu as pltpu
from jax.sharding import PartitionSpec as P

SIDE = 64
KERN = 32
ITERS = 2
CAP = 32
LANES = 128
ROWS = SIDE * SIDE // LANES
HALF = ROWS // 2
WIDE = 4 * SIDE
ORDER, KERNEL_OF, SLOT_OF, COUNT = range(4)
NEAR = 4
GROUP = 4
STRIDE = 8
F32 = jnp.float32
BF16 = jnp.bfloat16


def dot(a, b):
    return lax.dot_general(a, b, (((1,), (0,)), ((), ())), preferred_element_type=F32)


def dot_nt(a, b):
    return lax.dot_general(a, b, (((1,), (1,)), ((), ())), preferred_element_type=F32)


def iota(shape, dim):
    return lax.broadcasted_iota(jnp.int32, shape, dim)


def low_lanes(rows, dtype=F32):
    return (iota((rows, LANES), 1) < SIDE).astype(F32).astype(dtype)


def lane_sums(rows):
    coarse = rows.astype(BF16)
    fine = (rows - coarse.astype(F32)).astype(BF16)
    ones = jnp.ones((8, rows.shape[1]), BF16)
    return dot_nt(ones, coarse) + dot_nt(ones, fine)


def half_masks(rows):
    low = iota((rows, LANES), 1) < SIDE
    return low, jnp.logical_not(low)


def turned(value):
    return pltpu.roll(value, SIDE, 1)


def twofold(packed):
    low, flip = half_masks(ROWS)[0], turned(packed)
    return jnp.concatenate([jnp.where(low, packed, flip), jnp.where(low, flip, packed)], axis=0)


def rounded(stamp):
    if stamp.dtype == F32:
        stamp = jnp.maximum(stamp, 0.0).astype(BF16)
    return stamp.astype(F32)


def half_rows():
    return pl.multiple_of(lax.axis_index("band") * HALF, HALF)


def rows_of(ref):
    return jnp.concatenate([ref[i] for i in range(ref.shape[0])], axis=0)


def by_core(mine, theirs):
    first = lax.axis_index("band") == 0
    return jnp.where(first, mine, theirs), jnp.where(first, theirs, mine)


def lists_kernel(num_slots, slots_ref, hots, places):
    slots = rows_of(slots_ref)
    sources = slots.shape[1]
    valid = (slots < num_slots).astype(F32)
    upper = (iota((sources, sources), 0) <= iota((sources, sources), 1)).astype(F32)
    rank = dot(valid.astype(BF16), upper.astype(BF16))
    place = iota((LANES, sources), 0).astype(F32)
    names = iota((8, sources), 1).astype(F32).astype(BF16)
    for near in range(NEAR):
        row = slice(near + 1, near + 2)
        hot = ((place == rank[row] - 1.0).astype(F32) * valid[row]).astype(BF16)
        hots[near] = hot
        places[near : near + 1, :] = dot_nt(names, hot)[:1].astype(jnp.int32)
        count = jnp.broadcast_to(rank[row, sources - 1 :], (1, LANES))
        places[NEAR + near : NEAR + near + 1, :] = count.astype(jnp.int32)


def write_messages(messages, slots, amps, hots, places, stamp_of):
    first = lax.axis_index("band") == 0
    row = iota((ROWS, slots.shape[1]), 0)
    for turn in range(2):
        near = 2 * turn + lax.axis_index("band")

        def pick(n, carry, near=near, turn=turn):
            messages[turn][n] = stamp_of(places[near, n])
            return carry

        lax.fori_loop(0, CAP, pick, 0, unroll=8)
        slot = jnp.where(first, slots[2 * turn + 1 : 2 * turn + 2], slots[2 * turn + 2 : 2 * turn + 3]).astype(F32)
        meta = jnp.where(row == 0, slot + 1.0, 0.0)
        meta = jnp.where(row == 1, slots[0:1].astype(F32), meta)
        for band in range(amps.shape[0]):
            meta = jnp.where(row == 2 + band, amps[band : band + 1], meta)
        hot = jnp.where(first, hots[2 * turn].astype(F32), hots[2 * turn + 1].astype(F32)).astype(BF16)
        messages[turn][CAP] = dot_nt(meta.astype(BF16), hot).astype(BF16)


def pack_kernel(places, slots_ref, amps_mine, amps_theirs, hots, morph, *out):
    messages, amps_out, amps_q = out[:2], out[2], out[3]
    amps = jnp.concatenate(by_core(rows_of(amps_mine), rows_of(amps_theirs)), axis=0)
    write_messages(messages, rows_of(slots_ref), amps, hots, places, lambda s: morph[s])
    amps_out[...] = amps
    amps_q[...] = amps.astype(BF16).astype(F32)


def order_kernel(num_slots, again, *refs):
    amps, none = refs[NEAR], NEAR * CAP
    bands = amps.shape[0]
    meta = jnp.zeros((ROWS, LANES), F32)
    for turn in range(2):
        pair = by_core(refs[turn][CAP].astype(F32), refs[2 + turn][CAP].astype(F32))
        for core in range(2):
            meta = meta + pltpu.roll(pair[core], (2 * turn + core) * CAP, 1)
    amps[...] = by_core(meta[2 : 2 + bands], meta[2 + bands : 2 + 2 * bands])[0]
    if again:
        return
    plan, slot, kernel = refs[NEAR + 1], meta[0:1], meta[1:2]
    plan[SLOT_OF : SLOT_OF + 1, :LANES] = jnp.maximum(slot - 1.0, 0.0).astype(jnp.int32)
    live = (slot > 0.0).astype(F32)
    hot = (iota((num_slots, none), 0).astype(F32) == kernel).astype(F32) * live
    upto = (iota((none, none), 0) <= iota((none, none), 1)).astype(F32).astype(BF16)
    rank = dot(hot.astype(BF16), upto)
    size = jnp.max(rank, axis=1, keepdims=True)
    filled = ((size.astype(jnp.int32) + (GROUP - 1)) // GROUP).astype(F32)
    before = (iota((num_slots, num_slots), 1) < iota((num_slots, num_slots), 0)).astype(F32).astype(BF16)
    start = dot(before, jnp.broadcast_to(filled, (num_slots, none)).astype(BF16))
    place = jnp.sum(hot * (GROUP * start + rank), axis=0, keepdims=True) - 1.0
    eight = iota((8, none), 0)
    names = jnp.where(eight == 0, iota((8, none), 1).astype(F32) - none, 0.0).astype(BF16)
    for part in range(plan.shape[1] // LANES):
        at = (iota((LANES, none), 0) + part * LANES).astype(F32)
        hit = (at == place).astype(F32) * live
        found = dot_nt(names, hit.astype(BF16))[:1] + none
        plan[ORDER : ORDER + 1, part * LANES : (part + 1) * LANES] = found.astype(jnp.int32)
    chunk = iota((num_slots, LANES), 1).astype(F32)
    row = iota((num_slots, LANES), 0).astype(F32)
    inside = (chunk >= start[:, :LANES]) & (chunk < start[:, :LANES] + filled)
    kernels = jnp.sum(jnp.where(inside, row, 0.0), axis=0, keepdims=True)
    plan[KERNEL_OF : KERNEL_OF + 1, :LANES] = kernels.astype(jnp.int32)
    total = jnp.sum(filled, axis=0, keepdims=True)
    plan[COUNT : COUNT + 1, :LANES] = jnp.broadcast_to(total, (1, LANES)).astype(jnp.int32)


def quarter_start(quarter, held):
    parity, line = lax.axis_index("ra") % 2, lax.axis_index("dec") // (lax.axis_size("dec") // 2)
    shard = parity if quarter % 2 == 0 else 1 - parity
    half = line if quarter < 2 else 1 - line
    return (2 * shard + half) * held


def tables_kernel(bands, earlier, *refs):
    shards, (first_t, left, left_t, right, packed) = refs[: len(refs) - 5 - 4 * earlier], refs[-5:]
    held = shards[0].shape[1]
    for turn, ref in enumerate(shards):
        for band in range(bands):
            for r in range(ROWS):
                rows = pl.ds(turn * held * ROWS + r, held, stride=ROWS)
                packed[band, rows, :] = ref[band, :, r * LANES : (r + 1) * LANES].astype(F32)
    starts = [quarter_start(2 + turn, held) if earlier else turn * held for turn in range(len(shards))]
    if earlier:
        old_first, old_left, old_left_t, old_right = refs[len(shards) : len(shards) + 4]
        for turn in range(2):
            old, new = pl.ds(turn * held, held), pl.ds(quarter_start(turn, held), held)
            first_t[new] = old_first[old]
            right[new] = old_right[old]
            for band in range(bands):
                left[band, new] = old_left[band, old]
                left_t[band, new] = old_left_t[band, old]
    eye = (iota((SIDE, SIDE), 0) == iota((SIDE, SIDE), 1)).astype(F32).astype(BF16)
    row, col = iota((SIDE, SIDE), 0), iota((SIDE, SIDE), 1)
    even = (col == 2 * (row % ROWS) + row // ROWS).astype(F32).astype(BF16)
    even_t = (row == 2 * (col % ROWS) + col // ROWS).astype(F32).astype(BF16)
    rest = [jnp.zeros((SIDE * (4 - bands), SIDE), BF16)] if bands < 4 else []

    def step(place, carry):
        for turn, start in enumerate(starts):
            k = start + place
            at = pl.multiple_of((turn * held + place) * ROWS, ROWS)
            parts = [twofold(packed[band, pl.ds(at, ROWS), :]).astype(BF16) for band in range(bands)]
            lefts = dot_nt(jnp.concatenate([part[:, :SIDE] for part in parts], axis=0), even).astype(BF16)
            natural = []
            for band, part in enumerate(parts):
                rows = slice(band * SIDE, (band + 1) * SIDE)
                left[band, k] = lefts[rows]
                left_t[band, k] = dot_nt(even, part[:, :SIDE]).astype(BF16)
                both = dot(even_t, part).astype(BF16)
                right[k, rows, :] = both
                natural.append(both[:, :SIDE])
            if rest:
                right[k, bands * SIDE :, :] = jnp.zeros((SIDE * (4 - bands), LANES), BF16)
            first_t[k] = dot_nt(eye, jnp.concatenate(natural + rest, axis=0)).astype(BF16)
        return carry

    lax.fori_loop(0, held, step, 0, unroll=min(held, 4))


def make_tables(shards, bands, earlier=()):
    count = sum(x.shape[1] for x in shards)
    total = count + sum(x.shape[0] for x in earlier[:1])
    square = ((bands, total, SIDE, SIDE), BF16)
    return call(
        functools.partial(tables_kernel, bands, bool(earlier)),
        "tables",
        (*shards, *earlier),
        0,
        [((total, SIDE, WIDE), BF16), square, square, ((total, WIDE, LANES), BF16)],
        [((bands, count * ROWS, LANES), F32)],
        flops=2 * 10**9,
        moved=5 * 2**20,
    )


def home_sums_kernel(bands, lists, amps, morph, sums):
    first = lax.axis_index("band") * bands
    sums[...] = jnp.zeros_like(sums)

    def add(s, carry):
        q = lists[0, 0, s]
        stamp = rounded(morph[s])
        for band in range(bands):
            sums[band, q] += amps[first + band, s] * stamp
        return carry

    lax.fori_loop(0, lists.shape[2], add, 0, unroll=4)


def home_forward_kernel(bands, sums, observed, first_t, left, total, inner_all):
    num_slots = total.shape[1]
    masks = half_masks(SIDE)

    def inner_products(q, carry):
        images = []
        for band in range(bands):
            both = sums[band, q]
            images += [both[:, :SIDE], turned(both)[:, :SIDE]]
        inners = dot(jnp.concatenate(images, axis=0).astype(BF16), first_t[q])
        for band in range(bands):
            lanes = slice(band // 2 * LANES, (band // 2 + 1) * LANES)
            inner_all[band, q] = inners[band * SIDE : (band + 1) * SIDE, lanes].astype(BF16)
        return carry

    def slot(q, carry):
        for band in range(bands):
            image = dot(left[band, q], inner_all[band, q]) - twofold(observed[band, q].astype(F32))
            total[band, q] = jnp.where(masks[band % 2], image, 0.0)
        return carry

    lax.fori_loop(0, num_slots, inner_products, 0, unroll=4)
    lax.fori_loop(0, num_slots, slot, 0, unroll=4)


def chunk_reader(bands, plan, amps):
    none = NEAR * CAP

    def read(c):
        members = [plan[ORDER, c * GROUP + u] for u in range(GROUP)]
        held = [jnp.minimum(v, none - 1) for v in members]
        values = [[jnp.where(v < none, amps[band, h], 0.0) for v, h in zip(members, held)] for band in range(bands)]
        return plan[KERNEL_OF, c], members, [plan[SLOT_OF, h] for h in held], values

    return read, (plan[COUNT, 0] + STRIDE - 1) // STRIDE


def forward_kernel(bands, plan, amps, *refs):
    home, first_t, left = refs[NEAR : NEAR + 3]
    residual, inner_all, stamps, *totals = refs[NEAR + 3 :]
    totals = [totals[2 * band : 2 * band + 2] for band in range(bands)]
    num_slots = home.shape[1]
    none = NEAR * CAP
    core = lax.axis_index("band")
    for source, near in enumerate((core, 2 + core, 1 - core, 3 - core)):
        group = pl.ds(near * CAP, CAP)
        even = refs[source][pl.ds(0, CAP)].astype(F32)
        odd = turned(even.reshape(CAP * ROWS, LANES)).reshape(CAP, ROWS, LANES)
        stamps[group, pl.ds(0, ROWS), :] = even.astype(BF16)
        stamps[group, pl.ds(ROWS, ROWS), :] = odd.astype(BF16)
    stamps[none] = jnp.zeros((SIDE, LANES), BF16)
    for band in range(bands):
        totals[band][band % 2][...] = home[band]
        totals[band][1 - band % 2][...] = jnp.zeros_like(home[band])
    masks, row_masks = half_masks(SIDE), half_masks(1)
    read, rounds = chunk_reader(bands, plan, amps)

    def inner_products(turn, carry):
        for c in [STRIDE * turn + i for i in range(STRIDE)]:
            k, members, _, _ = read(c)
            stack = jnp.concatenate([stamps[v] for v in members], axis=0)
            inners = dot(stack[:, :SIDE], first_t[k])
            for band in range(bands):
                lanes = slice(band // 2 * LANES, (band // 2 + 1) * LANES)
                pairs = []
                for u in range(0, GROUP, 2):
                    x = inners[u * SIDE : (u + 1) * SIDE, lanes]
                    y = inners[(u + 1) * SIDE : (u + 2) * SIDE, lanes]
                    x, y = (x, turned(y)) if band % 2 == 0 else (turned(x), y)
                    pairs.append(jnp.where(masks[0], x, y))
                inner_all[c, band] = jnp.concatenate(pairs, axis=1).astype(BF16)
        return carry

    def images(turn, carry):
        for c in [STRIDE * turn + i for i in range(STRIDE)]:
            k, _, slots, values = read(c)
            for band in range(bands):
                image = dot(left[band, k], inner_all[c, band])
                for u in range(0, GROUP, 2):
                    lanes = slice(u // 2 * LANES, (u // 2 + 1) * LANES)
                    scale = jnp.where(row_masks[0], values[band][u], values[band][u + 1])
                    pair = image[:, lanes] * scale
                    for part in (0, 1):
                        totals[band][part][slots[u + part]] += pair
        return carry

    lax.fori_loop(0, rounds, inner_products, 0)
    lax.fori_loop(0, rounds, images, 0)

    def slot(q, carry):
        for band in range(bands):
            model = jnp.where(masks[0], totals[band][0][q], totals[band][1][q])
            residual[band, q] = (model + turned(model)).astype(BF16)
        return carry

    lax.fori_loop(0, num_slots, slot, 0, unroll=8)


def backward_kernel(bands, plan, amps, *refs):
    residual, inner_all, left_t, right, keep, send, stacks, sums = refs
    none = NEAR * CAP
    sums[...] = jnp.zeros_like(sums)
    keep[...] = jnp.zeros_like(keep)
    send[...] = jnp.zeros_like(send)
    masks, row_masks, packed_low = half_masks(SIDE), half_masks(1), half_masks(ROWS)[0]
    read, rounds = chunk_reader(bands, plan, amps)
    spare = none // 2
    core = lax.axis_index("band")

    def outer_products(turn, carry):
        for c in [STRIDE * turn + i for i in range(STRIDE)]:
            k, members, slots, values = read(c)
            outers = []
            for band in range(bands):
                pairs = [
                    jnp.where(masks[0], residual[band, slots[u]], residual[band, slots[u + 1]])
                    for u in range(0, GROUP, 2)
                ]
                outer = dot(left_t[band, k], jnp.concatenate(pairs, axis=1))
                along = jnp.sum(inner_all[c, band].astype(F32) * outer, axis=0, keepdims=True)
                scaled = []
                for u in range(0, GROUP, 2):
                    lanes = slice(u // 2 * LANES, (u // 2 + 1) * LANES)
                    for part in (0, 1):
                        row = jnp.where(row_masks[part], along[:, lanes], 0.0)
                        sums[band, pl.ds(members[u + part], 1), :] = row
                    scale = jnp.where(row_masks[0], values[band][u], values[band][u + 1])
                    scaled.append(outer[:, lanes] * scale)
                outers.append(scaled)
            outers += [[jnp.zeros((SIDE, LANES), F32)] * (GROUP // 2)] * (4 - bands)
            for pair in range(GROUP // 2):
                b0, b1, b2, b3 = [outers[band][pair] for band in range(4)]
                if bands > 3:
                    last = [jnp.where(masks[0], b2, turned(b3)), jnp.where(masks[0], turned(b2), b3)]
                else:
                    last = [b2, turned(b2)]
                first = [jnp.where(masks[0], b0, turned(b1)), jnp.where(masks[0], turned(b0), b1)]
                for part in (0, 1):
                    rows = slice((2 * pair + part) * SIDE, (2 * pair + part + 1) * SIDE)
                    stacks[c, rows, :] = jnp.concatenate([first[part], last[part]], axis=1).astype(BF16)
        return carry

    def gradients(turn, carry):
        for c in [STRIDE * turn + i for i in range(STRIDE)]:
            k, members, _, _ = read(c)
            depth = bands * SIDE
            grads = dot(stacks[c, :, :depth], right[k, :depth, :])
            for u, v in enumerate(members):
                top = grads[u * SIDE : u * SIDE + ROWS]
                low = grads[u * SIDE + ROWS : (u + 1) * SIDE]
                stamp = jnp.where(packed_low, top, low).astype(BF16)
                side, place = v // CAP % 2, v // (2 * CAP) * CAP + v % CAP
                keep[jnp.where(side == core, place, spare)] = stamp
                send[jnp.where(side == 1 - core, place, spare)] = stamp
        return carry

    lax.fori_loop(0, rounds, outer_products, 0)
    lax.fori_loop(0, rounds, gradients, 0)
    meta = amp_rows([lane_sums(sums[band, :none, :]) for band in range(bands)])
    keep[spare] = meta
    send[spare] = meta


def home_slots_kernel(bands, residual, left_t, right, back):
    num_slots = residual.shape[1]
    back[:, num_slots] = jnp.zeros((bands, ROWS, LANES), BF16)
    packed_low = half_masks(ROWS)[0]

    def slot(q, carry):
        for band in range(bands):
            outer = dot(left_t[band, q], residual[band, q]).astype(BF16)
            grad = dot(outer[:, :SIDE], right[q, band * SIDE : (band + 1) * SIDE, :])
            back[band, q] = jnp.where(packed_low, grad[:ROWS], grad[ROWS:]).astype(BF16)
        return carry

    lax.fori_loop(0, num_slots, slot, 0, unroll=8)


def home_gather_kernel(bands, last, lists, amps, eta_m, morph, back, received, keep, grad_a, sums):
    core = lax.axis_index("band")
    mine = pl.ds(half_rows(), HALF) if last else pl.ds(0, ROWS)

    def gather(s, carry):
        q = lists[0, 0, s]
        stamp = rounded(morph[s])
        grad = jnp.zeros((HALF if last else ROWS, LANES), F32)
        for ref, side in ((back, core), (received, 1 - core)):
            for band in range(bands):
                amp = amps[side * bands + band, s]
                if last:
                    grad = grad + amp * ref[band, q, mine, :].astype(F32)
                    if ref is received:
                        continue
                seen = ref[band, q].astype(F32)
                if not last:
                    grad = grad + amp * seen
                along = jnp.sum(seen * stamp, axis=0, keepdims=True)
                sums[side * bands + band, pl.ds(s, 1), :] = along
        keep[s] = jnp.maximum(morph[s, mine, :].astype(F32), 0.0) - eta_m[0, s] * grad
        return carry

    lax.fori_loop(0, lists.shape[2], gather, 0, unroll=4)
    for band in range(grad_a.shape[0]):
        rows = sums[core * bands + band] if last else sums[band]
        grad_a[band : band + 1, :] = lane_sums(rows)[:1]


def amp_rows(sums):
    eight = iota((8, LANES), 0)
    total = jnp.zeros((8, LANES), F32)
    for band, row in enumerate(sums):
        total = jnp.where(eight == band, row, total)
    coarse = total.astype(BF16).astype(F32)
    return jnp.concatenate([coarse, total - coarse, jnp.zeros((HALF, LANES), F32)], axis=0).astype(BF16)


def reduce_kernel(keep, received, *messages):
    for turn in range(2):
        part = pl.ds(turn * CAP, CAP)
        total = keep[part].astype(F32) + received[part].astype(F32)
        messages[turn][pl.ds(0, CAP)] = total.astype(BF16)
        pair = by_core(keep[2 * CAP].astype(F32), received[2 * CAP].astype(F32))
        meta = jnp.concatenate([pair[0][:HALF], pair[1][:HALF]], axis=0)
        messages[turn][CAP] = meta.astype(BF16)


def update_kernel(last, places, eta_m, slots_ref, eta_a, hots, amps_ref, grad_a, home, *refs):
    grads, out = refs[:NEAR], refs[NEAR:]
    state, amps_out, work = out[0], out[1], out[-1] if last else out[0]
    core = lax.axis_index("band")
    mine = pl.ds(half_rows(), HALF) if last else pl.ds(0, ROWS)
    nears = (core, 2 + core, 1 - core, 3 - core)
    lane = iota((ROWS, LANES), 1) // CAP
    meta = jnp.zeros((ROWS, LANES), F32)
    for ref, near in zip(grads, nears):
        meta = jnp.where(lane == near, ref[CAP].astype(F32), meta)
    all_hots = jnp.concatenate([hots[near, :CAP] for near in range(NEAR)], axis=0)
    from_near = dot(meta.astype(BF16), all_hots)
    bands = amps_ref.shape[0] // 2
    sides = [from_near[r : r + bands] + from_near[r + 8 : r + 8 + bands] for r in (0, HALF)]
    if last:
        amps = by_core(amps_ref[:bands], amps_ref[bands:])[0]
        total = grad_a[...] + by_core(sides[0], sides[1])[0]
    else:
        amps = amps_ref[...]
        total = grad_a[...] + jnp.concatenate(sides, axis=0)
    amps = jnp.maximum(amps - eta_a[...] * total, 0.0)
    if last:
        for band in range(bands):
            amps_out[band] = amps[band : band + 1]
    else:
        amps_out[...] = amps
    work[...] = home[...]
    for ref, near in zip(grads, nears):

        def add(n, carry, ref=ref, near=near):
            s = places[near, n]
            work[s] -= eta_m[0, s] * ref[n, mine, :].astype(F32)
            return carry

        lax.fori_loop(0, CAP, add, 0, unroll=8)

    if last:
        for r in range(HALF):
            state[:, r * LANES : (r + 1) * LANES] = jnp.maximum(work[:, r, :], 0.0)
        return
    amps_q, messages = out[2], out[3:5]
    amps_q[...] = amps.astype(BF16).astype(F32)

    def stamp_of(s):
        return jnp.maximum(state[s], 0.0).astype(BF16)

    write_messages(messages, rows_of(slots_ref), amps, hots, places, stamp_of)


def call(body, name, operands, scalars, outs, scratch=(), flops=0, moved=0):
    vmem, smem = pl.BlockSpec(memory_space=pltpu.VMEM), pl.BlockSpec(memory_space=pltpu.SMEM)
    return pl.pallas_call(
        body,
        out_shape=[jax.ShapeDtypeStruct(shape, dtype) for shape, dtype in outs],
        in_specs=[smem if i < scalars else vmem for i in range(len(operands))],
        out_specs=[vmem] * len(outs),
        scratch_shapes=[pltpu.VMEM(shape, dtype) for shape, dtype in scratch],
        compiler_params=pltpu.CompilerParams(vmem_limit_bytes=40 * 2**20),
        cost_estimate=pl.CostEstimate(flops=flops, bytes_accessed=moved, transcendentals=0),
        name=name,
    )(*operands)


def stepped(value, axis, step):
    shape = [lax.axis_size(name) for name in ("ra", "dec", "band")]

    def device(ra, dec, band):
        return (ra * shape[1] + dec) * shape[2] + band

    pairs = []
    for ra in range(shape[0]):
        for dec in range(shape[1]):
            for band, by in ((0, step), (1, -step)):
                if axis == "ra":
                    pairs.append((device(ra, dec, band), device((ra + by) % shape[0], dec, band)))
                elif 0 <= dec + by < shape[1]:
                    pairs.append((device(ra, dec, band), device(ra, dec + by, band)))
    return lax.ppermute(value, ("ra", "dec", "band"), pairs)


def swapped(value):
    return lax.ppermute(value, "band", [(0, 1), (1, 0)])


def all_tables(psf, num_slots, messages, sums):
    bands, held = psf.shape[:2]
    lines = lax.axis_size("dec")
    if lax.axis_size("ra") == 4 and 2 * held == num_slots and held % 2 == 0 and lines % 2 == 0:
        across = [(i, (i + lines // 2) % lines) for i in range(lines)]
        along = [(0, 1), (1, 0), (2, 3), (3, 2)]
        mine = jnp.where(lax.axis_index("dec") < lines // 2, psf[:, : held // 2], psf[:, held // 2 :])
        far = lax.ppermute(mine, "ra", [(0, 2), (1, 3)])
        far, sums = lax.optimization_barrier((far, sums))
        here = jnp.where(lax.axis_index("ra") < 2, mine, far)
        here, messages[0] = lax.optimization_barrier((here, messages[0]))
        near = lax.ppermute(here, "ra", along)
        near, messages[1] = lax.optimization_barrier((near, messages[1]))
        halves = make_tables((here, near), bands)
        others = (lax.ppermute(here, "dec", across), lax.ppermute(near, "dec", across))
        return make_tables(others, bands, halves), messages, sums
    return make_tables((lax.all_gather(psf, "ra", axis=1, tiled=True)[:, :num_slots],), bands), messages, sums


def shards(morphology, sed_amps, slot_lists, morph_step, sed_step, psf_kernels, observed):
    bands, num_slots, sources = sed_amps.shape[2], observed.shape[3], morphology.shape[2]
    lists, amps = slot_lists[0, 0][:, None, :], sed_amps[0, 0][:, None, :]
    eta_m, eta_a = morph_step[0], sed_step[0]
    full = morphology[0, 0].reshape(sources, ROWS, LANES)
    seen = observed[0, 0].reshape(bands, num_slots, ROWS, LANES)
    stamp = ((CAP + 1, ROWS, LANES), BF16)
    all_stamps = (sources, ROWS, LANES)
    near_all = NEAR * CAP
    chunks = -(-(near_all // GROUP + num_slots) // STRIDE) * STRIDE
    amps_theirs = swapped(amps)
    hots, places = call(
        functools.partial(lists_kernel, num_slots),
        "lists",
        (lists,),
        0,
        [
            ((NEAR, LANES, sources), BF16),
            ((2 * NEAR, LANES), jnp.int32),
        ],
        moved=2**20,
    )
    *messages, amps, amps_q = call(
        pack_kernel,
        "pack",
        (places, lists, amps, amps_theirs, hots, full),
        1,
        [stamp] * 2 + [((2 * bands, sources), F32)] * 2,
        moved=2**20,
    )
    def home_sums(amps_q, morph):
        return call(
            functools.partial(home_sums_kernel, bands),
            "home_sums",
            (lists, amps_q, morph),
            2,
            [((bands, num_slots + 1, ROWS, LANES), F32)],
            moved=4 * 2**20,
        )[0]

    sums = home_sums(amps_q, full)
    tables, messages, sums = all_tables(psf_kernels, num_slots, messages, sums)
    first_t, left, left_t, right = tables
    morph, plan = full, None
    for sweep in range(ITERS):
        last = sweep == ITERS - 1
        own = [stepped(messages[0], "ra", 1), stepped(messages[1], "dec", 1)]
        if sweep == 0:
            left, *own = lax.optimization_barrier((left, *own))
        else:
            sums = home_sums(amps_q, morph)
        home = call(
            functools.partial(home_forward_kernel, bands),
            "home_forward",
            (sums, seen, first_t, left),
            0,
            [((bands, num_slots, SIDE, LANES), F32)],
            [((bands, num_slots, SIDE, LANES), BF16)],
            flops=2 * 10**9,
            moved=4 * 2**20,
        )[0]
        if sweep > 0:
            own = [lax.optimization_barrier((home, x))[1] for x in own]
        other = [swapped(x) for x in own]
        amps_near, *new_plan = call(
            functools.partial(order_kernel, num_slots, sweep > 0),
            "order",
            (*own, *other),
            0,
            [((bands, LANES), F32)] + [((8, -(-chunks * GROUP // LANES) * LANES), jnp.int32)] * (sweep == 0),
            moved=2**20,
        )
        plan = new_plan[0] if new_plan else plan
        residual, inner_all = call(
            functools.partial(forward_kernel, bands),
            "forward",
            (plan, amps_near, *own, *other, home, first_t, left),
            2,
            [
                ((bands, num_slots, SIDE, LANES), BF16),
                ((chunks, bands, SIDE, WIDE), BF16),
            ],
            [((near_all + 1, SIDE, LANES), BF16)] + [((num_slots, SIDE, LANES), F32)] * (2 * bands),
            flops=3 * 10**9,
            moved=8 * 2**20,
        )
        half_of_near = ((near_all // 2 + 1, ROWS, LANES), BF16)
        keep, send = call(
            functools.partial(backward_kernel, bands),
            "backward",
            (plan, amps_near, residual, inner_all, left_t, right),
            2,
            [half_of_near] * 2,
            [((chunks, WIDE, WIDE), BF16), ((bands, near_all + 8, LANES), F32)],
            flops=3 * 10**9,
            moved=8 * 2**20,
        )
        received = swapped(send)
        back = call(
            functools.partial(home_slots_kernel, bands),
            "home_slots",
            (residual, left_t, right),
            0,
            [((bands, num_slots + 1, ROWS, LANES), BF16)],
            flops=2 * 10**9,
            moved=4 * 2**20,
        )[0]
        received, back = lax.optimization_barrier((received, back))
        grads = call(reduce_kernel, "reduce", (keep, received), 0, [stamp] * 2, moved=2 * 2**20)
        grads = [stepped(grads[0], "ra", -1), stepped(grads[1], "dec", -1)]
        back_received = swapped(back)
        bands_here = bands if last else 2 * bands
        part = (sources, HALF, LANES) if last else all_stamps
        home_grad, grad_a = call(
            functools.partial(home_gather_kernel, bands, last),
            "home_gather",
            (lists, amps_q, eta_m, morph, back, back_received),
            3,
            [(part, F32), ((bands_here, sources), F32)],
            [((2 * bands, sources, LANES), F32)],
            moved=4 * 2**20,
        )
        grads = [lax.optimization_barrier((home_grad, x))[1] for x in grads]
        grads += [swapped(x) for x in grads]
        outs = [((sources, HALF * LANES) if last else all_stamps, F32)]
        outs += [((bands, 1, sources) if last else (2 * bands, sources), F32)]
        if not last:
            outs += [((bands_here, sources), F32)] + [stamp] * 2
        state, amps, *more = call(
            functools.partial(update_kernel, last),
            "update",
            (places, eta_m, lists, eta_a, hots, amps, grad_a, home_grad, *grads),
            2,
            outs,
            [(part, F32)] if last else (),
            moved=3 * 2**20,
        )
        if not last:
            morph = state
            amps_q, *messages = more
    return state[None, None], amps.reshape(1, 1, bands, sources)


def solution(mesh):
    in_specs = (
        P("ra", "dec", None, None),
        P("ra", "dec", "band", None),
        P("ra", "dec", None, None),
        P("ra", "dec", None),
        P("ra", "dec", None),
        P("band", "ra", None),
        P("ra", "dec", "band", None, None),
    )
    out_specs = (P("ra", "dec", None, "band"), P("ra", "dec", "band", None))
    return jax.shard_map(shards, mesh=mesh, in_specs=in_specs, out_specs=out_specs, check_vma=False)
```

```python
import functools

import jax
import jax.numpy as jnp
from jax import lax
from jax.experimental import pallas as pl
from jax.experimental.pallas import tpu as pltpu
from jax.sharding import PartitionSpec as P

SIDE = 64
KERN = 32
ITERS = 2
CAP = 32
LANES = 128
ROWS = SIDE * SIDE // LANES
HALF = ROWS // 2
WIDE = 4 * SIDE
ORDER, KERNEL_OF, SLOT_OF, COUNT = range(4)
NEAR = 4
GROUP = 4
STRIDE = 8
F32 = jnp.float32
BF16 = jnp.bfloat16


def dot(a, b):
    return lax.dot_general(a, b, (((1,), (0,)), ((), ())), preferred_element_type=F32)


def dot_nt(a, b):
    return lax.dot_general(a, b, (((1,), (1,)), ((), ())), preferred_element_type=F32)


def iota(shape, dim):
    return lax.broadcasted_iota(jnp.int32, shape, dim)


def low_lanes(rows, dtype=F32):
    return (iota((rows, LANES), 1) < SIDE).astype(F32).astype(dtype)


def lane_sums(rows):
    coarse = rows.astype(BF16)
    fine = (rows - coarse.astype(F32)).astype(BF16)
    ones = jnp.ones((8, rows.shape[1]), BF16)
    return dot_nt(ones, coarse) + dot_nt(ones, fine)


def half_masks(rows):
    low = iota((rows, LANES), 1) < SIDE
    return low, jnp.logical_not(low)


def turned(value):
    return pltpu.roll(value, SIDE, 1)


def twofold(packed):
    low, flip = half_masks(ROWS)[0], turned(packed)
    return jnp.concatenate([jnp.where(low, packed, flip), jnp.where(low, flip, packed)], axis=0)


def rounded(stamp):
    if stamp.dtype == F32:
        stamp = jnp.maximum(stamp, 0.0).astype(BF16)
    return stamp.astype(F32)


def half_rows():
    return pl.multiple_of(lax.axis_index("band") * HALF, HALF)


def rows_of(ref):
    return jnp.concatenate([ref[i] for i in range(ref.shape[0])], axis=0)


def by_core(mine, theirs):
    first = lax.axis_index("band") == 0
    return jnp.where(first, mine, theirs), jnp.where(first, theirs, mine)


def lists_kernel(num_slots, slots_ref, hots, places):
    slots = rows_of(slots_ref)
    sources = slots.shape[1]
    valid = (slots < num_slots).astype(F32)
    upper = (iota((sources, sources), 0) <= iota((sources, sources), 1)).astype(F32)
    rank = dot(valid.astype(BF16), upper.astype(BF16))
    place = iota((LANES, sources), 0).astype(F32)
    names = iota((8, sources), 1).astype(F32).astype(BF16)
    for near in range(NEAR):
        row = slice(near + 1, near + 2)
        hot = ((place == rank[row] - 1.0).astype(F32) * valid[row]).astype(BF16)
        hots[near] = hot
        places[near : near + 1, :] = dot_nt(names, hot)[:1].astype(jnp.int32)
        count = jnp.broadcast_to(rank[row, sources - 1 :], (1, LANES))
        places[NEAR + near : NEAR + near + 1, :] = count.astype(jnp.int32)


def write_messages(messages, slots, amps, hots, places, stamp_of):
    first = lax.axis_index("band") == 0
    row = iota((ROWS, slots.shape[1]), 0)
    for turn in range(2):
        near = 2 * turn + lax.axis_index("band")

        def pick(n, carry, near=near, turn=turn):
            messages[turn][n] = stamp_of(places[near, n])
            return carry

        lax.fori_loop(0, CAP, pick, 0, unroll=8)
        slot = jnp.where(first, slots[2 * turn + 1 : 2 * turn + 2], slots[2 * turn + 2 : 2 * turn + 3]).astype(F32)
        meta = jnp.where(row == 0, slot + 1.0, 0.0)
        meta = jnp.where(row == 1, slots[0:1].astype(F32), meta)
        for band in range(amps.shape[0]):
            meta = jnp.where(row == 2 + band, amps[band : band + 1], meta)
        hot = jnp.where(first, hots[2 * turn].astype(F32), hots[2 * turn + 1].astype(F32)).astype(BF16)
        messages[turn][CAP] = dot_nt(meta.astype(BF16), hot).astype(BF16)


def pack_kernel(places, slots_ref, amps_mine, amps_theirs, hots, morph, *out):
    messages, amps_out, amps_q = out[:2], out[2], out[3]
    amps = jnp.concatenate(by_core(rows_of(amps_mine), rows_of(amps_theirs)), axis=0)
    write_messages(messages, rows_of(slots_ref), amps, hots, places, lambda s: morph[s])
    amps_out[...] = amps
    amps_q[...] = amps.astype(BF16).astype(F32)


def order_kernel(num_slots, again, *refs):
    amps, none = refs[NEAR], NEAR * CAP
    bands = amps.shape[0]
    meta = jnp.zeros((ROWS, LANES), F32)
    for turn in range(2):
        pair = by_core(refs[turn][CAP].astype(F32), refs[2 + turn][CAP].astype(F32))
        for core in range(2):
            meta = meta + pltpu.roll(pair[core], (2 * turn + core) * CAP, 1)
    amps[...] = by_core(meta[2 : 2 + bands], meta[2 + bands : 2 + 2 * bands])[0]
    if again:
        return
    plan, slot, kernel = refs[NEAR + 1], meta[0:1], meta[1:2]
    plan[SLOT_OF : SLOT_OF + 1, :LANES] = jnp.maximum(slot - 1.0, 0.0).astype(jnp.int32)
    live = (slot > 0.0).astype(F32)
    hot = (iota((num_slots, none), 0).astype(F32) == kernel).astype(F32) * live
    upto = (iota((none, none), 0) <= iota((none, none), 1)).astype(F32).astype(BF16)
    rank = dot(hot.astype(BF16), upto)
    size = jnp.max(rank, axis=1, keepdims=True)
    filled = ((size.astype(jnp.int32) + (GROUP - 1)) // GROUP).astype(F32)
    before = (iota((num_slots, num_slots), 1) < iota((num_slots, num_slots), 0)).astype(F32).astype(BF16)
    start = dot(before, jnp.broadcast_to(filled, (num_slots, none)).astype(BF16))
    place = jnp.sum(hot * (GROUP * start + rank), axis=0, keepdims=True) - 1.0
    eight = iota((8, none), 0)
    names = jnp.where(eight == 0, iota((8, none), 1).astype(F32) - none, 0.0).astype(BF16)
    for part in range(plan.shape[1] // LANES):
        at = (iota((LANES, none), 0) + part * LANES).astype(F32)
        hit = (at == place).astype(F32) * live
        found = dot_nt(names, hit.astype(BF16))[:1] + none
        plan[ORDER : ORDER + 1, part * LANES : (part + 1) * LANES] = found.astype(jnp.int32)
    chunk = iota((num_slots, LANES), 1).astype(F32)
    row = iota((num_slots, LANES), 0).astype(F32)
    inside = (chunk >= start[:, :LANES]) & (chunk < start[:, :LANES] + filled)
    kernels = jnp.sum(jnp.where(inside, row, 0.0), axis=0, keepdims=True)
    plan[KERNEL_OF : KERNEL_OF + 1, :LANES] = kernels.astype(jnp.int32)
    total = jnp.sum(filled, axis=0, keepdims=True)
    plan[COUNT : COUNT + 1, :LANES] = jnp.broadcast_to(total, (1, LANES)).astype(jnp.int32)


def quarter_start(quarter, held):
    parity, line = lax.axis_index("ra") % 2, lax.axis_index("dec") // (lax.axis_size("dec") // 2)
    shard = parity if quarter % 2 == 0 else 1 - parity
    half = line if quarter < 2 else 1 - line
    return (2 * shard + half) * held


def tables_kernel(bands, earlier, *refs):
    shards, (first_t, left, left_t, right, packed) = refs[: len(refs) - 5 - 4 * earlier], refs[-5:]
    held = shards[0].shape[1]
    for turn, ref in enumerate(shards):
        for band in range(bands):
            for r in range(ROWS):
                rows = pl.ds(turn * held * ROWS + r, held, stride=ROWS)
                packed[band, rows, :] = ref[band, :, r * LANES : (r + 1) * LANES].astype(F32)
    starts = [quarter_start(2 + turn, held) if earlier else turn * held for turn in range(len(shards))]
    if earlier:
        old_first, old_left, old_left_t, old_right = refs[len(shards) : len(shards) + 4]
        for turn in range(2):
            old, new = pl.ds(turn * held, held), pl.ds(quarter_start(turn, held), held)
            first_t[new] = old_first[old]
            right[new] = old_right[old]
            for band in range(bands):
                left[band, new] = old_left[band, old]
                left_t[band, new] = old_left_t[band, old]
    eye = (iota((SIDE, SIDE), 0) == iota((SIDE, SIDE), 1)).astype(F32).astype(BF16)
    row, col = iota((SIDE, SIDE), 0), iota((SIDE, SIDE), 1)
    even = (col == 2 * (row % ROWS) + row // ROWS).astype(F32).astype(BF16)
    even_t = (row == 2 * (col % ROWS) + col // ROWS).astype(F32).astype(BF16)
    rest = [jnp.zeros((SIDE * (4 - bands), SIDE), BF16)] if bands < 4 else []

    def step(place, carry):
        for turn, start in enumerate(starts):
            k = start + place
            at = pl.multiple_of((turn * held + place) * ROWS, ROWS)
            parts = [twofold(packed[band, pl.ds(at, ROWS), :]).astype(BF16) for band in range(bands)]
            lefts = dot_nt(jnp.concatenate([part[:, :SIDE] for part in parts], axis=0), even).astype(BF16)
            natural = []
            for band, part in enumerate(parts):
                rows = slice(band * SIDE, (band + 1) * SIDE)
                left[band, k] = lefts[rows]
                left_t[band, k] = dot_nt(even, part[:, :SIDE]).astype(BF16)
                both = dot(even_t, part).astype(BF16)
                right[k, rows, :] = both
                natural.append(both[:, :SIDE])
            if rest:
                right[k, bands * SIDE :, :] = jnp.zeros((SIDE * (4 - bands), LANES), BF16)
            first_t[k] = dot_nt(eye, jnp.concatenate(natural + rest, axis=0)).astype(BF16)
        return carry

    lax.fori_loop(0, held, step, 0, unroll=min(held, 4))


def make_tables(shards, bands, earlier=()):
    count = sum(x.shape[1] for x in shards)
    total = count + sum(x.shape[0] for x in earlier[:1])
    square = ((bands, total, SIDE, SIDE), BF16)
    return call(
        functools.partial(tables_kernel, bands, bool(earlier)),
        "tables",
        (*shards, *earlier),
        0,
        [((total, SIDE, WIDE), BF16), square, square, ((total, WIDE, LANES), BF16)],
        [((bands, count * ROWS, LANES), F32)],
        flops=2 * 10**9,
        moved=5 * 2**20,
    )


def home_sums_kernel(bands, lists, amps, morph, sums):
    first = lax.axis_index("band") * bands
    sums[...] = jnp.zeros_like(sums)

    def add(s, carry):
        q = lists[0, 0, s]
        stamp = rounded(morph[s])
        for band in range(bands):
            sums[band, q] += amps[first + band, s] * stamp
        return carry

    lax.fori_loop(0, lists.shape[2], add, 0, unroll=4)


def home_forward_kernel(bands, sums, observed, first_t, left, total, inner_all):
    num_slots = total.shape[1]
    masks = half_masks(SIDE)

    def inner_products(q, carry):
        images = []
        for band in range(bands):
            both = sums[band, q]
            images += [both[:, :SIDE], turned(both)[:, :SIDE]]
        inners = dot(jnp.concatenate(images, axis=0).astype(BF16), first_t[q])
        for band in range(bands):
            lanes = slice(band // 2 * LANES, (band // 2 + 1) * LANES)
            inner_all[band, q] = inners[band * SIDE : (band + 1) * SIDE, lanes].astype(BF16)
        return carry

    def slot(q, carry):
        for band in range(bands):
            image = dot(left[band, q], inner_all[band, q]) - twofold(observed[band, q].astype(F32))
            total[band, q] = jnp.where(masks[band % 2], image, 0.0)
        return carry

    lax.fori_loop(0, num_slots, inner_products, 0, unroll=4)
    lax.fori_loop(0, num_slots, slot, 0, unroll=4)


def chunk_reader(bands, plan, amps):
    none = NEAR * CAP

    def read(c):
        members = [plan[ORDER, c * GROUP + u] for u in range(GROUP)]
        held = [jnp.minimum(v, none - 1) for v in members]
        values = [[jnp.where(v < none, amps[band, h], 0.0) for v, h in zip(members, held)] for band in range(bands)]
        return plan[KERNEL_OF, c], members, [plan[SLOT_OF, h] for h in held], values

    return read, (plan[COUNT, 0] + STRIDE - 1) // STRIDE


def forward_kernel(bands, plan, amps, *refs):
    home, first_t, left = refs[NEAR : NEAR + 3]
    residual, inner_all, stamps, *totals = refs[NEAR + 3 :]
    totals = [totals[2 * band : 2 * band + 2] for band in range(bands)]
    num_slots = home.shape[1]
    none = NEAR * CAP
    core = lax.axis_index("band")
    for source, near in enumerate((core, 2 + core, 1 - core, 3 - core)):
        group = pl.ds(near * CAP, CAP)
        even = refs[source][pl.ds(0, CAP)].astype(F32)
        odd = turned(even.reshape(CAP * ROWS, LANES)).reshape(CAP, ROWS, LANES)
        stamps[group, pl.ds(0, ROWS), :] = even.astype(BF16)
        stamps[group, pl.ds(ROWS, ROWS), :] = odd.astype(BF16)
    stamps[none] = jnp.zeros((SIDE, LANES), BF16)
    for band in range(bands):
        totals[band][band % 2][...] = home[band]
        totals[band][1 - band % 2][...] = jnp.zeros_like(home[band])
    masks, row_masks = half_masks(SIDE), half_masks(1)
    read, rounds = chunk_reader(bands, plan, amps)

    def inner_products(turn, carry):
        for c in [STRIDE * turn + i for i in range(STRIDE)]:
            k, members, _, _ = read(c)
            stack = jnp.concatenate([stamps[v] for v in members], axis=0)
            inners = dot(stack[:, :SIDE], first_t[k])
            for band in range(bands):
                lanes = slice(band // 2 * LANES, (band // 2 + 1) * LANES)
                pairs = []
                for u in range(0, GROUP, 2):
                    x = inners[u * SIDE : (u + 1) * SIDE, lanes]
                    y = inners[(u + 1) * SIDE : (u + 2) * SIDE, lanes]
                    x, y = (x, turned(y)) if band % 2 == 0 else (turned(x), y)
                    pairs.append(jnp.where(masks[0], x, y))
                inner_all[c, band] = jnp.concatenate(pairs, axis=1).astype(BF16)
        return carry

    def images(turn, carry):
        for c in [STRIDE * turn + i for i in range(STRIDE)]:
            k, _, slots, values = read(c)
            for band in range(bands):
                image = dot(left[band, k], inner_all[c, band])
                for u in range(0, GROUP, 2):
                    lanes = slice(u // 2 * LANES, (u // 2 + 1) * LANES)
                    scale = jnp.where(row_masks[0], values[band][u], values[band][u + 1])
                    pair = image[:, lanes] * scale
                    for part in (0, 1):
                        totals[band][part][slots[u + part]] += pair
        return carry

    lax.fori_loop(0, rounds, inner_products, 0)
    lax.fori_loop(0, rounds, images, 0)

    def slot(q, carry):
        for band in range(bands):
            model = jnp.where(masks[0], totals[band][0][q], totals[band][1][q])
            residual[band, q] = (model + turned(model)).astype(BF16)
        return carry

    lax.fori_loop(0, num_slots, slot, 0, unroll=8)


def backward_kernel(bands, plan, amps, *refs):
    residual, inner_all, left_t, right, keep, send, stacks, sums = refs
    none = NEAR * CAP
    sums[...] = jnp.zeros_like(sums)
    keep[...] = jnp.zeros_like(keep)
    send[...] = jnp.zeros_like(send)
    masks, row_masks, packed_low = half_masks(SIDE), half_masks(1), half_masks(ROWS)[0]
    read, rounds = chunk_reader(bands, plan, amps)
    spare = none // 2
    core = lax.axis_index("band")

    def outer_products(turn, carry):
        for c in [STRIDE * turn + i for i in range(STRIDE)]:
            k, members, slots, values = read(c)
            outers = []
            for band in range(bands):
                pairs = [
                    jnp.where(masks[0], residual[band, slots[u]], residual[band, slots[u + 1]])
                    for u in range(0, GROUP, 2)
                ]
                outer = dot(left_t[band, k], jnp.concatenate(pairs, axis=1))
                along = jnp.sum(inner_all[c, band].astype(F32) * outer, axis=0, keepdims=True)
                scaled = []
                for u in range(0, GROUP, 2):
                    lanes = slice(u // 2 * LANES, (u // 2 + 1) * LANES)
                    for part in (0, 1):
                        row = jnp.where(row_masks[part], along[:, lanes], 0.0)
                        sums[band, pl.ds(members[u + part], 1), :] = row
                    scale = jnp.where(row_masks[0], values[band][u], values[band][u + 1])
                    scaled.append(outer[:, lanes] * scale)
                outers.append(scaled)
            outers += [[jnp.zeros((SIDE, LANES), F32)] * (GROUP // 2)] * (4 - bands)
            for pair in range(GROUP // 2):
                b0, b1, b2, b3 = [outers[band][pair] for band in range(4)]
                if bands > 3:
                    last = [jnp.where(masks[0], b2, turned(b3)), jnp.where(masks[0], turned(b2), b3)]
                else:
                    last = [b2, turned(b2)]
                first = [jnp.where(masks[0], b0, turned(b1)), jnp.where(masks[0], turned(b0), b1)]
                for part in (0, 1):
                    rows = slice((2 * pair + part) * SIDE, (2 * pair + part + 1) * SIDE)
                    stacks[c, rows, :] = jnp.concatenate([first[part], last[part]], axis=1).astype(BF16)
        return carry

    def gradients(turn, carry):
        for c in [STRIDE * turn + i for i in range(STRIDE)]:
            k, members, _, _ = read(c)
            depth = bands * SIDE
            grads = dot(stacks[c, :, :depth], right[k, :depth, :])
            for u, v in enumerate(members):
                top = grads[u * SIDE : u * SIDE + ROWS]
                low = grads[u * SIDE + ROWS : (u + 1) * SIDE]
                stamp = jnp.where(packed_low, top, low).astype(BF16)
                side, place = v // CAP % 2, v // (2 * CAP) * CAP + v % CAP
                keep[jnp.where(side == core, place, spare)] = stamp
                send[jnp.where(side == 1 - core, place, spare)] = stamp
        return carry

    lax.fori_loop(0, rounds, outer_products, 0)
    lax.fori_loop(0, rounds, gradients, 0)
    meta = amp_rows([lane_sums(sums[band, :none, :]) for band in range(bands)])
    keep[spare] = meta
    send[spare] = meta


def home_slots_kernel(bands, residual, left_t, right, back):
    num_slots = residual.shape[1]
    back[:, num_slots] = jnp.zeros((bands, ROWS, LANES), BF16)
    packed_low = half_masks(ROWS)[0]

    def slot(q, carry):
        for band in range(bands):
            outer = dot(left_t[band, q], residual[band, q]).astype(BF16)
            grad = dot(outer[:, :SIDE], right[q, band * SIDE : (band + 1) * SIDE, :])
            back[band, q] = jnp.where(packed_low, grad[:ROWS], grad[ROWS:]).astype(BF16)
        return carry

    lax.fori_loop(0, num_slots, slot, 0, unroll=8)


def home_gather_kernel(bands, last, lists, amps, eta_m, morph, back, received, keep, grad_a, sums):
    core = lax.axis_index("band")
    mine = pl.ds(half_rows(), HALF) if last else pl.ds(0, ROWS)

    def gather(s, carry):
        q = lists[0, 0, s]
        stamp = rounded(morph[s])
        grad = jnp.zeros((HALF if last else ROWS, LANES), F32)
        for ref, side in ((back, core), (received, 1 - core)):
            for band in range(bands):
                amp = amps[side * bands + band, s]
                if last:
                    grad = grad + amp * ref[band, q, mine, :].astype(F32)
                    if ref is received:
                        continue
                seen = ref[band, q].astype(F32)
                if not last:
                    grad = grad + amp * seen
                along = jnp.sum(seen * stamp, axis=0, keepdims=True)
                sums[side * bands + band, pl.ds(s, 1), :] = along
        keep[s] = jnp.maximum(morph[s, mine, :].astype(F32), 0.0) - eta_m[0, s] * grad
        return carry

    lax.fori_loop(0, lists.shape[2], gather, 0, unroll=4)
    for band in range(grad_a.shape[0]):
        rows = sums[core * bands + band] if last else sums[band]
        grad_a[band : band + 1, :] = lane_sums(rows)[:1]


def amp_rows(sums):
    eight = iota((8, LANES), 0)
    total = jnp.zeros((8, LANES), F32)
    for band, row in enumerate(sums):
        total = jnp.where(eight == band, row, total)
    coarse = total.astype(BF16).astype(F32)
    return jnp.concatenate([coarse, total - coarse, jnp.zeros((HALF, LANES), F32)], axis=0).astype(BF16)


def reduce_kernel(keep, received, *messages):
    for turn in range(2):
        part = pl.ds(turn * CAP, CAP)
        total = keep[part].astype(F32) + received[part].astype(F32)
        messages[turn][pl.ds(0, CAP)] = total.astype(BF16)
        pair = by_core(keep[2 * CAP].astype(F32), received[2 * CAP].astype(F32))
        meta = jnp.concatenate([pair[0][:HALF], pair[1][:HALF]], axis=0)
        messages[turn][CAP] = meta.astype(BF16)


def update_kernel(last, places, eta_m, slots_ref, eta_a, hots, amps_ref, grad_a, home, *refs):
    grads, out = refs[:NEAR], refs[NEAR:]
    state, amps_out, work = out[0], out[1], out[-1] if last else out[0]
    core = lax.axis_index("band")
    mine = pl.ds(half_rows(), HALF) if last else pl.ds(0, ROWS)
    nears = (core, 2 + core, 1 - core, 3 - core)
    lane = iota((ROWS, LANES), 1) // CAP
    meta = jnp.zeros((ROWS, LANES), F32)
    for ref, near in zip(grads, nears):
        meta = jnp.where(lane == near, ref[CAP].astype(F32), meta)
    all_hots = jnp.concatenate([hots[near, :CAP] for near in range(NEAR)], axis=0)
    from_near = dot(meta.astype(BF16), all_hots)
    bands = amps_ref.shape[0] // 2
    sides = [from_near[r : r + bands] + from_near[r + 8 : r + 8 + bands] for r in (0, HALF)]
    if last:
        amps = by_core(amps_ref[:bands], amps_ref[bands:])[0]
        total = grad_a[...] + by_core(sides[0], sides[1])[0]
    else:
        amps = amps_ref[...]
        total = grad_a[...] + jnp.concatenate(sides, axis=0)
    amps = jnp.maximum(amps - eta_a[...] * total, 0.0)
    if last:
        for band in range(bands):
            amps_out[band] = amps[band : band + 1]
    else:
        amps_out[...] = amps
    work[...] = home[...]
    for ref, near in zip(grads, nears):

        def add(n, carry, ref=ref, near=near):
            s = places[near, n]
            work[s] -= eta_m[0, s] * ref[n, mine, :].astype(F32)
            return carry

        lax.fori_loop(0, CAP, add, 0, unroll=8)

    if last:
        for r in range(HALF):
            state[:, r * LANES : (r + 1) * LANES] = jnp.maximum(work[:, r, :], 0.0)
        return
    amps_q, messages = out[2], out[3:5]
    amps_q[...] = amps.astype(BF16).astype(F32)

    def stamp_of(s):
        return jnp.maximum(state[s], 0.0).astype(BF16)

    write_messages(messages, rows_of(slots_ref), amps, hots, places, stamp_of)


def call(body, name, operands, scalars, outs, scratch=(), flops=0, moved=0):
    vmem, smem = pl.BlockSpec(memory_space=pltpu.VMEM), pl.BlockSpec(memory_space=pltpu.SMEM)
    return pl.pallas_call(
        body,
        out_shape=[jax.ShapeDtypeStruct(shape, dtype) for shape, dtype in outs],
        in_specs=[smem if i < scalars else vmem for i in range(len(operands))],
        out_specs=[vmem] * len(outs),
        scratch_shapes=[pltpu.VMEM(shape, dtype) for shape, dtype in scratch],
        compiler_params=pltpu.CompilerParams(vmem_limit_bytes=40 * 2**20),
        cost_estimate=pl.CostEstimate(flops=flops, bytes_accessed=moved, transcendentals=0),
        name=name,
    )(*operands)


def stepped(value, axis, step):
    shape = [lax.axis_size(name) for name in ("ra", "dec", "band")]

    def device(ra, dec, band):
        return (ra * shape[1] + dec) * shape[2] + band

    pairs = []
    for ra in range(shape[0]):
        for dec in range(shape[1]):
            for band, by in ((0, step), (1, -step)):
                if axis == "ra":
                    pairs.append((device(ra, dec, band), device((ra + by) % shape[0], dec, band)))
                elif 0 <= dec + by < shape[1]:
                    pairs.append((device(ra, dec, band), device(ra, dec + by, band)))
    return lax.ppermute(value, ("ra", "dec", "band"), pairs)


def swapped(value):
    return lax.ppermute(value, "band", [(0, 1), (1, 0)])


def all_tables(psf, num_slots, stamps, sums):
    bands, held = psf.shape[:2]
    lines = lax.axis_size("dec")
    if lax.axis_size("ra") == 4 and 2 * held == num_slots and held % 2 == 0 and lines % 2 == 0:
        across = [(i, (i + lines // 2) % lines) for i in range(lines)]
        along = [(0, 1), (1, 0), (2, 3), (3, 2)]
        mine = jnp.where(lax.axis_index("dec") < lines // 2, psf[:, : held // 2], psf[:, held // 2 :])
        far = lax.ppermute(mine, "ra", [(0, 2), (1, 3)])
        far, sums = lax.optimization_barrier((far, sums))
        here = jnp.where(lax.axis_index("ra") < 2, mine, far)
        here_across = lax.ppermute(here, "dec", across)
        here, *stamps = lax.optimization_barrier((here, *stamps))
        near = lax.ppermute(here, "ra", along)
        halves = make_tables((here, near), bands)
        others = (here_across, lax.ppermute(near, "dec", across))
        return make_tables(others, bands, halves), stamps, sums
    return make_tables((lax.all_gather(psf, "ra", axis=1, tiled=True)[:, :num_slots],), bands), stamps, sums


def shards(morphology, sed_amps, slot_lists, morph_step, sed_step, psf_kernels, observed):
    bands, num_slots, sources = sed_amps.shape[2], observed.shape[3], morphology.shape[2]
    lists, amps = slot_lists[0, 0][:, None, :], sed_amps[0, 0][:, None, :]
    eta_m, eta_a = morph_step[0], sed_step[0]
    full = morphology[0, 0].reshape(sources, ROWS, LANES)
    seen = observed[0, 0].reshape(bands, num_slots, ROWS, LANES)
    stamp = ((CAP + 1, ROWS, LANES), BF16)
    all_stamps = (sources, ROWS, LANES)
    near_all = NEAR * CAP
    chunks = -(-(near_all // GROUP + num_slots) // STRIDE) * STRIDE
    amps_theirs = swapped(amps)
    hots, places = call(
        functools.partial(lists_kernel, num_slots),
        "lists",
        (lists,),
        0,
        [
            ((NEAR, LANES, sources), BF16),
            ((2 * NEAR, LANES), jnp.int32),
        ],
        moved=2**20,
    )
    *messages, amps, amps_q = call(
        pack_kernel,
        "pack",
        (places, lists, amps, amps_theirs, hots, full),
        1,
        [stamp] * 2 + [((2 * bands, sources), F32)] * 2,
        moved=2**20,
    )
    def home_sums(amps_q, morph):
        return call(
            functools.partial(home_sums_kernel, bands),
            "home_sums",
            (lists, amps_q, morph),
            2,
            [((bands, num_slots + 1, ROWS, LANES), F32)],
            moved=4 * 2**20,
        )[0]

    sums = home_sums(amps_q, full)
    own = [stepped(messages[0], "ra", 1), stepped(messages[1], "dec", 1)]
    tables, own, sums = all_tables(psf_kernels, num_slots, own, sums)
    first_t, left, left_t, right = tables
    morph, plan = full, None
    for sweep in range(ITERS):
        last = sweep == ITERS - 1
        if sweep > 0:
            own = [stepped(messages[0], "ra", 1), stepped(messages[1], "dec", 1)]
            sums = home_sums(amps_q, morph)
        home = call(
            functools.partial(home_forward_kernel, bands),
            "home_forward",
            (sums, seen, first_t, left),
            0,
            [((bands, num_slots, SIDE, LANES), F32)],
            [((bands, num_slots, SIDE, LANES), BF16)],
            flops=2 * 10**9,
            moved=4 * 2**20,
        )[0]
        if sweep > 0:
            own = [lax.optimization_barrier((home, x))[1] for x in own]
        other = [swapped(x) for x in own]
        amps_near, *new_plan = call(
            functools.partial(order_kernel, num_slots, sweep > 0),
            "order",
            (*own, *other),
            0,
            [((bands, LANES), F32)] + [((8, -(-chunks * GROUP // LANES) * LANES), jnp.int32)] * (sweep == 0),
            moved=2**20,
        )
        plan = new_plan[0] if new_plan else plan
        residual, inner_all = call(
            functools.partial(forward_kernel, bands),
            "forward",
            (plan, amps_near, *own, *other, home, first_t, left),
            2,
            [
                ((bands, num_slots, SIDE, LANES), BF16),
                ((chunks, bands, SIDE, WIDE), BF16),
            ],
            [((near_all + 1, SIDE, LANES), BF16)] + [((num_slots, SIDE, LANES), F32)] * (2 * bands),
            flops=3 * 10**9,
            moved=8 * 2**20,
        )
        half_of_near = ((near_all // 2 + 1, ROWS, LANES), BF16)
        keep, send = call(
            functools.partial(backward_kernel, bands),
            "backward",
            (plan, amps_near, residual, inner_all, left_t, right),
            2,
            [half_of_near] * 2,
            [((chunks, WIDE, WIDE), BF16), ((bands, near_all + 8, LANES), F32)],
            flops=3 * 10**9,
            moved=8 * 2**20,
        )
        received = swapped(send)
        back = call(
            functools.partial(home_slots_kernel, bands),
            "home_slots",
            (residual, left_t, right),
            0,
            [((bands, num_slots + 1, ROWS, LANES), BF16)],
            flops=2 * 10**9,
            moved=4 * 2**20,
        )[0]
        received, back = lax.optimization_barrier((received, back))
        grads = call(reduce_kernel, "reduce", (keep, received), 0, [stamp] * 2, moved=2 * 2**20)
        grads = [stepped(grads[0], "ra", -1), stepped(grads[1], "dec", -1)]
        back_received = swapped(back)
        bands_here = bands if last else 2 * bands
        part = (sources, HALF, LANES) if last else all_stamps
        home_grad, grad_a = call(
            functools.partial(home_gather_kernel, bands, last),
            "home_gather",
            (lists, amps_q, eta_m, morph, back, back_received),
            3,
            [(part, F32), ((bands_here, sources), F32)],
            [((2 * bands, sources, LANES), F32)],
            moved=4 * 2**20,
        )
        grads = [lax.optimization_barrier((home_grad, x))[1] for x in grads]
        grads += [swapped(x) for x in grads]
        outs = [((sources, HALF * LANES) if last else all_stamps, F32)]
        outs += [((bands, 1, sources) if last else (2 * bands, sources), F32)]
        if not last:
            outs += [((bands_here, sources), F32)] + [stamp] * 2
        state, amps, *more = call(
            functools.partial(update_kernel, last),
            "update",
            (places, eta_m, lists, eta_a, hots, amps, grad_a, home_grad, *grads),
            2,
            outs,
            [(part, F32)] if last else (),
            moved=3 * 2**20,
        )
        if not last:
            morph = state
            amps_q, *messages = more
    return state[None, None], amps.reshape(1, 1, bands, sources)


def solution(mesh):
    in_specs = (
        P("ra", "dec", None, None),
        P("ra", "dec", "band", None),
        P("ra", "dec", None, None),
        P("ra", "dec", None),
        P("ra", "dec", None),
        P("band", "ra", None),
        P("ra", "dec", "band", None, None),
    )
    out_specs = (P("ra", "dec", None, "band"), P("ra", "dec", "band", None))
    return jax.shard_map(shards, mesh=mesh, in_specs=in_specs, out_specs=out_specs, check_vma=False)
```

```python
import functools

import jax
import jax.numpy as jnp
from jax import lax
from jax.experimental import pallas as pl
from jax.experimental.pallas import tpu as pltpu
from jax.sharding import PartitionSpec as P

SIDE = 64
KERN = 32
ITERS = 2
CAP = 32
LANES = 128
ROWS = SIDE * SIDE // LANES
HALF = ROWS // 2
WIDE = 4 * SIDE
ORDER, KERNEL_OF, SLOT_OF, COUNT = range(4)
NEAR = 4
GROUP = 4
STRIDE = 8
F32 = jnp.float32
BF16 = jnp.bfloat16


def dot(a, b):
    return lax.dot_general(a, b, (((1,), (0,)), ((), ())), preferred_element_type=F32)


def dot_nt(a, b):
    return lax.dot_general(a, b, (((1,), (1,)), ((), ())), preferred_element_type=F32)


def iota(shape, dim):
    return lax.broadcasted_iota(jnp.int32, shape, dim)


def low_lanes(rows, dtype=F32):
    return (iota((rows, LANES), 1) < SIDE).astype(F32).astype(dtype)


def lane_sums(rows):
    coarse = rows.astype(BF16)
    fine = (rows - coarse.astype(F32)).astype(BF16)
    ones = jnp.ones((8, rows.shape[1]), BF16)
    return dot_nt(ones, coarse) + dot_nt(ones, fine)


def half_masks(rows):
    low = iota((rows, LANES), 1) < SIDE
    return low, jnp.logical_not(low)


def turned(value):
    return pltpu.roll(value, SIDE, 1)


def twofold(packed):
    low, flip = half_masks(ROWS)[0], turned(packed)
    return jnp.concatenate([jnp.where(low, packed, flip), jnp.where(low, flip, packed)], axis=0)


def rounded(stamp):
    if stamp.dtype == F32:
        stamp = jnp.maximum(stamp, 0.0).astype(BF16)
    return stamp.astype(F32)


def half_rows():
    return pl.multiple_of(lax.axis_index("band") * HALF, HALF)


def rows_of(ref):
    return jnp.concatenate([ref[i] for i in range(ref.shape[0])], axis=0)


def by_core(mine, theirs):
    first = lax.axis_index("band") == 0
    return jnp.where(first, mine, theirs), jnp.where(first, theirs, mine)


def lists_kernel(num_slots, slots_ref, hots, places):
    slots = rows_of(slots_ref)
    sources = slots.shape[1]
    valid = (slots < num_slots).astype(F32)
    upper = (iota((sources, sources), 0) <= iota((sources, sources), 1)).astype(F32)
    rank = dot(valid.astype(BF16), upper.astype(BF16))
    place = iota((LANES, sources), 0).astype(F32)
    names = iota((8, sources), 1).astype(F32).astype(BF16)
    for near in range(NEAR):
        row = slice(near + 1, near + 2)
        hot = ((place == rank[row] - 1.0).astype(F32) * valid[row]).astype(BF16)
        hots[near] = hot
        places[near : near + 1, :] = dot_nt(names, hot)[:1].astype(jnp.int32)
        count = jnp.broadcast_to(rank[row, sources - 1 :], (1, LANES))
        places[NEAR + near : NEAR + near + 1, :] = count.astype(jnp.int32)


def write_messages(messages, slots, amps, hots, places, stamp_of):
    first = lax.axis_index("band") == 0
    row = iota((ROWS, slots.shape[1]), 0)
    for turn in range(2):
        near = 2 * turn + lax.axis_index("band")

        def pick(n, carry, near=near, turn=turn):
            messages[turn][n] = stamp_of(places[near, n])
            return carry

        lax.fori_loop(0, CAP, pick, 0, unroll=8)
        slot = jnp.where(first, slots[2 * turn + 1 : 2 * turn + 2], slots[2 * turn + 2 : 2 * turn + 3]).astype(F32)
        meta = jnp.where(row == 0, slot + 1.0, 0.0)
        meta = jnp.where(row == 1, slots[0:1].astype(F32), meta)
        for band in range(amps.shape[0]):
            meta = jnp.where(row == 2 + band, amps[band : band + 1], meta)
        hot = jnp.where(first, hots[2 * turn].astype(F32), hots[2 * turn + 1].astype(F32)).astype(BF16)
        messages[turn][CAP] = dot_nt(meta.astype(BF16), hot).astype(BF16)


def pack_kernel(places, slots_ref, amps_mine, amps_theirs, hots, morph, *out):
    messages, amps_out, amps_q = out[:2], out[2], out[3]
    amps = jnp.concatenate(by_core(rows_of(amps_mine), rows_of(amps_theirs)), axis=0)
    write_messages(messages, rows_of(slots_ref), amps, hots, places, lambda s: morph[s])
    amps_out[...] = amps
    amps_q[...] = amps.astype(BF16).astype(F32)


def order_kernel(num_slots, again, *refs):
    amps, none = refs[NEAR], NEAR * CAP
    bands = amps.shape[0]
    meta = jnp.zeros((ROWS, LANES), F32)
    for turn in range(2):
        pair = by_core(refs[turn][CAP].astype(F32), refs[2 + turn][CAP].astype(F32))
        for core in range(2):
            meta = meta + pltpu.roll(pair[core], (2 * turn + core) * CAP, 1)
    amps[...] = by_core(meta[2 : 2 + bands], meta[2 + bands : 2 + 2 * bands])[0]
    if again:
        return
    plan, slot, kernel = refs[NEAR + 1], meta[0:1], meta[1:2]
    plan[SLOT_OF : SLOT_OF + 1, :LANES] = jnp.maximum(slot - 1.0, 0.0).astype(jnp.int32)
    live = (slot > 0.0).astype(F32)
    hot = (iota((num_slots, none), 0).astype(F32) == kernel).astype(F32) * live
    upto = (iota((none, none), 0) <= iota((none, none), 1)).astype(F32).astype(BF16)
    rank = dot(hot.astype(BF16), upto)
    size = jnp.max(rank, axis=1, keepdims=True)
    filled = ((size.astype(jnp.int32) + (GROUP - 1)) // GROUP).astype(F32)
    before = (iota((num_slots, num_slots), 1) < iota((num_slots, num_slots), 0)).astype(F32).astype(BF16)
    start = dot(before, jnp.broadcast_to(filled, (num_slots, none)).astype(BF16))
    place = jnp.sum(hot * (GROUP * start + rank), axis=0, keepdims=True) - 1.0
    eight = iota((8, none), 0)
    names = jnp.where(eight == 0, iota((8, none), 1).astype(F32) - none, 0.0).astype(BF16)
    for part in range(plan.shape[1] // LANES):
        at = (iota((LANES, none), 0) + part * LANES).astype(F32)
        hit = (at == place).astype(F32) * live
        found = dot_nt(names, hit.astype(BF16))[:1] + none
        plan[ORDER : ORDER + 1, part * LANES : (part + 1) * LANES] = found.astype(jnp.int32)
    chunk = iota((num_slots, LANES), 1).astype(F32)
    row = iota((num_slots, LANES), 0).astype(F32)
    inside = (chunk >= start[:, :LANES]) & (chunk < start[:, :LANES] + filled)
    kernels = jnp.sum(jnp.where(inside, row, 0.0), axis=0, keepdims=True)
    plan[KERNEL_OF : KERNEL_OF + 1, :LANES] = kernels.astype(jnp.int32)
    total = jnp.sum(filled, axis=0, keepdims=True)
    plan[COUNT : COUNT + 1, :LANES] = jnp.broadcast_to(total, (1, LANES)).astype(jnp.int32)


def quarter_start(quarter, held):
    parity, line = lax.axis_index("ra") % 2, lax.axis_index("dec") // (lax.axis_size("dec") // 2)
    shard = parity if quarter % 2 == 0 else 1 - parity
    half = line if quarter < 2 else 1 - line
    return (2 * shard + half) * held


def tables_kernel(bands, earlier, *refs):
    shards, (first_t, left, left_t, right, packed) = refs[: len(refs) - 5 - 4 * earlier], refs[-5:]
    held = shards[0].shape[1]
    for turn, ref in enumerate(shards):
        for band in range(bands):
            for r in range(ROWS):
                rows = pl.ds(turn * held * ROWS + r, held, stride=ROWS)
                packed[band, rows, :] = ref[band, :, r * LANES : (r + 1) * LANES].astype(F32)
    starts = [quarter_start(2 + turn, held) if earlier else turn * held for turn in range(len(shards))]
    if earlier:
        old_first, old_left, old_left_t, old_right = refs[len(shards) : len(shards) + 4]
        for turn in range(2):
            old, new = pl.ds(turn * held, held), pl.ds(quarter_start(turn, held), held)
            first_t[new] = old_first[old]
            right[new] = old_right[old]
            for band in range(bands):
                left[band, new] = old_left[band, old]
                left_t[band, new] = old_left_t[band, old]
    eye = (iota((SIDE, SIDE), 0) == iota((SIDE, SIDE), 1)).astype(F32).astype(BF16)
    row, col = iota((SIDE, SIDE), 0), iota((SIDE, SIDE), 1)
    even = (col == 2 * (row % ROWS) + row // ROWS).astype(F32).astype(BF16)
    even_t = (row == 2 * (col % ROWS) + col // ROWS).astype(F32).astype(BF16)
    rest = [jnp.zeros((SIDE * (4 - bands), SIDE), BF16)] if bands < 4 else []

    def step(place, carry):
        for turn, start in enumerate(starts):
            k = start + place
            at = pl.multiple_of((turn * held + place) * ROWS, ROWS)
            parts = [twofold(packed[band, pl.ds(at, ROWS), :]).astype(BF16) for band in range(bands)]
            lefts = dot_nt(jnp.concatenate([part[:, :SIDE] for part in parts], axis=0), even).astype(BF16)
            natural = []
            for band, part in enumerate(parts):
                rows = slice(band * SIDE, (band + 1) * SIDE)
                left[band, k] = lefts[rows]
                left_t[band, k] = dot_nt(even, part[:, :SIDE]).astype(BF16)
                both = dot(even_t, part).astype(BF16)
                right[k, rows, :] = both
                natural.append(both[:, :SIDE])
            if rest:
                right[k, bands * SIDE :, :] = jnp.zeros((SIDE * (4 - bands), LANES), BF16)
            first_t[k] = dot_nt(eye, jnp.concatenate(natural + rest, axis=0)).astype(BF16)
        return carry

    lax.fori_loop(0, held, step, 0, unroll=min(held, 4))


def make_tables(shards, bands, earlier=()):
    count = sum(x.shape[1] for x in shards)
    total = count + sum(x.shape[0] for x in earlier[:1])
    square = ((bands, total, SIDE, SIDE), BF16)
    return call(
        functools.partial(tables_kernel, bands, bool(earlier)),
        "tables",
        (*shards, *earlier),
        0,
        [((total, SIDE, WIDE), BF16), square, square, ((total, WIDE, LANES), BF16)],
        [((bands, count * ROWS, LANES), F32)],
        flops=2 * 10**9,
        moved=5 * 2**20,
    )


def home_sums_kernel(bands, lists, amps, morph, sums):
    first = lax.axis_index("band") * bands
    sums[...] = jnp.zeros_like(sums)

    def add(s, carry):
        q = lists[0, 0, s]
        stamp = rounded(morph[s])
        for band in range(bands):
            sums[band, q] += amps[first + band, s] * stamp
        return carry

    lax.fori_loop(0, lists.shape[2], add, 0, unroll=4)


def home_forward_kernel(bands, sums, observed, first_t, left, total, inner_all):
    num_slots = total.shape[1]
    masks = half_masks(SIDE)

    def inner_products(q, carry):
        images = []
        for band in range(bands):
            both = sums[band, q]
            images += [both[:, :SIDE], turned(both)[:, :SIDE]]
        inners = dot(jnp.concatenate(images, axis=0).astype(BF16), first_t[q])
        for band in range(bands):
            lanes = slice(band // 2 * LANES, (band // 2 + 1) * LANES)
            inner_all[band, q] = inners[band * SIDE : (band + 1) * SIDE, lanes].astype(BF16)
        return carry

    def slot(q, carry):
        for band in range(bands):
            image = dot(left[band, q], inner_all[band, q]) - twofold(observed[band, q].astype(F32))
            total[band, q] = jnp.where(masks[band % 2], image, 0.0)
        return carry

    lax.fori_loop(0, num_slots, inner_products, 0, unroll=4)
    lax.fori_loop(0, num_slots, slot, 0, unroll=4)


def chunk_reader(bands, plan, amps):
    none = NEAR * CAP

    def read(c):
        members = [plan[ORDER, c * GROUP + u] for u in range(GROUP)]
        held = [jnp.minimum(v, none - 1) for v in members]
        values = [[jnp.where(v < none, amps[band, h], 0.0) for v, h in zip(members, held)] for band in range(bands)]
        return plan[KERNEL_OF, c], members, [plan[SLOT_OF, h] for h in held], values

    return read, (plan[COUNT, 0] + STRIDE - 1) // STRIDE


def visitors_kernel(bands, plan, amps, *refs):
    home, first_t, left, left_t, right = refs[NEAR : NEAR + 5]
    residual, keep, send, upper, inner_all, stamps, stacks, sums, *totals = refs[NEAR + 5 :]
    totals = [totals[2 * band : 2 * band + 2] for band in range(bands)]
    num_slots = home.shape[1]
    none = NEAR * CAP
    core = lax.axis_index("band")
    for source, near in enumerate((core, 2 + core, 1 - core, 3 - core)):
        group = pl.ds(near * CAP, CAP)
        even = refs[source][pl.ds(0, CAP)].astype(F32)
        odd = turned(even.reshape(CAP * ROWS, LANES)).reshape(CAP, ROWS, LANES)
        stamps[group, pl.ds(0, ROWS), :] = even.astype(BF16)
        stamps[group, pl.ds(ROWS, ROWS), :] = odd.astype(BF16)
    stamps[none] = jnp.zeros((SIDE, LANES), BF16)
    for band in range(bands):
        totals[band][band % 2][...] = home[band]
        totals[band][1 - band % 2][...] = jnp.zeros_like(home[band])
    masks, row_masks = half_masks(SIDE), half_masks(1)
    read, rounds = chunk_reader(bands, plan, amps)

    def inner_products(turn, carry):
        for c in [STRIDE * turn + i for i in range(STRIDE)]:
            k, members, _, _ = read(c)
            stack = jnp.concatenate([stamps[v] for v in members], axis=0)
            inners = dot(stack[:, :SIDE], first_t[k])
            for band in range(bands):
                lanes = slice(band // 2 * LANES, (band // 2 + 1) * LANES)
                pairs = []
                for u in range(0, GROUP, 2):
                    x = inners[u * SIDE : (u + 1) * SIDE, lanes]
                    y = inners[(u + 1) * SIDE : (u + 2) * SIDE, lanes]
                    x, y = (x, turned(y)) if band % 2 == 0 else (turned(x), y)
                    pairs.append(jnp.where(masks[0], x, y))
                inner_all[c, band] = jnp.concatenate(pairs, axis=1).astype(BF16)
        return carry

    def images(turn, carry):
        for c in [STRIDE * turn + i for i in range(STRIDE)]:
            k, _, slots, values = read(c)
            for band in range(bands):
                image = dot(left[band, k], inner_all[c, band])
                for u in range(0, GROUP, 2):
                    lanes = slice(u // 2 * LANES, (u // 2 + 1) * LANES)
                    scale = jnp.where(row_masks[0], values[band][u], values[band][u + 1])
                    pair = image[:, lanes] * scale
                    for part in (0, 1):
                        totals[band][part][slots[u + part]] += pair
        return carry

    lax.fori_loop(0, rounds, inner_products, 0)
    lax.fori_loop(0, rounds, images, 0)

    def slot(q, carry):
        for band in range(bands):
            model = jnp.where(masks[0], totals[band][0][q], totals[band][1][q])
            both = model + turned(model)
            residual[band, q] = jnp.where(masks[0], both, 0.0).astype(BF16)
            upper[band, q] = jnp.where(masks[1], both, 0.0).astype(BF16)
        return carry

    lax.fori_loop(0, num_slots, slot, 0, unroll=8)

    sums[...] = jnp.zeros_like(sums)
    keep[...] = jnp.zeros_like(keep)
    send[...] = jnp.zeros_like(send)
    packed_low, spare = half_masks(ROWS)[0], none // 2

    def outer_products(turn, carry):
        for c in [STRIDE * turn + i for i in range(STRIDE)]:
            k, members, slots, values = read(c)
            outers = []
            for band in range(bands):
                pairs = [
                    residual[band, slots[u]] + upper[band, slots[u + 1]]
                    for u in range(0, GROUP, 2)
                ]
                outer = dot(left_t[band, k], jnp.concatenate(pairs, axis=1))
                along = jnp.sum(inner_all[c, band].astype(F32) * outer, axis=0, keepdims=True)
                scaled = []
                for u in range(0, GROUP, 2):
                    lanes = slice(u // 2 * LANES, (u // 2 + 1) * LANES)
                    for part in (0, 1):
                        row = jnp.where(row_masks[part], along[:, lanes], 0.0)
                        sums[band, pl.ds(members[u + part], 1), :] = row
                    scale = jnp.where(row_masks[0], values[band][u], values[band][u + 1])
                    scaled.append(outer[:, lanes] * scale)
                outers.append(scaled)
            outers += [[jnp.zeros((SIDE, LANES), F32)] * (GROUP // 2)] * (4 - bands)
            for pair in range(GROUP // 2):
                b0, b1, b2, b3 = [outers[band][pair] for band in range(4)]
                if bands > 3:
                    last = [jnp.where(masks[0], b2, turned(b3)), jnp.where(masks[0], turned(b2), b3)]
                else:
                    last = [b2, turned(b2)]
                first = [jnp.where(masks[0], b0, turned(b1)), jnp.where(masks[0], turned(b0), b1)]
                for part in (0, 1):
                    rows = slice((2 * pair + part) * SIDE, (2 * pair + part + 1) * SIDE)
                    stacks[c, rows, :] = jnp.concatenate([first[part], last[part]], axis=1).astype(BF16)
        return carry

    def gradients(turn, carry):
        for c in [STRIDE * turn + i for i in range(STRIDE)]:
            k, members, _, _ = read(c)
            depth = bands * SIDE
            grads = dot(stacks[c, :, :depth], right[k, :depth, :])
            for u, v in enumerate(members):
                top = grads[u * SIDE : u * SIDE + ROWS]
                low = grads[u * SIDE + ROWS : (u + 1) * SIDE]
                stamp = jnp.where(packed_low, top, low).astype(BF16)
                side, place = v // CAP % 2, v // (2 * CAP) * CAP + v % CAP
                keep[jnp.where(side == core, place, spare)] = stamp
                send[jnp.where(side == 1 - core, place, spare)] = stamp
        return carry

    lax.fori_loop(0, rounds, outer_products, 0)
    lax.fori_loop(0, rounds, gradients, 0)
    meta = amp_rows([lane_sums(sums[band, :none, :]) for band in range(bands)])
    keep[spare] = meta
    send[spare] = meta


def home_slots_kernel(bands, residual, left_t, right, back):
    num_slots = residual.shape[1]
    back[:, num_slots] = jnp.zeros((bands, ROWS, LANES), BF16)
    packed_low = half_masks(ROWS)[0]

    def slot(q, carry):
        for band in range(bands):
            outer = dot(left_t[band, q], residual[band, q]).astype(BF16)
            grad = dot(outer[:, :SIDE], right[q, band * SIDE : (band + 1) * SIDE, :])
            back[band, q] = jnp.where(packed_low, grad[:ROWS], grad[ROWS:]).astype(BF16)
        return carry

    lax.fori_loop(0, num_slots, slot, 0, unroll=8)


def home_gather_kernel(bands, last, lists, amps, eta_m, morph, back, received, keep, grad_a, sums):
    core = lax.axis_index("band")
    mine = pl.ds(half_rows(), HALF) if last else pl.ds(0, ROWS)

    def gather(s, carry):
        q = lists[0, 0, s]
        stamp = rounded(morph[s])
        grad = jnp.zeros((HALF if last else ROWS, LANES), F32)
        for ref, side in ((back, core), (received, 1 - core)):
            for band in range(bands):
                amp = amps[side * bands + band, s]
                if last:
                    grad = grad + amp * ref[band, q, mine, :].astype(F32)
                    if ref is received:
                        continue
                seen = ref[band, q].astype(F32)
                if not last:
                    grad = grad + amp * seen
                along = jnp.sum(seen * stamp, axis=0, keepdims=True)
                sums[side * bands + band, pl.ds(s, 1), :] = along
        keep[s] = jnp.maximum(morph[s, mine, :].astype(F32), 0.0) - eta_m[0, s] * grad
        return carry

    lax.fori_loop(0, lists.shape[2], gather, 0, unroll=4)
    for band in range(grad_a.shape[0]):
        rows = sums[core * bands + band] if last else sums[band]
        grad_a[band : band + 1, :] = lane_sums(rows)[:1]


def amp_rows(sums):
    eight = iota((8, LANES), 0)
    total = jnp.zeros((8, LANES), F32)
    for band, row in enumerate(sums):
        total = jnp.where(eight == band, row, total)
    coarse = total.astype(BF16).astype(F32)
    return jnp.concatenate([coarse, total - coarse, jnp.zeros((HALF, LANES), F32)], axis=0).astype(BF16)


def reduce_kernel(keep, received, *messages):
    for turn in range(2):
        part = pl.ds(turn * CAP, CAP)
        total = keep[part].astype(F32) + received[part].astype(F32)
        messages[turn][pl.ds(0, CAP)] = total.astype(BF16)
        pair = by_core(keep[2 * CAP].astype(F32), received[2 * CAP].astype(F32))
        meta = jnp.concatenate([pair[0][:HALF], pair[1][:HALF]], axis=0)
        messages[turn][CAP] = meta.astype(BF16)


def update_kernel(last, places, eta_m, slots_ref, eta_a, hots, amps_ref, grad_a, home, *refs):
    grads, out = refs[:NEAR], refs[NEAR:]
    state, amps_out, work = out[0], out[1], out[-1] if last else out[0]
    core = lax.axis_index("band")
    mine = pl.ds(half_rows(), HALF) if last else pl.ds(0, ROWS)
    nears = (core, 2 + core, 1 - core, 3 - core)
    lane = iota((ROWS, LANES), 1) // CAP
    meta = jnp.zeros((ROWS, LANES), F32)
    for ref, near in zip(grads, nears):
        meta = jnp.where(lane == near, ref[CAP].astype(F32), meta)
    all_hots = jnp.concatenate([hots[near, :CAP] for near in range(NEAR)], axis=0)
    from_near = dot(meta.astype(BF16), all_hots)
    bands = amps_ref.shape[0] // 2
    sides = [from_near[r : r + bands] + from_near[r + 8 : r + 8 + bands] for r in (0, HALF)]
    if last:
        amps = by_core(amps_ref[:bands], amps_ref[bands:])[0]
        total = grad_a[...] + by_core(sides[0], sides[1])[0]
    else:
        amps = amps_ref[...]
        total = grad_a[...] + jnp.concatenate(sides, axis=0)
    amps = jnp.maximum(amps - eta_a[...] * total, 0.0)
    if last:
        for band in range(bands):
            amps_out[band] = amps[band : band + 1]
    else:
        amps_out[...] = amps
    work[...] = home[...]
    for ref, near in zip(grads, nears):

        def add(n, carry, ref=ref, near=near):
            s = places[near, n]
            work[s] -= eta_m[0, s] * ref[n, mine, :].astype(F32)
            return carry

        lax.fori_loop(0, CAP, add, 0, unroll=8)

    if last:
        for r in range(HALF):
            state[:, r * LANES : (r + 1) * LANES] = jnp.maximum(work[:, r, :], 0.0)
        return
    amps_q, messages = out[2], out[3:5]
    amps_q[...] = amps.astype(BF16).astype(F32)

    def stamp_of(s):
        return jnp.maximum(state[s], 0.0).astype(BF16)

    write_messages(messages, rows_of(slots_ref), amps, hots, places, stamp_of)


def call(body, name, operands, scalars, outs, scratch=(), flops=0, moved=0):
    vmem, smem = pl.BlockSpec(memory_space=pltpu.VMEM), pl.BlockSpec(memory_space=pltpu.SMEM)
    return pl.pallas_call(
        body,
        out_shape=[jax.ShapeDtypeStruct(shape, dtype) for shape, dtype in outs],
        in_specs=[smem if i < scalars else vmem for i in range(len(operands))],
        out_specs=[vmem] * len(outs),
        scratch_shapes=[pltpu.VMEM(shape, dtype) for shape, dtype in scratch],
        compiler_params=pltpu.CompilerParams(vmem_limit_bytes=40 * 2**20),
        cost_estimate=pl.CostEstimate(flops=flops, bytes_accessed=moved, transcendentals=0),
        name=name,
    )(*operands)


def stepped(value, axis, step):
    shape = [lax.axis_size(name) for name in ("ra", "dec", "band")]

    def device(ra, dec, band):
        return (ra * shape[1] + dec) * shape[2] + band

    pairs = []
    for ra in range(shape[0]):
        for dec in range(shape[1]):
            for band, by in ((0, step), (1, -step)):
                if axis == "ra":
                    pairs.append((device(ra, dec, band), device((ra + by) % shape[0], dec, band)))
                elif 0 <= dec + by < shape[1]:
                    pairs.append((device(ra, dec, band), device(ra, dec + by, band)))
    return lax.ppermute(value, ("ra", "dec", "band"), pairs)


def swapped(value):
    return lax.ppermute(value, "band", [(0, 1), (1, 0)])


def all_tables(psf, num_slots, messages, sums):
    bands, held = psf.shape[:2]
    lines = lax.axis_size("dec")
    if lax.axis_size("ra") == 4 and 2 * held == num_slots and held % 2 == 0 and lines % 2 == 0:
        across = [(i, (i + lines // 2) % lines) for i in range(lines)]
        along = [(0, 1), (1, 0), (2, 3), (3, 2)]
        mine = jnp.where(lax.axis_index("dec") < lines // 2, psf[:, : held // 2], psf[:, held // 2 :])
        far = lax.ppermute(mine, "ra", [(0, 2), (1, 3)])
        far, sums = lax.optimization_barrier((far, sums))
        here = jnp.where(lax.axis_index("ra") < 2, mine, far)
        here, messages[0] = lax.optimization_barrier((here, messages[0]))
        near = lax.ppermute(here, "ra", along)
        near, messages[1] = lax.optimization_barrier((near, messages[1]))
        halves = make_tables((here, near), bands)
        others = (lax.ppermute(here, "dec", across), lax.ppermute(near, "dec", across))
        return make_tables(others, bands, halves), messages, sums
    return make_tables((lax.all_gather(psf, "ra", axis=1, tiled=True)[:, :num_slots],), bands), messages, sums


def shards(morphology, sed_amps, slot_lists, morph_step, sed_step, psf_kernels, observed):
    bands, num_slots, sources = sed_amps.shape[2], observed.shape[3], morphology.shape[2]
    lists, amps = slot_lists[0, 0][:, None, :], sed_amps[0, 0][:, None, :]
    eta_m, eta_a = morph_step[0], sed_step[0]
    full = morphology[0, 0].reshape(sources, ROWS, LANES)
    seen = observed[0, 0].reshape(bands, num_slots, ROWS, LANES)
    stamp = ((CAP + 1, ROWS, LANES), BF16)
    all_stamps = (sources, ROWS, LANES)
    near_all = NEAR * CAP
    chunks = -(-(near_all // GROUP + num_slots) // STRIDE) * STRIDE
    amps_theirs = swapped(amps)
    hots, places = call(
        functools.partial(lists_kernel, num_slots),
        "lists",
        (lists,),
        0,
        [
            ((NEAR, LANES, sources), BF16),
            ((2 * NEAR, LANES), jnp.int32),
        ],
        moved=2**20,
    )
    *messages, amps, amps_q = call(
        pack_kernel,
        "pack",
        (places, lists, amps, amps_theirs, hots, full),
        1,
        [stamp] * 2 + [((2 * bands, sources), F32)] * 2,
        moved=2**20,
    )
    def home_sums(amps_q, morph):
        return call(
            functools.partial(home_sums_kernel, bands),
            "home_sums",
            (lists, amps_q, morph),
            2,
            [((bands, num_slots + 1, ROWS, LANES), F32)],
            moved=4 * 2**20,
        )[0]

    sums = home_sums(amps_q, full)
    tables, messages, sums = all_tables(psf_kernels, num_slots, messages, sums)
    first_t, left, left_t, right = tables
    morph, plan = full, None
    for sweep in range(ITERS):
        last = sweep == ITERS - 1
        own = [stepped(messages[0], "ra", 1), stepped(messages[1], "dec", 1)]
        if sweep == 0:
            left, *own = lax.optimization_barrier((left, *own))
        else:
            sums = home_sums(amps_q, morph)
        home = call(
            functools.partial(home_forward_kernel, bands),
            "home_forward",
            (sums, seen, first_t, left),
            0,
            [((bands, num_slots, SIDE, LANES), F32)],
            [((bands, num_slots, SIDE, LANES), BF16)],
            flops=2 * 10**9,
            moved=4 * 2**20,
        )[0]
        if sweep > 0:
            own = [lax.optimization_barrier((home, x))[1] for x in own]
        other = [swapped(x) for x in own]
        amps_near, *new_plan = call(
            functools.partial(order_kernel, num_slots, sweep > 0),
            "order",
            (*own, *other),
            0,
            [((bands, LANES), F32)] + [((8, -(-chunks * GROUP // LANES) * LANES), jnp.int32)] * (sweep == 0),
            moved=2**20,
        )
        plan = new_plan[0] if new_plan else plan
        half_of_near = ((near_all // 2 + 1, ROWS, LANES), BF16)
        wide_slots = ((bands, num_slots, SIDE, LANES), BF16)
        residual, keep, send = call(
            functools.partial(visitors_kernel, bands),
            "visitors",
            (plan, amps_near, *own, *other, home, first_t, left, left_t, right),
            2,
            [wide_slots, half_of_near, half_of_near],
            [
                wide_slots,
                ((chunks, bands, SIDE, WIDE), BF16),
                ((near_all + 1, SIDE, LANES), BF16),
                ((chunks, WIDE, WIDE), BF16),
                ((bands, near_all + 8, LANES), F32),
            ]
            + [((num_slots, SIDE, LANES), F32)] * (2 * bands),
            flops=6 * 10**9,
            moved=8 * 2**20,
        )
        received = swapped(send)
        back = call(
            functools.partial(home_slots_kernel, bands),
            "home_slots",
            (residual, left_t, right),
            0,
            [((bands, num_slots + 1, ROWS, LANES), BF16)],
            flops=2 * 10**9,
            moved=4 * 2**20,
        )[0]
        received, back = lax.optimization_barrier((received, back))
        grads = call(reduce_kernel, "reduce", (keep, received), 0, [stamp] * 2, moved=2 * 2**20)
        grads = [stepped(grads[0], "ra", -1), stepped(grads[1], "dec", -1)]
        back_received = swapped(back)
        bands_here = bands if last else 2 * bands
        part = (sources, HALF, LANES) if last else all_stamps
        home_grad, grad_a = call(
            functools.partial(home_gather_kernel, bands, last),
            "home_gather",
            (lists, amps_q, eta_m, morph, back, back_received),
            3,
            [(part, F32), ((bands_here, sources), F32)],
            [((2 * bands, sources, LANES), F32)],
            moved=4 * 2**20,
        )
        grads = [lax.optimization_barrier((home_grad, x))[1] for x in grads]
        grads += [swapped(x) for x in grads]
        outs = [((sources, HALF * LANES) if last else all_stamps, F32)]
        outs += [((bands, 1, sources) if last else (2 * bands, sources), F32)]
        if not last:
            outs += [((bands_here, sources), F32)] + [stamp] * 2
        state, amps, *more = call(
            functools.partial(update_kernel, last),
            "update",
            (places, eta_m, lists, eta_a, hots, amps, grad_a, home_grad, *grads),
            2,
            outs,
            [(part, F32)] if last else (),
            moved=3 * 2**20,
        )
        if not last:
            morph = state
            amps_q, *messages = more
    return state[None, None], amps.reshape(1, 1, bands, sources)


def solution(mesh):
    in_specs = (
        P("ra", "dec", None, None),
        P("ra", "dec", "band", None),
        P("ra", "dec", None, None),
        P("ra", "dec", None),
        P("ra", "dec", None),
        P("band", "ra", None),
        P("ra", "dec", "band", None, None),
    )
    out_specs = (P("ra", "dec", None, "band"), P("ra", "dec", "band", None))
    return jax.shard_map(shards, mesh=mesh, in_specs=in_specs, out_specs=out_specs, check_vma=False)
```

```python
import functools

import jax
import jax.numpy as jnp
from jax import lax
from jax.experimental import pallas as pl
from jax.experimental.pallas import tpu as pltpu
from jax.sharding import PartitionSpec as P

SIDE = 64
KERN = 32
ITERS = 2
CAP = 32
LANES = 128
ROWS = SIDE * SIDE // LANES
HALF = ROWS // 2
WIDE = 4 * SIDE
ORDER, KERNEL_OF, SLOT_OF, COUNT = range(4)
NEAR = 4
GROUP = 4
STRIDE = 8
F32 = jnp.float32
BF16 = jnp.bfloat16


def dot(a, b):
    return lax.dot_general(a, b, (((1,), (0,)), ((), ())), preferred_element_type=F32)


def dot_nt(a, b):
    return lax.dot_general(a, b, (((1,), (1,)), ((), ())), preferred_element_type=F32)


def iota(shape, dim):
    return lax.broadcasted_iota(jnp.int32, shape, dim)


def low_lanes(rows, dtype=F32):
    return (iota((rows, LANES), 1) < SIDE).astype(F32).astype(dtype)


def lane_sums(rows):
    coarse = rows.astype(BF16)
    fine = (rows - coarse.astype(F32)).astype(BF16)
    ones = jnp.ones((8, rows.shape[1]), BF16)
    return dot_nt(ones, coarse) + dot_nt(ones, fine)


def half_masks(rows):
    low = iota((rows, LANES), 1) < SIDE
    return low, jnp.logical_not(low)


def turned(value):
    return pltpu.roll(value, SIDE, 1)


def twofold(packed):
    low, flip = half_masks(ROWS)[0], turned(packed)
    return jnp.concatenate([jnp.where(low, packed, flip), jnp.where(low, flip, packed)], axis=0)


def rounded(stamp):
    if stamp.dtype == F32:
        stamp = jnp.maximum(stamp, 0.0).astype(BF16)
    return stamp.astype(F32)


def half_rows():
    return pl.multiple_of(lax.axis_index("band") * HALF, HALF)


def rows_of(ref):
    return jnp.concatenate([ref[i] for i in range(ref.shape[0])], axis=0)


def by_core(mine, theirs):
    first = lax.axis_index("band") == 0
    return jnp.where(first, mine, theirs), jnp.where(first, theirs, mine)


def lists_kernel(num_slots, slots_ref, hots, places):
    slots = rows_of(slots_ref)
    sources = slots.shape[1]
    valid = (slots < num_slots).astype(F32)
    upper = (iota((sources, sources), 0) <= iota((sources, sources), 1)).astype(F32)
    rank = dot(valid.astype(BF16), upper.astype(BF16))
    place = iota((LANES, sources), 0).astype(F32)
    names = iota((8, sources), 1).astype(F32).astype(BF16)
    for near in range(NEAR):
        row = slice(near + 1, near + 2)
        hot = ((place == rank[row] - 1.0).astype(F32) * valid[row]).astype(BF16)
        hots[near] = hot
        places[near : near + 1, :] = dot_nt(names, hot)[:1].astype(jnp.int32)
        count = jnp.broadcast_to(rank[row, sources - 1 :], (1, LANES))
        places[NEAR + near : NEAR + near + 1, :] = count.astype(jnp.int32)


def write_messages(messages, slots, amps, hots, places, stamp_of):
    first = lax.axis_index("band") == 0
    row = iota((ROWS, slots.shape[1]), 0)
    for turn in range(2):
        near = 2 * turn + lax.axis_index("band")

        def pick(n, carry, near=near, turn=turn):
            messages[turn][n] = stamp_of(places[near, n])
            return carry

        lax.fori_loop(0, CAP, pick, 0, unroll=8)
        slot = jnp.where(first, slots[2 * turn + 1 : 2 * turn + 2], slots[2 * turn + 2 : 2 * turn + 3]).astype(F32)
        meta = jnp.where(row == 0, slot + 1.0, 0.0)
        meta = jnp.where(row == 1, slots[0:1].astype(F32), meta)
        for band in range(amps.shape[0]):
            meta = jnp.where(row == 2 + band, amps[band : band + 1], meta)
        hot = jnp.where(first, hots[2 * turn].astype(F32), hots[2 * turn + 1].astype(F32)).astype(BF16)
        messages[turn][CAP] = dot_nt(meta.astype(BF16), hot).astype(BF16)


def pack_kernel(places, slots_ref, amps_mine, amps_theirs, hots, morph, *out):
    messages, amps_out, amps_q = out[:2], out[2], out[3]
    amps = jnp.concatenate(by_core(rows_of(amps_mine), rows_of(amps_theirs)), axis=0)
    write_messages(messages, rows_of(slots_ref), amps, hots, places, lambda s: morph[s])
    amps_out[...] = amps
    amps_q[...] = amps.astype(BF16).astype(F32)


def order_kernel(num_slots, again, *refs):
    amps, none = refs[NEAR], NEAR * CAP
    bands = amps.shape[0]
    meta = jnp.zeros((ROWS, LANES), F32)
    for turn in range(2):
        pair = by_core(refs[turn][CAP].astype(F32), refs[2 + turn][CAP].astype(F32))
        for core in range(2):
            meta = meta + pltpu.roll(pair[core], (2 * turn + core) * CAP, 1)
    amps[...] = by_core(meta[2 : 2 + bands], meta[2 + bands : 2 + 2 * bands])[0]
    if again:
        return
    plan, slot, kernel = refs[NEAR + 1], meta[0:1], meta[1:2]
    plan[SLOT_OF : SLOT_OF + 1, :LANES] = jnp.maximum(slot - 1.0, 0.0).astype(jnp.int32)
    live = (slot > 0.0).astype(F32)
    hot = (iota((num_slots, none), 0).astype(F32) == kernel).astype(F32) * live
    upto = (iota((none, none), 0) <= iota((none, none), 1)).astype(F32).astype(BF16)
    rank = dot(hot.astype(BF16), upto)
    size = jnp.max(rank, axis=1, keepdims=True)
    filled = ((size.astype(jnp.int32) + (GROUP - 1)) // GROUP).astype(F32)
    before = (iota((num_slots, num_slots), 1) < iota((num_slots, num_slots), 0)).astype(F32).astype(BF16)
    start = dot(before, jnp.broadcast_to(filled, (num_slots, none)).astype(BF16))
    place = jnp.sum(hot * (GROUP * start + rank), axis=0, keepdims=True) - 1.0
    eight = iota((8, none), 0)
    names = jnp.where(eight == 0, iota((8, none), 1).astype(F32) - none, 0.0).astype(BF16)
    for part in range(plan.shape[1] // LANES):
        at = (iota((LANES, none), 0) + part * LANES).astype(F32)
        hit = (at == place).astype(F32) * live
        found = dot_nt(names, hit.astype(BF16))[:1] + none
        plan[ORDER : ORDER + 1, part * LANES : (part + 1) * LANES] = found.astype(jnp.int32)
    chunk = iota((num_slots, LANES), 1).astype(F32)
    row = iota((num_slots, LANES), 0).astype(F32)
    inside = (chunk >= start[:, :LANES]) & (chunk < start[:, :LANES] + filled)
    kernels = jnp.sum(jnp.where(inside, row, 0.0), axis=0, keepdims=True)
    plan[KERNEL_OF : KERNEL_OF + 1, :LANES] = kernels.astype(jnp.int32)
    total = jnp.sum(filled, axis=0, keepdims=True)
    plan[COUNT : COUNT + 1, :LANES] = jnp.broadcast_to(total, (1, LANES)).astype(jnp.int32)


def quarter_start(quarter, held):
    parity, line = lax.axis_index("ra") % 2, lax.axis_index("dec") // (lax.axis_size("dec") // 2)
    shard = parity if quarter % 2 == 0 else 1 - parity
    half = line if quarter < 2 else 1 - line
    return (2 * shard + half) * held


def tables_kernel(bands, earlier, *refs):
    shards, (first_t, left, left_t, right, packed) = refs[: len(refs) - 5 - 4 * earlier], refs[-5:]
    held = shards[0].shape[1]
    for turn, ref in enumerate(shards):
        for band in range(bands):
            for r in range(ROWS):
                rows = pl.ds(turn * held * ROWS + r, held, stride=ROWS)
                packed[band, rows, :] = ref[band, :, r * LANES : (r + 1) * LANES].astype(F32)
    starts = [quarter_start(2 + turn, held) if earlier else turn * held for turn in range(len(shards))]
    if earlier:
        old_first, old_left, old_left_t, old_right = refs[len(shards) : len(shards) + 4]
        for turn in range(2):
            old, new = pl.ds(turn * held, held), pl.ds(quarter_start(turn, held), held)
            first_t[new] = old_first[old]
            right[new] = old_right[old]
            for band in range(bands):
                left[band, new] = old_left[band, old]
                left_t[band, new] = old_left_t[band, old]
    eye = (iota((SIDE, SIDE), 0) == iota((SIDE, SIDE), 1)).astype(F32).astype(BF16)
    row, col = iota((SIDE, SIDE), 0), iota((SIDE, SIDE), 1)
    even = (col == 2 * (row % ROWS) + row // ROWS).astype(F32).astype(BF16)
    even_t = (row == 2 * (col % ROWS) + col // ROWS).astype(F32).astype(BF16)
    rest = [jnp.zeros((SIDE * (4 - bands), SIDE), BF16)] if bands < 4 else []

    def step(place, carry):
        for turn, start in enumerate(starts):
            k = start + place
            at = pl.multiple_of((turn * held + place) * ROWS, ROWS)
            parts = [twofold(packed[band, pl.ds(at, ROWS), :]).astype(BF16) for band in range(bands)]
            lefts = dot_nt(jnp.concatenate([part[:, :SIDE] for part in parts], axis=0), even).astype(BF16)
            natural = []
            for band, part in enumerate(parts):
                rows = slice(band * SIDE, (band + 1) * SIDE)
                left[band, k] = lefts[rows]
                left_t[band, k] = dot_nt(even, part[:, :SIDE]).astype(BF16)
                both = dot(even_t, part).astype(BF16)
                right[k, rows, :] = both
                natural.append(both[:, :SIDE])
            if rest:
                right[k, bands * SIDE :, :] = jnp.zeros((SIDE * (4 - bands), LANES), BF16)
            first_t[k] = dot_nt(eye, jnp.concatenate(natural + rest, axis=0)).astype(BF16)
        return carry

    lax.fori_loop(0, held, step, 0, unroll=min(held, 4))


def make_tables(shards, bands, earlier=()):
    count = sum(x.shape[1] for x in shards)
    total = count + sum(x.shape[0] for x in earlier[:1])
    square = ((bands, total, SIDE, SIDE), BF16)
    return call(
        functools.partial(tables_kernel, bands, bool(earlier)),
        "tables",
        (*shards, *earlier),
        0,
        [((total, SIDE, WIDE), BF16), square, square, ((total, WIDE, LANES), BF16)],
        [((bands, count * ROWS, LANES), F32)],
        flops=2 * 10**9,
        moved=5 * 2**20,
    )


def home_sums_kernel(bands, lists, amps, morph, sums):
    first = lax.axis_index("band") * bands
    sums[...] = jnp.zeros_like(sums)

    def add(s, carry):
        q = lists[0, 0, s]
        stamp = rounded(morph[s])
        for band in range(bands):
            sums[band, q] += amps[first + band, s] * stamp
        return carry

    lax.fori_loop(0, lists.shape[2], add, 0, unroll=4)


def home_forward_kernel(bands, sums, observed, first_t, left, total, inner_all):
    num_slots = total.shape[1]
    masks = half_masks(SIDE)

    def inner_products(q, carry):
        images = []
        for band in range(bands):
            both = sums[band, q]
            images += [both[:, :SIDE], turned(both)[:, :SIDE]]
        inners = dot(jnp.concatenate(images, axis=0).astype(BF16), first_t[q])
        for band in range(bands):
            lanes = slice(band // 2 * LANES, (band // 2 + 1) * LANES)
            inner_all[band, q] = inners[band * SIDE : (band + 1) * SIDE, lanes].astype(BF16)
        return carry

    def slot(q, carry):
        for band in range(bands):
            image = dot(left[band, q], inner_all[band, q]) - twofold(observed[band, q].astype(F32))
            total[band, q] = jnp.where(masks[band % 2], image, 0.0)
        return carry

    lax.fori_loop(0, num_slots, inner_products, 0, unroll=4)
    lax.fori_loop(0, num_slots, slot, 0, unroll=4)


def chunk_reader(bands, plan, amps):
    none = NEAR * CAP

    def read(c):
        members = [plan[ORDER, c * GROUP + u] for u in range(GROUP)]
        held = [jnp.minimum(v, none - 1) for v in members]
        values = [[jnp.where(v < none, amps[band, h], 0.0) for v, h in zip(members, held)] for band in range(bands)]
        return plan[KERNEL_OF, c], members, [plan[SLOT_OF, h] for h in held], values

    count = plan[COUNT, 0]
    full = (count + STRIDE // 2 - 1) // STRIDE
    rest = (count > STRIDE * full).astype(jnp.int32)

    def for_chunks(body):
        def whole(turn, carry):
            body([STRIDE * turn + i for i in range(STRIDE)])
            return carry

        def half(turn, carry):
            body([STRIDE * full + i for i in range(STRIDE // 2)])
            return carry

        lax.fori_loop(0, full, whole, 0)
        lax.fori_loop(0, rest, half, 0)

    return read, for_chunks


def visitors_kernel(bands, plan, amps, *refs):
    home, first_t, left, left_t, right = refs[NEAR : NEAR + 5]
    residual, keep, send, upper, inner_all, stamps, stacks, sums, *totals = refs[NEAR + 5 :]
    totals = [totals[2 * band : 2 * band + 2] for band in range(bands)]
    num_slots = home.shape[1]
    none = NEAR * CAP
    core = lax.axis_index("band")
    for source, near in enumerate((core, 2 + core, 1 - core, 3 - core)):
        group = pl.ds(near * CAP, CAP)
        even = refs[source][pl.ds(0, CAP)].astype(F32)
        odd = turned(even.reshape(CAP * ROWS, LANES)).reshape(CAP, ROWS, LANES)
        stamps[group, pl.ds(0, ROWS), :] = even.astype(BF16)
        stamps[group, pl.ds(ROWS, ROWS), :] = odd.astype(BF16)
    stamps[none] = jnp.zeros((SIDE, LANES), BF16)
    for band in range(bands):
        totals[band][band % 2][...] = home[band]
        totals[band][1 - band % 2][...] = jnp.zeros_like(home[band])
    masks, row_masks = half_masks(SIDE), half_masks(1)
    read, for_chunks = chunk_reader(bands, plan, amps)

    def inner_products(some):
        for c in some:
            k, members, _, _ = read(c)
            stack = jnp.concatenate([stamps[v] for v in members], axis=0)
            inners = dot(stack[:, :SIDE], first_t[k])
            for band in range(bands):
                lanes = slice(band // 2 * LANES, (band // 2 + 1) * LANES)
                pairs = []
                for u in range(0, GROUP, 2):
                    x = inners[u * SIDE : (u + 1) * SIDE, lanes]
                    y = inners[(u + 1) * SIDE : (u + 2) * SIDE, lanes]
                    x, y = (x, turned(y)) if band % 2 == 0 else (turned(x), y)
                    pairs.append(jnp.where(masks[0], x, y))
                inner_all[c, band] = jnp.concatenate(pairs, axis=1).astype(BF16)

    def images(some):
        for c in some:
            k, _, slots, values = read(c)
            for band in range(bands):
                image = dot(left[band, k], inner_all[c, band])
                for u in range(0, GROUP, 2):
                    lanes = slice(u // 2 * LANES, (u // 2 + 1) * LANES)
                    scale = jnp.where(row_masks[0], values[band][u], values[band][u + 1])
                    pair = image[:, lanes] * scale
                    for part in (0, 1):
                        totals[band][part][slots[u + part]] += pair

    for_chunks(inner_products)
    for_chunks(images)

    def slot(q, carry):
        for band in range(bands):
            model = jnp.where(masks[0], totals[band][0][q], totals[band][1][q])
            both = model + turned(model)
            residual[band, q] = jnp.where(masks[0], both, 0.0).astype(BF16)
            upper[band, q] = jnp.where(masks[1], both, 0.0).astype(BF16)
        return carry

    lax.fori_loop(0, num_slots, slot, 0, unroll=8)

    sums[...] = jnp.zeros_like(sums)
    keep[...] = jnp.zeros_like(keep)
    send[...] = jnp.zeros_like(send)
    packed_low, spare = half_masks(ROWS)[0], none // 2

    def outer_products(some):
        for c in some:
            k, members, slots, values = read(c)
            outers = []
            for band in range(bands):
                pairs = [
                    residual[band, slots[u]] + upper[band, slots[u + 1]]
                    for u in range(0, GROUP, 2)
                ]
                outer = dot(left_t[band, k], jnp.concatenate(pairs, axis=1))
                along = jnp.sum(inner_all[c, band].astype(F32) * outer, axis=0, keepdims=True)
                scaled = []
                for u in range(0, GROUP, 2):
                    lanes = slice(u // 2 * LANES, (u // 2 + 1) * LANES)
                    for part in (0, 1):
                        row = jnp.where(row_masks[part], along[:, lanes], 0.0)
                        sums[band, pl.ds(members[u + part], 1), :] = row
                    scale = jnp.where(row_masks[0], values[band][u], values[band][u + 1])
                    scaled.append(outer[:, lanes] * scale)
                outers.append(scaled)
            outers += [[jnp.zeros((SIDE, LANES), F32)] * (GROUP // 2)] * (4 - bands)
            for pair in range(GROUP // 2):
                b0, b1, b2, b3 = [outers[band][pair] for band in range(4)]
                if bands > 3:
                    last = [jnp.where(masks[0], b2, turned(b3)), jnp.where(masks[0], turned(b2), b3)]
                else:
                    last = [b2, turned(b2)]
                first = [jnp.where(masks[0], b0, turned(b1)), jnp.where(masks[0], turned(b0), b1)]
                for part in (0, 1):
                    rows = slice((2 * pair + part) * SIDE, (2 * pair + part + 1) * SIDE)
                    stacks[c, rows, :] = jnp.concatenate([first[part], last[part]], axis=1).astype(BF16)

    def gradients(some):
        for c in some:
            k, members, _, _ = read(c)
            depth = bands * SIDE
            grads = dot(stacks[c, :, :depth], right[k, :depth, :])
            for u, v in enumerate(members):
                top = grads[u * SIDE : u * SIDE + ROWS]
                low = grads[u * SIDE + ROWS : (u + 1) * SIDE]
                stamp = jnp.where(packed_low, top, low).astype(BF16)
                side, place = v // CAP % 2, v // (2 * CAP) * CAP + v % CAP
                keep[jnp.where(side == core, place, spare)] = stamp
                send[jnp.where(side == 1 - core, place, spare)] = stamp

    for_chunks(outer_products)
    for_chunks(gradients)
    meta = amp_rows([lane_sums(sums[band, :none, :]) for band in range(bands)])
    keep[spare] = meta
    send[spare] = meta


def home_slots_kernel(bands, residual, left_t, right, back):
    num_slots = residual.shape[1]
    back[:, num_slots] = jnp.zeros((bands, ROWS, LANES), BF16)
    packed_low = half_masks(ROWS)[0]

    def slot(q, carry):
        for band in range(bands):
            outer = dot(left_t[band, q], residual[band, q]).astype(BF16)
            grad = dot(outer[:, :SIDE], right[q, band * SIDE : (band + 1) * SIDE, :])
            back[band, q] = jnp.where(packed_low, grad[:ROWS], grad[ROWS:]).astype(BF16)
        return carry

    lax.fori_loop(0, num_slots, slot, 0, unroll=8)


def home_gather_kernel(bands, last, lists, amps, eta_m, morph, back, received, keep, grad_a, sums):
    core = lax.axis_index("band")
    mine = pl.ds(half_rows(), HALF) if last else pl.ds(0, ROWS)

    def gather(s, carry):
        q = lists[0, 0, s]
        stamp = rounded(morph[s])
        grad = jnp.zeros((HALF if last else ROWS, LANES), F32)
        for ref, side in ((back, core), (received, 1 - core)):
            for band in range(bands):
                amp = amps[side * bands + band, s]
                if last:
                    grad = grad + amp * ref[band, q, mine, :].astype(F32)
                    if ref is received:
                        continue
                seen = ref[band, q].astype(F32)
                if not last:
                    grad = grad + amp * seen
                along = jnp.sum(seen * stamp, axis=0, keepdims=True)
                sums[side * bands + band, pl.ds(s, 1), :] = along
        keep[s] = jnp.maximum(morph[s, mine, :].astype(F32), 0.0) - eta_m[0, s] * grad
        return carry

    lax.fori_loop(0, lists.shape[2], gather, 0, unroll=4)
    for band in range(grad_a.shape[0]):
        rows = sums[core * bands + band] if last else sums[band]
        grad_a[band : band + 1, :] = lane_sums(rows)[:1]


def amp_rows(sums):
    eight = iota((8, LANES), 0)
    total = jnp.zeros((8, LANES), F32)
    for band, row in enumerate(sums):
        total = jnp.where(eight == band, row, total)
    coarse = total.astype(BF16).astype(F32)
    return jnp.concatenate([coarse, total - coarse, jnp.zeros((HALF, LANES), F32)], axis=0).astype(BF16)


def reduce_kernel(keep, received, *messages):
    for turn in range(2):
        part = pl.ds(turn * CAP, CAP)
        total = keep[part].astype(F32) + received[part].astype(F32)
        messages[turn][pl.ds(0, CAP)] = total.astype(BF16)
        pair = by_core(keep[2 * CAP].astype(F32), received[2 * CAP].astype(F32))
        meta = jnp.concatenate([pair[0][:HALF], pair[1][:HALF]], axis=0)
        messages[turn][CAP] = meta.astype(BF16)


def update_kernel(last, places, eta_m, slots_ref, eta_a, hots, amps_ref, grad_a, home, *refs):
    grads, out = refs[:NEAR], refs[NEAR:]
    state, amps_out, work = out[0], out[1], out[-1] if last else out[0]
    core = lax.axis_index("band")
    mine = pl.ds(half_rows(), HALF) if last else pl.ds(0, ROWS)
    nears = (core, 2 + core, 1 - core, 3 - core)
    lane = iota((ROWS, LANES), 1) // CAP
    meta = jnp.zeros((ROWS, LANES), F32)
    for ref, near in zip(grads, nears):
        meta = jnp.where(lane == near, ref[CAP].astype(F32), meta)
    all_hots = jnp.concatenate([hots[near, :CAP] for near in range(NEAR)], axis=0)
    from_near = dot(meta.astype(BF16), all_hots)
    bands = amps_ref.shape[0] // 2
    sides = [from_near[r : r + bands] + from_near[r + 8 : r + 8 + bands] for r in (0, HALF)]
    if last:
        amps = by_core(amps_ref[:bands], amps_ref[bands:])[0]
        total = grad_a[...] + by_core(sides[0], sides[1])[0]
    else:
        amps = amps_ref[...]
        total = grad_a[...] + jnp.concatenate(sides, axis=0)
    amps = jnp.maximum(amps - eta_a[...] * total, 0.0)
    if last:
        for band in range(bands):
            amps_out[band] = amps[band : band + 1]
    else:
        amps_out[...] = amps
    work[...] = home[...]
    for ref, near in zip(grads, nears):

        def add(n, carry, ref=ref, near=near):
            s = places[near, n]
            work[s] -= eta_m[0, s] * ref[n, mine, :].astype(F32)
            return carry

        lax.fori_loop(0, CAP, add, 0, unroll=8)

    if last:
        for r in range(HALF):
            state[:, r * LANES : (r + 1) * LANES] = jnp.maximum(work[:, r, :], 0.0)
        return
    amps_q, messages = out[2], out[3:5]
    amps_q[...] = amps.astype(BF16).astype(F32)

    def stamp_of(s):
        return jnp.maximum(state[s], 0.0).astype(BF16)

    write_messages(messages, rows_of(slots_ref), amps, hots, places, stamp_of)


def call(body, name, operands, scalars, outs, scratch=(), flops=0, moved=0):
    vmem, smem = pl.BlockSpec(memory_space=pltpu.VMEM), pl.BlockSpec(memory_space=pltpu.SMEM)
    return pl.pallas_call(
        body,
        out_shape=[jax.ShapeDtypeStruct(shape, dtype) for shape, dtype in outs],
        in_specs=[smem if i < scalars else vmem for i in range(len(operands))],
        out_specs=[vmem] * len(outs),
        scratch_shapes=[pltpu.VMEM(shape, dtype) for shape, dtype in scratch],
        compiler_params=pltpu.CompilerParams(vmem_limit_bytes=40 * 2**20),
        cost_estimate=pl.CostEstimate(flops=flops, bytes_accessed=moved, transcendentals=0),
        name=name,
    )(*operands)


def stepped(value, axis, step):
    shape = [lax.axis_size(name) for name in ("ra", "dec", "band")]

    def device(ra, dec, band):
        return (ra * shape[1] + dec) * shape[2] + band

    pairs = []
    for ra in range(shape[0]):
        for dec in range(shape[1]):
            for band, by in ((0, step), (1, -step)):
                if axis == "ra":
                    pairs.append((device(ra, dec, band), device((ra + by) % shape[0], dec, band)))
                elif 0 <= dec + by < shape[1]:
                    pairs.append((device(ra, dec, band), device(ra, dec + by, band)))
    return lax.ppermute(value, ("ra", "dec", "band"), pairs)


def swapped(value):
    return lax.ppermute(value, "band", [(0, 1), (1, 0)])


def all_tables(psf, num_slots, messages, sums):
    bands, held = psf.shape[:2]
    lines = lax.axis_size("dec")
    if lax.axis_size("ra") == 4 and 2 * held == num_slots and held % 2 == 0 and lines % 2 == 0:
        across = [(i, (i + lines // 2) % lines) for i in range(lines)]
        along = [(0, 1), (1, 0), (2, 3), (3, 2)]
        mine = jnp.where(lax.axis_index("dec") < lines // 2, psf[:, : held // 2], psf[:, held // 2 :])
        far = lax.ppermute(mine, "ra", [(0, 2), (1, 3)])
        far, sums = lax.optimization_barrier((far, sums))
        here = jnp.where(lax.axis_index("ra") < 2, mine, far)
        here, messages[0] = lax.optimization_barrier((here, messages[0]))
        near = lax.ppermute(here, "ra", along)
        near, messages[1] = lax.optimization_barrier((near, messages[1]))
        halves = make_tables((here, near), bands)
        others = (lax.ppermute(here, "dec", across), lax.ppermute(near, "dec", across))
        return make_tables(others, bands, halves), messages, sums
    return make_tables((lax.all_gather(psf, "ra", axis=1, tiled=True)[:, :num_slots],), bands), messages, sums


def shards(morphology, sed_amps, slot_lists, morph_step, sed_step, psf_kernels, observed):
    bands, num_slots, sources = sed_amps.shape[2], observed.shape[3], morphology.shape[2]
    lists, amps = slot_lists[0, 0][:, None, :], sed_amps[0, 0][:, None, :]
    eta_m, eta_a = morph_step[0], sed_step[0]
    full = morphology[0, 0].reshape(sources, ROWS, LANES)
    seen = observed[0, 0].reshape(bands, num_slots, ROWS, LANES)
    stamp = ((CAP + 1, ROWS, LANES), BF16)
    all_stamps = (sources, ROWS, LANES)
    near_all = NEAR * CAP
    chunks = -(-(near_all // GROUP + num_slots) // STRIDE) * STRIDE
    amps_theirs = swapped(amps)
    hots, places = call(
        functools.partial(lists_kernel, num_slots),
        "lists",
        (lists,),
        0,
        [
            ((NEAR, LANES, sources), BF16),
            ((2 * NEAR, LANES), jnp.int32),
        ],
        moved=2**20,
    )
    *messages, amps, amps_q = call(
        pack_kernel,
        "pack",
        (places, lists, amps, amps_theirs, hots, full),
        1,
        [stamp] * 2 + [((2 * bands, sources), F32)] * 2,
        moved=2**20,
    )
    def home_sums(amps_q, morph):
        return call(
            functools.partial(home_sums_kernel, bands),
            "home_sums",
            (lists, amps_q, morph),
            2,
            [((bands, num_slots + 1, ROWS, LANES), F32)],
            moved=4 * 2**20,
        )[0]

    sums = home_sums(amps_q, full)
    tables, messages, sums = all_tables(psf_kernels, num_slots, messages, sums)
    first_t, left, left_t, right = tables
    morph, plan = full, None
    for sweep in range(ITERS):
        last = sweep == ITERS - 1
        own = [stepped(messages[0], "ra", 1), stepped(messages[1], "dec", 1)]
        if sweep == 0:
            left, *own = lax.optimization_barrier((left, *own))
        else:
            sums = home_sums(amps_q, morph)
        home = call(
            functools.partial(home_forward_kernel, bands),
            "home_forward",
            (sums, seen, first_t, left),
            0,
            [((bands, num_slots, SIDE, LANES), F32)],
            [((bands, num_slots, SIDE, LANES), BF16)],
            flops=2 * 10**9,
            moved=4 * 2**20,
        )[0]
        if sweep > 0:
            own = [lax.optimization_barrier((home, x))[1] for x in own]
        other = [swapped(x) for x in own]
        amps_near, *new_plan = call(
            functools.partial(order_kernel, num_slots, sweep > 0),
            "order",
            (*own, *other),
            0,
            [((bands, LANES), F32)] + [((8, -(-chunks * GROUP // LANES) * LANES), jnp.int32)] * (sweep == 0),
            moved=2**20,
        )
        plan = new_plan[0] if new_plan else plan
        half_of_near = ((near_all // 2 + 1, ROWS, LANES), BF16)
        wide_slots = ((bands, num_slots, SIDE, LANES), BF16)
        residual, keep, send = call(
            functools.partial(visitors_kernel, bands),
            "visitors",
            (plan, amps_near, *own, *other, home, first_t, left, left_t, right),
            2,
            [wide_slots, half_of_near, half_of_near],
            [
                wide_slots,
                ((chunks, bands, SIDE, WIDE), BF16),
                ((near_all + 1, SIDE, LANES), BF16),
                ((chunks, WIDE, WIDE), BF16),
                ((bands, near_all + 8, LANES), F32),
            ]
            + [((num_slots, SIDE, LANES), F32)] * (2 * bands),
            flops=6 * 10**9,
            moved=8 * 2**20,
        )
        received = swapped(send)
        back = call(
            functools.partial(home_slots_kernel, bands),
            "home_slots",
            (residual, left_t, right),
            0,
            [((bands, num_slots + 1, ROWS, LANES), BF16)],
            flops=2 * 10**9,
            moved=4 * 2**20,
        )[0]
        received, back = lax.optimization_barrier((received, back))
        grads = call(reduce_kernel, "reduce", (keep, received), 0, [stamp] * 2, moved=2 * 2**20)
        grads = [stepped(grads[0], "ra", -1), stepped(grads[1], "dec", -1)]
        back_received = swapped(back)
        bands_here = bands if last else 2 * bands
        part = (sources, HALF, LANES) if last else all_stamps
        home_grad, grad_a = call(
            functools.partial(home_gather_kernel, bands, last),
            "home_gather",
            (lists, amps_q, eta_m, morph, back, back_received),
            3,
            [(part, F32), ((bands_here, sources), F32)],
            [((2 * bands, sources, LANES), F32)],
            moved=4 * 2**20,
        )
        grads = [lax.optimization_barrier((home_grad, x))[1] for x in grads]
        grads += [swapped(x) for x in grads]
        outs = [((sources, HALF * LANES) if last else all_stamps, F32)]
        outs += [((bands, 1, sources) if last else (2 * bands, sources), F32)]
        if not last:
            outs += [((bands_here, sources), F32)] + [stamp] * 2
        state, amps, *more = call(
            functools.partial(update_kernel, last),
            "update",
            (places, eta_m, lists, eta_a, hots, amps, grad_a, home_grad, *grads),
            2,
            outs,
            [(part, F32)] if last else (),
            moved=3 * 2**20,
        )
        if not last:
            morph = state
            amps_q, *messages = more
    return state[None, None], amps.reshape(1, 1, bands, sources)


def solution(mesh):
    in_specs = (
        P("ra", "dec", None, None),
        P("ra", "dec", "band", None),
        P("ra", "dec", None, None),
        P("ra", "dec", None),
        P("ra", "dec", None),
        P("band", "ra", None),
        P("ra", "dec", "band", None, None),
    )
    out_specs = (P("ra", "dec", None, "band"), P("ra", "dec", "band", None))
    return jax.shard_map(shards, mesh=mesh, in_specs=in_specs, out_specs=out_specs, check_vma=False)
```
